32 devices in a mesh: dp: 8 (over z, x), tensor: 4 (over y, core).
Axes of the slice: x: 2, y: 2, z: 4, core: 2. Of those that a mesh axis runs over, the one named last changes fastest.
Arguments:
- tokens: bfloat16 [8192, 2048], P(('dp', 'tensor')), may hold values from -6 to 6
- cotangent: bfloat16 [8192, 2048], P(('dp', 'tensor')), may hold values from -7 to 7
- doc_lengths: int32 [8, 2], P('dp'), may hold values from 1 to 768, 1024 in all within a row
- attend_in: float32 [2048, 3072], P('dp', 'tensor'), may hold values from -0.125 to 0.125
- attend_out: float32 [2048, 2048], P('tensor', 'dp'), may hold values from -3 to 3
- feed_in: float32 [2, 2048, 8192], P(None, 'dp', 'tensor'), may hold values from -1 to 1
- feed_out: float32 [8192, 2048], P('tensor', 'dp'), may hold values from -1 to 1
- norm_gains: float32 [2, 2048], P(None, 'dp'), may hold values from 0 to 3, as said below
- moment_attend_in: float32 [2048, 3072], P('dp', 'tensor'), may hold values from -1 to 1
- square_attend_in: float32 [2048, 3072], P('dp', 'tensor'), may hold values from 0 to 1, as said below
- moment_attend_out: float32 [2048, 2048], P('tensor', 'dp'), may hold values from -1 to 1
- square_attend_out: float32 [2048, 2048], P('tensor', 'dp'), may hold values from 0 to 1, as said below
- moment_feed_in: float32 [2, 2048, 8192], P(None, 'dp', 'tensor'), may hold values from -1 to 1
- square_feed_in: float32 [2, 2048, 8192], P(None, 'dp', 'tensor'), may hold values from 0 to 1, as said below
- moment_feed_out: float32 [8192, 2048], P('tensor', 'dp'), may hold values from -1 to 1
- square_feed_out: float32 [8192, 2048], P('tensor', 'dp'), may hold values from 0 to 1, as said below
- moment_gains: float32 [2, 2048], P(None, 'dp'), may hold values from -1 to 1
- square_gains: float32 [2, 2048], P(None, 'dp'), may hold values from 0 to 1, as said below
Outputs:
- block_out: bfloat16 [8192, 2048], P(('dp', 'tensor'))
- tokens_grad: bfloat16 [8192, 2048], P(('dp', 'tensor'))
- grad_norm: float32 [], replicated
- updated_attend_in: float32 [2048, 3072], P('dp', 'tensor')
- moment_attend_in_next: float32 [2048, 3072], P('dp', 'tensor')
- square_attend_in_next: float32 [2048, 3072], P('dp', 'tensor')
- updated_attend_out: float32 [2048, 2048], P('tensor', 'dp')
- moment_attend_out_next: float32 [2048, 2048], P('tensor', 'dp')
- square_attend_out_next: float32 [2048, 2048], P('tensor', 'dp')
- updated_feed_in: float32 [2, 2048, 8192], P(None, 'dp', 'tensor')
- moment_feed_in_next: float32 [2, 2048, 8192], P(None, 'dp', 'tensor')
- square_feed_in_next: float32 [2, 2048, 8192], P(None, 'dp', 'tensor')
- updated_feed_out: float32 [8192, 2048], P('tensor', 'dp')
- moment_feed_out_next: float32 [8192, 2048], P('tensor', 'dp')
- square_feed_out_next: float32 [8192, 2048], P('tensor', 'dp')
- updated_gains: float32 [2, 2048], P(None, 'dp')
- moment_gains_next: float32 [2, 2048], P(None, 'dp')
- square_gains_next: float32 [2, 2048], P(None, 'dp')
The draws below stay inside these ranges and needn't reach their ends.
Inputs may be any that keep to these rules, and one draw needn't show every extreme that they name: `norm_gains`: gains are positive. `square_attend_in`: second moments are positive. `square_attend_out`: second moments are positive. `square_feed_in`: second moments are positive. `square_feed_out`: second moments are positive. `square_gains`: second moments are positive.
All inputs are finite; a program needn't handle non-finite values.
Results may differ from the reference program's by a relative error of at most 0.025.
Values may be sent and summed in bfloat16 or wider, within the bound.
No kernel may reach another device: no remote copies, remote signals or barrier semaphores. Data moves between devices by JAX's collectives and lax.ppermute only.
A program may use at most 256 MiB of HBM per device.

```python
import math
import jax
import jax.numpy as jnp
import numpy as np
from jax import lax

D = 2048
H = 32
KV = 8
HD = 64
FF = 8192
QKVW = 3072
GROUP_ROWS = 1024
TOKENS = 8192
DOCS = 2
MOST_DOC = 768
STEP = 10
NPARAM = 60821504
N_DP = 8


CLIP_LIMIT = 0.25


def rising(count, low_end, high_end):
    return low_end + (high_end - low_end) * jnp.arange(count, dtype=jnp.float32) / (count - 1)


def bounded_normal(key, shape):
    return jax.random.truncated_normal(key, -4.0, 4.0, shape, jnp.float32)


def output_share():
    return min(1.0, math.sqrt(36.0 / GROUP_ROWS))


def first_moment(key, shape, share):
    entry_scale = share * CLIP_LIMIT / math.sqrt(NPARAM)
    return bounded_normal(key, shape) * (entry_scale / 9.0)


def second_moment(key, shape, share):
    entry_scale = share * CLIP_LIMIT / math.sqrt(NPARAM)
    logs = jax.random.uniform(key, shape, jnp.float32, math.log(1.0 / 19.0), math.log(4.0 / 19.0))
    return jnp.exp(logs) * (entry_scale * entry_scale)


def draw_cotangent(key, part):
    key = jax.random.fold_in(key, 1)
    base = bounded_normal(key, (TOKENS, D))
    factor = rising(D, 0.6, 1.4)
    return (base * factor[None, :]).astype(jnp.bfloat16)


def draw_attend_out(key, part):
    key = jax.random.fold_in(key, 2)
    fan = max(1, D * 8 // GROUP_ROWS)
    factor = rising(H, 0.6, 1.4)
    rows_factor = jnp.repeat(factor, HD)
    return bounded_normal(key, (H * HD, D)) / math.sqrt(fan) * rows_factor[:, None]


def draw_feed_in(key, part):
    key = jax.random.fold_in(key, 3)
    factor = rising(FF, 0.6, 1.4)
    columns = jnp.stack([jnp.ones((FF,), jnp.float32), factor])
    return bounded_normal(key, (2, D, FF)) / math.sqrt(D) * columns[:, None, :]


def draw_feed_out(key, part):
    key = jax.random.fold_in(key, 4)
    factor = rising(FF, 0.6, 1.4)
    return bounded_normal(key, (FF, D)) / math.sqrt(FF) * factor[:, None]


def draw_norm_gains(key, part):
    key = jax.random.fold_in(key, 5)
    factor = rising(D, 0.6, 1.4)
    return factor[None, :] * jax.random.uniform(key, (2, D), jnp.float32, 0.6, 1.4)


def draw_moment_attend_in(key, part):
    key = jax.random.fold_in(key, 11)
    return first_moment(key, (D, QKVW), 1.0)


def draw_square_attend_in(key, part):
    key = jax.random.fold_in(key, 12)
    return second_moment(key, (D, QKVW), 1.0)


def draw_moment_attend_out(key, part):
    key = jax.random.fold_in(key, 13)
    return first_moment(key, (H * HD, D), output_share())


def draw_square_attend_out(key, part):
    key = jax.random.fold_in(key, 14)
    return second_moment(key, (H * HD, D), output_share())


def draw_moment_feed_in(key, part):
    key = jax.random.fold_in(key, 15)
    return first_moment(key, (2, D, FF), 1.0)


def draw_square_feed_in(key, part):
    key = jax.random.fold_in(key, 16)
    return second_moment(key, (2, D, FF), 1.0)


def draw_moment_feed_out(key, part):
    key = jax.random.fold_in(key, 17)
    return first_moment(key, (FF, D), 1.0)


def draw_square_feed_out(key, part):
    key = jax.random.fold_in(key, 18)
    return second_moment(key, (FF, D), 1.0)


def draw_moment_gains(key, part):
    key = jax.random.fold_in(key, 19)
    return first_moment(key, (2, D), 1.0)


def draw_square_gains(key, part):
    key = jax.random.fold_in(key, 20)
    return second_moment(key, (2, D), 1.0)


def block_levels(key, shape, shards, least, top_value):
    def one(dim, parts):
        draws = jax.random.uniform(jax.random.fold_in(jax.random.fold_in(key, 6), dim), (parts,), jnp.float32, least / len(shards), top_value / len(shards))
        return jnp.repeat(jnp.exp(draws), shape[dim] // parts).reshape((-1,) + (1,) * (len(shape) - dim - 1))

    loudness = one(*shards[0])
    for cut in shards[1:]:
        loudness = loudness * one(*cut)
    return loudness


def split_up(count, total, most, slope):
    portions = [(1 << 20) // math.isqrt(grade ** slope) + 1 for grade in range(2, count + 1)]
    surplus, given = total - most - (count - 1), [1] * (count - 1)
    while surplus > 0:
        free = [i for i in range(count - 1) if given[i] < most]
        pool, remaining = sum([portions[i] for i in free]), surplus
        for i in free:
            extra = min(most - given[i], max(1, remaining * portions[i] // pool), surplus)
            given[i] = given[i] + extra
            surplus = surplus - extra
    return np.array([most] + given)


def uneven_parts(rng, number_of, total, limit, lean):
    if number_of == 2:
        one = jax.random.randint(rng, (), max(1, total - limit), min(limit, total - 1) + 1)
        return jnp.stack([one, total - one])
    tallies = jnp.asarray(split_up(number_of, total, limit, lean), jnp.int32)
    couples = (number_of - 1) // 2
    source_of, receiver = tallies[1:1 + 2 * couples:2], tallies[2:2 + 2 * couples:2]
    slack = jnp.minimum(source_of - 1, limit - receiver)
    shifted = jax.random.randint(jax.random.fold_in(rng, 1), (couples,), 0, 1 << 20) % (slack + 1)
    tallies = tallies.at[1:1 + 2 * couples:2].set(source_of - shifted).at[2:2 + 2 * couples:2].set(receiver + shifted)
    return tallies[jax.random.permutation(jax.random.fold_in(rng, 2), number_of)]


def centred(rng, shape, scale, most, split=(), kind=jnp.bfloat16):
    values = jax.random.normal(rng, shape, jnp.float32) * scale
    if len(split) > 0:
        values = block_levels(rng, shape, split, -0.22, 0.18) * values
    return jnp.clip(values, min=-most, max=most).astype(kind)


def setup_inputs(seed: int = 0) -> dict:
    seeds = jax.random.split(jax.random.key(seed), 19)
    return {
        "tokens": centred(seeds[0], (TOKENS, D), 1.0, 6.0, ((0, 32),)),
        "cotangent": draw_cotangent(jax.random.fold_in(seeds[18], 71), 0),
        "doc_lengths": jax.vmap(lambda own: uneven_parts(own, DOCS, GROUP_ROWS, MOST_DOC, 2))(jax.random.split(seeds[2], N_DP)).reshape((N_DP, DOCS)).astype(jnp.int32),
        "attend_in": centred(seeds[3], (D, QKVW), D ** -0.5, 0.125, ((0, 8), (1, 4)), jnp.float32),
        "attend_out": draw_attend_out(jax.random.fold_in(seeds[18], 71), 0),
        "feed_in": draw_feed_in(jax.random.fold_in(seeds[18], 71), 0),
        "feed_out": draw_feed_out(jax.random.fold_in(seeds[18], 71), 0),
        "norm_gains": draw_norm_gains(jax.random.fold_in(seeds[18], 71), 0),
        "moment_attend_in": draw_moment_attend_in(jax.random.fold_in(seeds[18], 71), 0),
        "square_attend_in": draw_square_attend_in(jax.random.fold_in(seeds[18], 71), 0),
        "moment_attend_out": draw_moment_attend_out(jax.random.fold_in(seeds[18], 71), 0),
        "square_attend_out": draw_square_attend_out(jax.random.fold_in(seeds[18], 71), 0),
        "moment_feed_in": draw_moment_feed_in(jax.random.fold_in(seeds[18], 71), 0),
        "square_feed_in": draw_square_feed_in(jax.random.fold_in(seeds[18], 71), 0),
        "moment_feed_out": draw_moment_feed_out(jax.random.fold_in(seeds[18], 71), 0),
        "square_feed_out": draw_square_feed_out(jax.random.fold_in(seeds[18], 71), 0),
        "moment_gains": draw_moment_gains(jax.random.fold_in(seeds[18], 71), 0),
        "square_gains": draw_square_gains(jax.random.fold_in(seeds[18], 71), 0),
    }


EPSILON = 1e-05
NEGATIVE = -1e+30
CLIP_LIMIT = 0.25
BETA_ONE = 0.9
BETA_TWO = 0.95
ADAM_EPSILON = 1e-08
MATRIX_RATE = 0.04
OUTPUT_RATE = 0.3
MATRIX_DECAY = 0.1
GAIN_RATE = 0.6
HIGHEST = lax.Precision.HIGHEST

@jax.custom_vjp
def low(v):
    return lax.optimization_barrier(v.astype(jnp.bfloat16)).astype(jnp.float32)

@jax.custom_vjp
def low_back(v):
    return v

def low_keep(v):
    return (low(v), None)

def low_pass(kept, grad):
    return (grad,)

def back_keep(v):
    return (v, None)

def back_low(kept, grad):
    return (low(grad),)
low.defvjp(low_keep, low_pass)
low_back.defvjp(back_keep, back_low)

def frequencies(head_size):
    half_index = jnp.arange(head_size // 2, dtype=jnp.float32)
    inverse = jnp.power(500000.0, -2.0 * half_index / head_size)
    wavelength = 2.0 * math.pi / inverse
    smooth = (8192.0 / wavelength - 1.0) / 3.0
    blended = (1.0 - smooth) * inverse / 32.0 + smooth * inverse
    return jnp.where(wavelength < 2048.0, inverse, jnp.where(wavelength > 8192.0, inverse / 32.0, blended))

def documents(lengths_row, rows):
    token_ids = jnp.arange(rows, dtype=jnp.int32)
    lengths_int = lengths_row.astype(jnp.int32)
    ends = jnp.cumsum(lengths_int).astype(jnp.int32)
    past = (token_ids[:, None] >= ends[None, :]).astype(jnp.int32)
    segments = lax.optimization_barrier(jnp.sum(past, axis=1)).astype(jnp.int32)
    positions = token_ids - lax.optimization_barrier(jnp.sum(past * lengths_int[None, :], axis=1)).astype(jnp.int32)
    return (token_ids, segments, positions)

def rotate(block, cosine, sine):
    half = block.shape[-1] // 2
    first = block[..., :half]
    second = block[..., half:]
    return jnp.concatenate([first * cosine - second * sine, second * cosine + first * sine], axis=-1)

def rms_scale(vector, gain):
    return vector * lax.rsqrt(lax.optimization_barrier(jnp.mean(vector * vector, axis=-1, keepdims=True)) + EPSILON) * gain

def attend(queries, keys, values, token_ids, segments):
    rows = queries.shape[0]
    block_rows = min(512, rows)
    scale = HD ** (-0.5)

    def one_block(index):
        start = (index * block_rows).astype(jnp.int32)
        query_block = lax.dynamic_slice_in_dim(queries, start, block_rows, 0)
        query_ids = lax.dynamic_slice_in_dim(token_ids, start, block_rows, 0)
        query_segments = lax.dynamic_slice_in_dim(segments, start, block_rows, 0)
        allowed = (query_segments[:, None] == segments[None, :]) & (query_ids[:, None] >= token_ids[None, :])
        scores = low_back(jnp.einsum('qkgd,tkd->kgqt', query_block, keys, precision=HIGHEST) * scale)
        scores = jnp.where(allowed[None, None], scores, NEGATIVE)
        peak = lax.optimization_barrier(jnp.max(scores, axis=-1, keepdims=True))
        raised = jnp.exp(scores - peak)
        probs = low(raised / lax.optimization_barrier(jnp.sum(raised, axis=-1, keepdims=True)))
        return jnp.einsum('kgqt,tkd->qkgd', probs, values, precision=HIGHEST)
    blocks = lax.map(jax.checkpoint(one_block), jnp.arange(rows // block_rows, dtype=jnp.int32))
    return blocks.reshape(queries.shape)

def layer(params, inputs, token_ids, segments, cosine, sine):
    attend_in, attend_out, feed_in, feed_out, gains = params
    rows = inputs.shape[0]
    group = H // KV
    normed_one = low(rms_scale(inputs, gains[0]))
    joined = low_back(jnp.dot(normed_one, attend_in, precision=HIGHEST))
    joined = joined.reshape(rows, KV, group + 2, HD)
    queries = low(rotate(joined[:, :, :group], cosine[:, None, None, :], sine[:, None, None, :]))
    keys = low(rotate(joined[:, :, group], cosine[:, None, :], sine[:, None, :]))
    values = low(joined[:, :, group + 1])
    attended = attend(queries, keys, values, token_ids, segments)
    attended = low(low_back(attended)).reshape(rows, H * HD)
    hidden_state = inputs + low_back(jnp.dot(attended, attend_out, precision=HIGHEST))
    normed_two = low(rms_scale(hidden_state, gains[1]))
    gate_up = low_back(jnp.einsum('sd,kdf->ksf', normed_two, feed_in, precision=HIGHEST))
    activated = low(jax.nn.silu(gate_up[0]) * gate_up[1])
    return hidden_state + low_back(jnp.dot(activated, feed_out, precision=HIGHEST))

def adam(weight, grad, moment, square, clip, rate, decay):
    clipped = clip * grad
    moment_new = BETA_ONE * moment + (1.0 - BETA_ONE) * clipped
    square_new = BETA_TWO * square + (1.0 - BETA_TWO) * clipped * clipped
    direction = moment_new / (1.0 - BETA_ONE ** STEP) / (jnp.sqrt(square_new / (1.0 - BETA_TWO ** STEP)) + ADAM_EPSILON)
    return (weight - rate * (direction + decay * weight), moment_new, square_new)

def reference(tokens, cotangent, doc_lengths, attend_in, attend_out, feed_in, feed_out, norm_gains, moment_attend_in, square_attend_in, moment_attend_out, square_attend_out, moment_feed_in, square_feed_in, moment_feed_out, square_feed_out, moment_gains, square_gains):
    masters = (attend_in, attend_out, feed_in, feed_out, norm_gains)
    params = tuple((low(weight) for weight in masters))
    inputs_all = tokens.astype(jnp.float32).reshape(N_DP, GROUP_ROWS, D)
    back_all = cotangent.astype(jnp.float32).reshape(N_DP, GROUP_ROWS, D)
    table = frequencies(HD)

    def one_group(totals, pieces):
        inputs, back, lengths_row = pieces
        token_ids, segments, positions = documents(lengths_row, GROUP_ROWS)
        angles = positions.astype(jnp.float32)[:, None] * table[None, :]
        cosine = jnp.cos(angles)
        sine = jnp.sin(angles)

        def forward(weights, rows_in):
            return layer(weights, rows_in, token_ids, segments, cosine, sine)
        result, pull = jax.vjp(forward, params, inputs)
        weight_grads, input_grad = pull(back)
        totals = jax.tree.map(lambda left, right: left + right, totals, weight_grads)
        return (totals, (result.astype(jnp.bfloat16), input_grad.astype(jnp.bfloat16)))
    zeros = tuple((jnp.zeros_like(weight) for weight in params))
    totals, (outputs, input_grads) = lax.scan(one_group, zeros, (inputs_all, back_all, doc_lengths))
    grads = tuple((total / TOKENS for total in totals))
    squares = jnp.zeros((), jnp.float32)
    for grad in grads:
        squares = squares + jnp.sum(grad * grad)
    grad_norm = jnp.sqrt(squares)
    clip = jnp.minimum(1.0, CLIP_LIMIT / (grad_norm + 1e-06))
    first = adam(attend_in, grads[0], moment_attend_in, square_attend_in, clip, MATRIX_RATE, MATRIX_DECAY)
    second = adam(attend_out, grads[1], moment_attend_out, square_attend_out, clip, OUTPUT_RATE, MATRIX_DECAY)
    third = adam(feed_in, grads[2], moment_feed_in, square_feed_in, clip, MATRIX_RATE, MATRIX_DECAY)
    fourth = adam(feed_out, grads[3], moment_feed_out, square_feed_out, clip, MATRIX_RATE, MATRIX_DECAY)
    fifth = adam(norm_gains, grads[4], moment_gains, square_gains, clip, GAIN_RATE, 0.0)
    return (outputs.reshape(TOKENS, D), input_grads.reshape(TOKENS, D), grad_norm, first[0], first[1], first[2], second[0], second[1], second[2], third[0], third[1], third[2], fourth[0], fourth[1], fourth[2], fifth[0], fifth[1], fifth[2])
```

```python
import functools
import math

import jax
import jax.numpy as jnp
from jax import lax
from jax.experimental import pallas as pl
from jax.experimental.pallas import tpu as pltpu
from jax.sharding import Mesh
from jax.sharding import PartitionSpec as P

H = 32
KV = 8
HD = 64
GROUP = H // KV
STEP = 10
LANES = 128
QUERY_ROWS = 256
CHUNKS = 2

EPSILON = 1e-05
NEGATIVE = -1e30
CLIP_LIMIT = 0.25
BETA_ONE = 0.9
BETA_TWO = 0.95
ADAM_EPSILON = 1e-08
MATRIX_RATE = 0.04
OUTPUT_RATE = 0.3
MATRIX_DECAY = 0.1
GAIN_RATE = 0.6

BF16 = jnp.bfloat16
F32 = jnp.float32


def flip(value, axes, sizes):
    count = math.prod(sizes[a] for a in axes)
    pairs = [(i, i ^ (count - 1)) for i in range(count)]
    return lax.ppermute(value, tuple(axes), pairs)


def combos(axes):
    return [
        tuple(a for i, a in enumerate(axes) if place >> (len(axes) - 1 - i) & 1)
        for place in range(2 ** len(axes))
    ]


def spread(block, links, core, sizes):
    parts = [block] + [flip(block, c, sizes) for c in combos(links)[1:]]
    mine = jnp.concatenate(parts, axis=0) if len(parts) > 1 else block
    return jnp.concatenate([mine, flip(mine, (core,), sizes)], axis=0)


def collect(partial, links, core, sizes):
    half = partial.shape[0] // 2
    near = flip(partial[half:], (core,), sizes)
    mine = (partial[:half].astype(F32) + near.astype(F32)).astype(BF16)
    places = combos(links)
    rows = half // len(places)
    total = mine[:rows].astype(F32)
    for place, c in enumerate(places):
        if place:
            total = total + flip(mine[place * rows : (place + 1) * rows], c, sizes).astype(F32)
    return total


def frequencies(head_size):
    half_index = jnp.arange(head_size // 2, dtype=F32)
    inverse = jnp.power(500000.0, -2.0 * half_index / head_size)
    wavelength = 2.0 * math.pi / inverse
    smooth = (8192.0 / wavelength - 1.0) / 3.0
    blended = (1.0 - smooth) * inverse / 32.0 + smooth * inverse
    return jnp.where(
        wavelength < 2048.0, inverse, jnp.where(wavelength > 8192.0, inverse / 32.0, blended)
    )


def rotation_tables(lengths_row, rows):
    token_ids = jnp.arange(rows, dtype=jnp.int32)
    ends = jnp.cumsum(lengths_row)
    past = (token_ids[:, None] >= ends[None, :]).astype(jnp.int32)
    positions = token_ids - jnp.sum(past * lengths_row[None, :], axis=1)
    angles = positions.astype(F32)[:, None] * frequencies(HD)[None, :]
    cosine, sine = jnp.cos(angles), jnp.sin(angles)
    return (
        jnp.concatenate([cosine] * 4, axis=1),
        jnp.concatenate([-sine, sine, -sine, sine], axis=1),
    )


def exchange_halves(tile):
    lane = lax.broadcasted_iota(jnp.int32, tile.shape, 1)
    return jnp.where(
        lane % HD < HD // 2,
        pltpu.roll(tile, LANES - HD // 2, 1),
        pltpu.roll(tile, HD // 2, 1),
    )


def block_place(meta_ref, j, devices):
    relative = meta_ref[0] ^ j
    return (relative & 1) * (devices // 2) + (relative >> 1)


def allowed_bias(meta_ref, docs, first, keys, queries):
    token = lax.broadcasted_iota(jnp.int32, (1, queries), 1) + first
    start = jnp.zeros((1, queries), jnp.int32)
    for j in range(docs - 1):
        start = jnp.where(token >= meta_ref[1 + j], meta_ref[1 + j], start)
    other = lax.broadcasted_iota(jnp.int32, (keys, queries), 0)
    return jnp.where((other <= token) & (other >= start), 0.0, NEGATIVE)


def last_dims(left, right):
    return lax.dot_general(left, right, (((1,), (1,)), ((), ())), preferred_element_type=F32)


def key_halves(qkv_ref, keep_keys, keep_values, keep_turned):
    tile = qkv_ref[:, 2 * LANES : 3 * LANES].astype(F32)
    lane = lax.broadcasted_iota(jnp.int32, tile.shape, 1)
    low = jnp.where(lane < HD, tile, 0.0)
    high = jnp.where(lane < HD, 0.0, tile)
    pairs = ((low, pltpu.roll(low, HD, 1)), (pltpu.roll(high, HD, 1), high))
    for half in range(2):
        if keep_keys is not None:
            keep_keys[half] = pairs[0][half].astype(BF16)
        if keep_values is not None:
            keep_values[half] = pairs[1][half].astype(BF16)
        if keep_turned is not None:
            source, ref = keep_turned
            ref[half] = pairs[source][half].T.astype(BF16)


def forward_kernel(docs, devices, meta_ref, joined_ref, cos_ref, sin_ref, attended_ref, qkv_ref, log_ref, keys_ref, turned_ref):
    rows = joined_ref.shape[0]
    block = rows // devices
    for j in range(devices):
        source = pl.multiple_of(block_place(meta_ref, j, devices) * block, block)
        here = slice(j * block, (j + 1) * block)
        cosine, sine = cos_ref[here, :], sin_ref[here, :]
        lane = lax.broadcasted_iota(jnp.int32, cosine.shape, 1)
        for t in range(3):
            tile = joined_ref[pl.ds(source, block), t * LANES : (t + 1) * LANES]
            turned = tile * cosine + exchange_halves(tile) * sine
            if t == 2:
                turned = jnp.where(lane < HD, turned, tile)
            qkv_ref[here, t * LANES : (t + 1) * LANES] = turned.astype(BF16)
    key_halves(qkv_ref, keys_ref, None, (1, turned_ref))
    for i in range(rows // QUERY_ROWS):
        keys = (i + 1) * QUERY_ROWS
        here = slice(i * QUERY_ROWS, keys)
        bias = allowed_bias(meta_ref, docs, i * QUERY_ROWS, keys, QUERY_ROWS)
        for t in range(2):
            query = qkv_ref[here, t * LANES : (t + 1) * LANES] * BF16(HD**-0.5)
            total = jnp.zeros((LANES, QUERY_ROWS), F32)
            for half in range(2):
                scores = last_dims(keys_ref[half, :keys, :], query) + bias
                peak = jnp.max(scores, axis=0, keepdims=True)
                raised = jnp.exp(scores - peak)
                mass = jnp.sum(raised, axis=0, keepdims=True)
                probs = (raised * (1.0 / mass)).astype(BF16)
                total = total + jnp.dot(
                    turned_ref[half, :, :keys], probs, preferred_element_type=F32
                )
                head = 2 * t + half
                log_ref[0, head : head + 1, here] = peak + jnp.log(mass)
            done = total.T.astype(BF16)
            step = min(block, QUERY_ROWS)
            for part in range(QUERY_ROWS // step):
                first = i * QUERY_ROWS + part * step
                place = block_place(meta_ref, first // block, devices) * block + first % block
                attended_ref[
                    pl.ds(pl.multiple_of(place, step), step), t * LANES : (t + 1) * LANES
                ] = done[part * step : (part + 1) * step, :]


def backward_kernel(docs, devices, meta_ref, qkv_ref, log_ref, back_ref, cos_ref, sin_ref, grad_ref, keys_ref, values_ref, turned_ref, key_total, value_total, query_total, back_here):
    rows = qkv_ref.shape[0]
    block = rows // devices
    key_halves(qkv_ref, keys_ref, values_ref, (0, turned_ref))
    for j in range(devices):
        source = pl.multiple_of(block_place(meta_ref, j, devices) * block, block)
        back_here[j * block : (j + 1) * block, :] = back_ref[pl.ds(source, block), :]
    key_total[...] = jnp.zeros_like(key_total)
    value_total[...] = jnp.zeros_like(value_total)
    for i in range(rows // QUERY_ROWS):
        keys = (i + 1) * QUERY_ROWS
        here = slice(i * QUERY_ROWS, keys)
        bias = allowed_bias(meta_ref, docs, i * QUERY_ROWS, keys, QUERY_ROWS)
        lane = lax.broadcasted_iota(jnp.int32, (QUERY_ROWS, LANES), 1)
        for t in range(2):
            columns = slice(t * LANES, (t + 1) * LANES)
            query = qkv_ref[here, columns] * BF16(HD**-0.5)
            back = back_here[here, columns]
            total = jnp.zeros((LANES, QUERY_ROWS), F32)
            for half in range(2):
                head = 2 * t + half
                mine = (lane < HD) if half == 0 else (lane >= HD)
                scores = last_dims(keys_ref[half, :keys, :], query) + bias
                probs = jnp.exp(scores - log_ref[0, head : head + 1, here])
                moved = last_dims(values_ref[half, :keys, :], back)
                inner = jnp.sum(probs * moved, axis=0, keepdims=True)
                grad = (probs * (moved - inner)).astype(BF16)
                total = total + jnp.dot(
                    turned_ref[half, :, :keys], grad, preferred_element_type=F32
                )
                key_total[:keys, :] += jnp.dot(
                    grad, jnp.where(mine, query, BF16(0)), preferred_element_type=F32
                )
                value_total[:keys, :] += jnp.dot(
                    probs.astype(BF16), jnp.where(mine, back, BF16(0)), preferred_element_type=F32
                )
            query_total[here, columns] = total.T * HD**-0.5
    for j in range(devices):
        place = pl.multiple_of(block_place(meta_ref, j, devices) * block, block)
        here = slice(j * block, (j + 1) * block)
        cosine, sine = cos_ref[here, :], sin_ref[here, :]
        lane = lax.broadcasted_iota(jnp.int32, cosine.shape, 1)
        for t in range(2):
            columns = slice(t * LANES, (t + 1) * LANES)
            tile = query_total[here, columns]
            grad_ref[pl.ds(place, block), columns] = (
                tile * cosine - exchange_halves(tile) * sine
            ).astype(BF16)
        tile = key_total[here, :]
        tile = tile + pltpu.roll(tile, HD, 1)
        other = value_total[here, :]
        other = other + pltpu.roll(other, HD, 1)
        tile = jnp.where(lane < HD, tile * cosine - exchange_halves(tile) * sine, other)
        grad_ref[pl.ds(place, block), 2 * LANES : 3 * LANES] = tile.astype(BF16)


def attend_forward(meta, joined, cosine, sine, docs, devices):
    rows, width = joined.shape
    wide = (GROUP + 2) * HD
    groups = width // wide
    whole = pl.BlockSpec((rows, LANES), lambda g: (0, 0))
    return pl.pallas_call(
        functools.partial(forward_kernel, docs, devices),
        grid=(groups,),
        in_specs=[
            pl.BlockSpec(memory_space=pltpu.SMEM),
            pl.BlockSpec((rows, wide), lambda g: (0, g)),
            whole,
            whole,
        ],
        out_specs=[
            pl.BlockSpec((rows, GROUP * HD), lambda g: (0, g)),
            pl.BlockSpec((rows, wide), lambda g: (0, g)),
            pl.BlockSpec((1, 8, rows), lambda g: (g, 0, 0)),
        ],
        out_shape=[
            jax.ShapeDtypeStruct((rows, groups * GROUP * HD), BF16),
            jax.ShapeDtypeStruct((rows, width), BF16),
            jax.ShapeDtypeStruct((groups, 8, rows), F32),
        ],
        scratch_shapes=[
            pltpu.VMEM((2, rows, LANES), BF16),
            pltpu.VMEM((2, LANES, rows), BF16),
        ],
        compiler_params=pltpu.CompilerParams(vmem_limit_bytes=32 * 2**20),
        cost_estimate=pl.CostEstimate(
            flops=groups * GROUP * rows * rows * LANES * 4,
            bytes_accessed=rows * width * 8,
            transcendentals=groups * GROUP * rows * rows // 2,
        ),
        name="attend_forward",
    )(meta, joined, cosine, sine)


def attend_backward(meta, qkv, logs, back, cosine, sine, docs, devices):
    rows, width = qkv.shape
    wide = (GROUP + 2) * HD
    groups = width // wide
    whole = pl.BlockSpec((rows, LANES), lambda g: (0, 0))
    return pl.pallas_call(
        functools.partial(backward_kernel, docs, devices),
        grid=(groups,),
        in_specs=[
            pl.BlockSpec(memory_space=pltpu.SMEM),
            pl.BlockSpec((rows, wide), lambda g: (0, g)),
            pl.BlockSpec((1, 8, rows), lambda g: (g, 0, 0)),
            pl.BlockSpec((rows, GROUP * HD), lambda g: (0, g)),
            whole,
            whole,
        ],
        out_specs=pl.BlockSpec((rows, wide), lambda g: (0, g)),
        out_shape=jax.ShapeDtypeStruct((rows, width), BF16),
        scratch_shapes=[
            pltpu.VMEM((2, rows, LANES), BF16),
            pltpu.VMEM((2, rows, LANES), BF16),
            pltpu.VMEM((2, LANES, rows), BF16),
            pltpu.VMEM((rows, LANES), F32),
            pltpu.VMEM((rows, LANES), F32),
            pltpu.VMEM((rows, GROUP * HD), F32),
            pltpu.VMEM((rows, GROUP * HD), BF16),
        ],
        compiler_params=pltpu.CompilerParams(vmem_limit_bytes=32 * 2**20),
        cost_estimate=pl.CostEstimate(
            flops=groups * GROUP * rows * rows * LANES * 10,
            bytes_accessed=rows * width * 8,
            transcendentals=groups * GROUP * rows * rows // 2,
        ),
        name="attend_backward",
    )(meta, qkv, logs, back, cosine, sine)


def product(left, right, left_dim, right_dim):
    return lax.dot_general(
        left, right, (((left_dim,), (right_dim,)), ((), ())), preferred_element_type=F32
    )


def norm_rate(vector):
    return lax.rsqrt(jnp.mean(vector * vector, axis=-1, keepdims=True) + EPSILON)


def norm_back(vector, rate, gain, grad):
    scaled = gain * grad
    inner = jnp.mean(vector * scaled, axis=-1, keepdims=True)
    return (
        rate * scaled - vector * (rate * rate * rate * inner),
        jnp.sum(grad * vector * rate, axis=0),
    )


def adam(weight, grad, moment, square, clip, rate, decay):
    clipped = clip * grad
    moment_new = BETA_ONE * moment + (1.0 - BETA_ONE) * clipped
    square_new = BETA_TWO * square + (1.0 - BETA_TWO) * clipped * clipped
    direction = (
        moment_new
        / (1.0 - BETA_ONE**STEP)
        / (jnp.sqrt(square_new / (1.0 - BETA_TWO**STEP)) + ADAM_EPSILON)
    )
    return (weight - rate * (direction + decay * weight), moment_new, square_new)


def in_order(mine, other, first, axis):
    return jnp.where(
        first,
        jnp.concatenate([mine, other], axis=axis),
        jnp.concatenate([other, mine], axis=axis),
    )


def shards(
    sizes,
    tensor,
    tokens,
    cotangent,
    doc_lengths,
    attend_in,
    attend_out,
    feed_in,
    feed_out,
    norm_gains,
    moment_attend_in,
    square_attend_in,
    moment_attend_out,
    square_attend_out,
    moment_feed_in,
    square_feed_in,
    moment_feed_out,
    square_feed_out,
    moment_gains,
    square_gains,
):
    pack_links, core = tensor[:-1], tensor[-1]
    feed_links = ("x",) + tuple(pack_links)
    devices = math.prod(sizes[a] for a in tensor)
    side = lax.axis_index("x")
    is_first = side == 0
    local_rows, width = tokens.shape
    rows = local_rows * devices
    token_total = rows * 2 * sizes["z"]
    inverse_total = 1.0 / token_total
    docs = doc_lengths.shape[1]
    meta = jnp.concatenate(
        [lax.axis_index(tuple(tensor))[None].astype(jnp.int32), jnp.cumsum(doc_lengths[0])]
    )
    cosine, sine = rotation_tables(doc_lengths[0], rows)

    attend_in_z = lax.all_gather(attend_in.astype(BF16), "z", axis=0, tiled=False)
    attend_in_x = flip(attend_in_z, ("x",), sizes)
    full_in = jnp.where(
        is_first,
        jnp.stack([attend_in_z, attend_in_x], axis=1),
        jnp.stack([attend_in_x, attend_in_z], axis=1),
    ).reshape(width, attend_in.shape[1])
    gains = lax.all_gather(norm_gains.astype(BF16), ("z", "x"), axis=1, tiled=True).astype(F32)
    attend_out_z = lax.all_gather(attend_out.T.astype(BF16), "z", axis=0, tiled=False)
    attend_out_x = flip(attend_out_z, ("x",), sizes)
    full_out = jnp.where(
        is_first,
        jnp.stack([attend_out_z, attend_out_x], axis=1),
        jnp.stack([attend_out_x, attend_out_z], axis=1),
    ).reshape(width, attend_out.shape[0])

    hidden = feed_in.shape[2] // 2
    slim = hidden // CHUNKS

    def halves(array, axis):
        size = array.shape[axis] // 2
        mine = lax.dynamic_slice_in_dim(array, side * size, size, axis)
        other = lax.dynamic_slice_in_dim(array, (1 - side) * size, size, axis)
        return mine, other

    in_mine, in_other = halves(feed_in.astype(BF16), 2)
    out_mine, out_other = halves(feed_out.T.astype(BF16), 1)
    weights = []
    for c in range(CHUNKS):
        cut = slice(c * slim, (c + 1) * slim)
        mine = jnp.concatenate([in_mine[0, :, cut], in_mine[1, :, cut], out_mine[:, cut]], axis=1)
        other = jnp.concatenate(
            [in_other[0, :, cut], in_other[1, :, cut], out_other[:, cut]], axis=1
        )
        local = in_order(mine, flip(other, ("x",), sizes), is_first, 0)
        weights.append(
            (
                lax.all_gather(local[:, : 2 * slim], "z", axis=0, tiled=True),
                lax.all_gather(local[:, 2 * slim :], "z", axis=0, tiled=True),
            )
        )

    inputs_all = spread(tokens, pack_links, core, sizes).astype(F32)
    normed_one = (inputs_all * norm_rate(inputs_all) * gains[0]).astype(BF16)
    joined = product(normed_one, full_in, 1, 0)
    attended, qkv, logs = attend_forward(meta, joined, cosine, sine, docs, devices)
    branch_one = collect(product(attended, full_out, 1, 1).astype(BF16), pack_links, core, sizes)
    inputs = tokens.astype(F32)
    hidden_state = inputs + branch_one
    rate_two = norm_rate(hidden_state)
    normed_two = (hidden_state * rate_two * gains[1]).astype(BF16)
    gathered_two = spread(normed_two, feed_links, core, sizes)
    gathered_back = spread(cotangent, feed_links, core, sizes)

    feed_in_parts, feed_out_parts = [], []
    forward_total, backward_total = 0.0, 0.0
    for c in range(CHUNKS):
        weight_in, weight_out = weights[c]
        gate_up = product(gathered_two, weight_in, 1, 0)
        grad_activated = product(gathered_back, weight_out, 1, 0)
        gate, upward = gate_up[:, :slim], gate_up[:, slim:]
        chance = jax.nn.sigmoid(gate)
        silu = gate * chance
        activated = (silu * upward).astype(BF16)
        grad_gate = grad_activated * upward * (chance * (1.0 + gate * (1.0 - chance)))
        grad_upward = grad_activated * silu
        grad_gate_up = jnp.concatenate([grad_gate.astype(BF16), grad_upward.astype(BF16)], axis=1)
        feed_out_parts.append(
            lax.psum_scatter(
                (product(gathered_back, activated, 0, 0) * inverse_total).astype(BF16),
                "z",
                scatter_dimension=0,
                tiled=True,
            )
        )
        feed_in_parts.append(
            lax.psum_scatter(
                (product(gathered_two, grad_gate_up, 0, 0) * inverse_total).astype(BF16),
                "z",
                scatter_dimension=0,
                tiled=True,
            )
        )
        backward_total = backward_total + product(grad_gate_up, weight_in, 1, 1)
        forward_total = forward_total + product(activated, weight_out, 1, 1)
    grad_normed_two = collect(backward_total.astype(BF16), feed_links, core, sizes)
    branch_two = collect(forward_total.astype(BF16), feed_links, core, sizes)
    block_out = (hidden_state + branch_two).astype(BF16)

    grad_from_two, gain_two_grad = norm_back(hidden_state, rate_two, gains[1], grad_normed_two)
    grad_hidden = cotangent.astype(F32) + grad_from_two
    gathered_grad = spread(grad_hidden.astype(BF16), pack_links, core, sizes)
    grad_attended = product(gathered_grad, full_out, 1, 0).astype(BF16)
    grad_joined = attend_backward(meta, qkv, logs, grad_attended, cosine, sine, docs, devices)
    grad_normed_one = collect(
        product(grad_joined, full_in, 1, 1).astype(BF16), pack_links, core, sizes
    )
    grad_from_one, gain_one_grad = norm_back(inputs, norm_rate(inputs), gains[0], grad_normed_one)
    tokens_grad = (grad_hidden + grad_from_one).astype(BF16)

    def sum_documents(grad):
        split = (grad * inverse_total).astype(BF16).reshape(sizes["z"], 2, -1, grad.shape[1])
        mine = lax.dynamic_index_in_dim(split, side, 1, keepdims=False)
        other = lax.dynamic_index_in_dim(split, 1 - side, 1, keepdims=False)
        both = (mine.astype(F32) + flip(other, ("x",), sizes).astype(F32)).astype(BF16)
        return lax.psum_scatter(both, "z", scatter_dimension=0, tiled=False).astype(F32)

    attend_out_shard = sum_documents(product(gathered_grad, attended, 0, 0)).T
    attend_in_shard = sum_documents(product(normed_one, grad_joined, 0, 0))

    def regroup(part):
        mine, other = halves(part, 0)
        return in_order(mine[:, None], flip(other, ("x",), sizes)[:, None], is_first, 1)

    pieces_in = [
        regroup(part).reshape(-1, 2, 2, slim) for part in feed_in_parts
    ]
    feed_in_shard = (
        jnp.stack(pieces_in, axis=3)
        .transpose(2, 0, 1, 3, 4)
        .reshape(feed_in.shape)
        .astype(F32)
    )
    pieces_out = [regroup(part) for part in feed_out_parts]
    feed_out_shard = (
        jnp.stack(pieces_out, axis=2).reshape(feed_out.shape[1], feed_out.shape[0]).T.astype(F32)
    )

    matrix_squares = (
        jnp.sum(attend_in_shard * attend_in_shard)
        + jnp.sum(attend_out_shard * attend_out_shard)
        + jnp.sum(feed_in_shard * feed_in_shard)
        + jnp.sum(feed_out_shard * feed_out_shard)
    )
    gain_partial = jnp.stack([gain_one_grad, gain_two_grad]) * inverse_total
    total_squares, gain_grads = lax.psum(
        (matrix_squares, gain_partial), ("z", "x") + tuple(tensor)
    )
    grad_norm = jnp.sqrt(total_squares + jnp.sum(gain_grads * gain_grads))
    clip = jnp.minimum(1.0, CLIP_LIMIT / (grad_norm + 1e-06))
    gain_width = norm_gains.shape[1]
    gain_shard = lax.dynamic_slice_in_dim(
        gain_grads, lax.axis_index(("z", "x")) * gain_width, gain_width, 1
    )
    first = adam(attend_in, attend_in_shard, moment_attend_in, square_attend_in, clip, MATRIX_RATE, MATRIX_DECAY)
    second = adam(attend_out, attend_out_shard, moment_attend_out, square_attend_out, clip, OUTPUT_RATE, MATRIX_DECAY)
    third = adam(feed_in, feed_in_shard, moment_feed_in, square_feed_in, clip, MATRIX_RATE, MATRIX_DECAY)
    fourth = adam(feed_out, feed_out_shard, moment_feed_out, square_feed_out, clip, MATRIX_RATE, MATRIX_DECAY)
    fifth = adam(norm_gains, gain_shard, moment_gains, square_gains, clip, GAIN_RATE, 0.0)
    return (block_out, tokens_grad, grad_norm, *first, *second, *third, *fourth, *fifth)


def solution(mesh):
    depth, across = mesh.shape["dp"], mesh.shape["tensor"]
    tensor = tuple("t" + str(i) for i in range(across.bit_length() - 1))
    sizes = {"z": depth // 2, "x": 2, **{a: 2 for a in tensor}}
    assert depth % 2 == 0 and 2 ** len(tensor) == across
    fine = Mesh(mesh.devices.reshape(tuple(sizes.values())), tuple(sizes))
    dp = ("z", "x")
    both = P(dp + tensor, None)
    rows_cut, columns_cut = P(dp, tensor), P(tensor, dp)
    feed_cut, gain_cut = P(None, dp, tensor), P(None, dp)
    state = (rows_cut,) * 3 + (columns_cut,) * 3 + (feed_cut,) * 3 + (columns_cut,) * 3 + (gain_cut,) * 3
    return jax.shard_map(
        functools.partial(shards, sizes, tensor),
        mesh=fine,
        in_specs=(both, both, P(dp, None), rows_cut, columns_cut, feed_cut, columns_cut, gain_cut)
        + (rows_cut,) * 2
        + (columns_cut,) * 2
        + (feed_cut,) * 2
        + (columns_cut,) * 2
        + (gain_cut,) * 2,
        out_specs=(both, both, P()) + state,
        check_vma=False,
    )
```

```python
import functools
import math

import jax
import jax.numpy as jnp
from jax import lax
from jax.experimental import pallas as pl
from jax.experimental.pallas import tpu as pltpu
from jax.sharding import Mesh
from jax.sharding import PartitionSpec as P

H = 32
KV = 8
HD = 64
GROUP = H // KV
STEP = 10
LANES = 128
QUERY_ROWS = 256
UNITS = 4

EPSILON = 1e-05
NEGATIVE = -1e30
CLIP_LIMIT = 0.25
BETA_ONE = 0.9
BETA_TWO = 0.95
ADAM_EPSILON = 1e-08
MATRIX_RATE = 0.04
OUTPUT_RATE = 0.3
MATRIX_DECAY = 0.1
GAIN_RATE = 0.6

BF16 = jnp.bfloat16
F32 = jnp.float32


def flip(value, axes, sizes):
    count = math.prod(sizes[a] for a in axes)
    pairs = [(i, i ^ (count - 1)) for i in range(count)]
    return lax.ppermute(value, tuple(axes), pairs)


def combos(axes):
    return [
        tuple(a for i, a in enumerate(axes) if place >> (len(axes) - 1 - i) & 1)
        for place in range(2 ** len(axes))
    ]


def add_kernel(mine_ref, near_ref, *out_refs):
    for k, ref in enumerate(out_refs):

        @pl.when(pl.program_id(0) == k)
        def _():
            ref[...] = (mine_ref[...].astype(F32) + near_ref[...].astype(F32)).astype(BF16)


def add_blocks(mine, near, count):
    rows, width = mine.shape[0] // count, mine.shape[1]
    cut = pl.BlockSpec((rows, width), lambda i: (i, 0))
    return pl.pallas_call(
        add_kernel,
        grid=(count,),
        in_specs=[cut, cut],
        out_specs=[pl.BlockSpec((rows, width), lambda i: (0, 0))] * count,
        out_shape=[jax.ShapeDtypeStruct((rows, width), BF16)] * count,
        compiler_params=pltpu.CompilerParams(vmem_limit_bytes=32 * 2**20),
        cost_estimate=pl.CostEstimate(
            flops=mine.size, bytes_accessed=6 * mine.size, transcendentals=0
        ),
        name="add_blocks",
    )(mine, near)


def collect(mine, near, links, core, sizes):
    places = combos(links)
    blocks = add_blocks(mine, flip(near, (core,), sizes), len(places))
    return blocks[0], [flip(block, c, sizes) for block, c in zip(blocks[1:], places[1:])]


def added(own, moved):
    return sum((block.astype(F32) for block in moved), own.astype(F32))


def gather_depth(block, sizes):
    copies = jnp.broadcast_to(block, (sizes["z"],) + block.shape)
    return lax.all_to_all(copies, "z", 0, 0, tiled=True)


def sum_depth(blocks):
    arrived = lax.all_to_all(blocks, "z", 0, 0, tiled=True)
    return jnp.sum(arrived.astype(F32), axis=0).astype(BF16)


def sum_everywhere(value, tensor, sizes):
    for a in tuple(reversed(tensor)) + ("x",):
        value = value + flip(value, (a,), sizes)
    step, count = 1, sizes["z"]
    while step < count:
        value = value + lax.ppermute(value, "z", [(i, i ^ step) for i in range(count)])
        step *= 2
    return value


def frequencies(head_size):
    half_index = jnp.arange(head_size // 2, dtype=F32)
    inverse = jnp.power(500000.0, -2.0 * half_index / head_size)
    wavelength = 2.0 * math.pi / inverse
    smooth = (8192.0 / wavelength - 1.0) / 3.0
    blended = (1.0 - smooth) * inverse / 32.0 + smooth * inverse
    return jnp.where(
        wavelength < 2048.0, inverse, jnp.where(wavelength > 8192.0, inverse / 32.0, blended)
    )


def rotation_tables(lengths_row, rows):
    token_ids = jnp.arange(rows, dtype=jnp.int32)
    ends = jnp.cumsum(lengths_row)
    past = (token_ids[:, None] >= ends[None, :]).astype(jnp.int32)
    positions = token_ids - jnp.sum(past * lengths_row[None, :], axis=1)
    angles = positions.astype(F32)[:, None] * frequencies(HD)[None, :]
    cosine, sine = jnp.cos(angles), jnp.sin(angles)
    return (
        jnp.concatenate([cosine] * 4, axis=1),
        jnp.concatenate([-sine, sine, -sine, sine], axis=1),
    )


def exchange_halves(tile):
    lane = lax.broadcasted_iota(jnp.int32, tile.shape, 1)
    return jnp.where(
        lane % HD < HD // 2,
        pltpu.roll(tile, LANES - HD // 2, 1),
        pltpu.roll(tile, HD // 2, 1),
    )


def block_place(meta_ref, j, devices):
    relative = meta_ref[0] ^ j
    return (relative & 1) * (devices // 2) + (relative >> 1)


def allowed_bias(meta_ref, docs, first, keys, queries):
    token = lax.broadcasted_iota(jnp.int32, (1, queries), 1) + first
    start = jnp.zeros((1, queries), jnp.int32)
    for j in range(docs - 1):
        start = jnp.where(token >= meta_ref[1 + j], meta_ref[1 + j], start)
    other = lax.broadcasted_iota(jnp.int32, (keys, queries), 0)
    return jnp.where((other <= token) & (other >= start), 0.0, NEGATIVE)


def last_dims(left, right):
    return lax.dot_general(left, right, (((1,), (1,)), ((), ())), preferred_element_type=F32)


def key_halves(qkv_ref, keep_keys, keep_values, keep_turned):
    tile = qkv_ref[:, 2 * LANES : 3 * LANES].astype(F32)
    lane = lax.broadcasted_iota(jnp.int32, tile.shape, 1)
    low = jnp.where(lane < HD, tile, 0.0)
    high = jnp.where(lane < HD, 0.0, tile)
    pairs = ((low, pltpu.roll(low, HD, 1)), (pltpu.roll(high, HD, 1), high))
    for half in range(2):
        if keep_keys is not None:
            keep_keys[half] = pairs[0][half].astype(BF16)
        if keep_values is not None:
            keep_values[half] = pairs[1][half].astype(BF16)
        if keep_turned is not None:
            source, ref = keep_turned
            ref[half] = pairs[source][half].T.astype(BF16)


def forward_kernel(docs, devices, meta_ref, joined_ref, cos_ref, sin_ref, attended_ref, qkv_ref, log_ref, keys_ref, turned_ref):
    rows = joined_ref.shape[0]
    block = rows // devices
    for j in range(devices):
        source = pl.multiple_of(block_place(meta_ref, j, devices) * block, block)
        here = slice(j * block, (j + 1) * block)
        cosine, sine = cos_ref[here, :], sin_ref[here, :]
        lane = lax.broadcasted_iota(jnp.int32, cosine.shape, 1)
        for t in range(3):
            tile = joined_ref[pl.ds(source, block), t * LANES : (t + 1) * LANES]
            turned = tile * cosine + exchange_halves(tile) * sine
            if t == 2:
                turned = jnp.where(lane < HD, turned, tile)
            qkv_ref[here, t * LANES : (t + 1) * LANES] = turned.astype(BF16)
    key_halves(qkv_ref, keys_ref, None, (1, turned_ref))
    for i in range(rows // QUERY_ROWS):
        keys = (i + 1) * QUERY_ROWS
        here = slice(i * QUERY_ROWS, keys)
        bias = allowed_bias(meta_ref, docs, i * QUERY_ROWS, keys, QUERY_ROWS)
        for t in range(2):
            query = qkv_ref[here, t * LANES : (t + 1) * LANES] * BF16(HD**-0.5)
            total = jnp.zeros((LANES, QUERY_ROWS), F32)
            for half in range(2):
                scores = last_dims(keys_ref[half, :keys, :], query) + bias
                peak = jnp.max(scores, axis=0, keepdims=True)
                raised = jnp.exp(scores - peak)
                mass = jnp.sum(raised, axis=0, keepdims=True)
                probs = (raised * (1.0 / mass)).astype(BF16)
                total = total + jnp.dot(
                    turned_ref[half, :, :keys], probs, preferred_element_type=F32
                )
                head = 2 * t + half
                log_ref[0, head : head + 1, here] = peak + jnp.log(mass)
            done = total.T.astype(BF16)
            step = min(block, QUERY_ROWS)
            for part in range(QUERY_ROWS // step):
                first = i * QUERY_ROWS + part * step
                place = block_place(meta_ref, first // block, devices) * block + first % block
                attended_ref[
                    pl.ds(pl.multiple_of(place, step), step), t * LANES : (t + 1) * LANES
                ] = done[part * step : (part + 1) * step, :]


def backward_kernel(docs, devices, meta_ref, qkv_ref, log_ref, back_ref, cos_ref, sin_ref, grad_ref, keys_ref, values_ref, turned_ref, key_total, value_total, query_total, back_here):
    rows = qkv_ref.shape[0]
    block = rows // devices
    key_halves(qkv_ref, keys_ref, values_ref, (0, turned_ref))
    for j in range(devices):
        source = pl.multiple_of(block_place(meta_ref, j, devices) * block, block)
        back_here[j * block : (j + 1) * block, :] = back_ref[pl.ds(source, block), :]
    key_total[...] = jnp.zeros_like(key_total)
    value_total[...] = jnp.zeros_like(value_total)
    for i in range(rows // QUERY_ROWS):
        keys = (i + 1) * QUERY_ROWS
        here = slice(i * QUERY_ROWS, keys)
        bias = allowed_bias(meta_ref, docs, i * QUERY_ROWS, keys, QUERY_ROWS)
        lane = lax.broadcasted_iota(jnp.int32, (QUERY_ROWS, LANES), 1)
        for t in range(2):
            columns = slice(t * LANES, (t + 1) * LANES)
            query = qkv_ref[here, columns] * BF16(HD**-0.5)
            back = back_here[here, columns]
            total = jnp.zeros((LANES, QUERY_ROWS), F32)
            for half in range(2):
                head = 2 * t + half
                mine = (lane < HD) if half == 0 else (lane >= HD)
                scores = last_dims(keys_ref[half, :keys, :], query) + bias
                probs = jnp.exp(scores - log_ref[0, head : head + 1, here])
                moved = last_dims(values_ref[half, :keys, :], back)
                inner = jnp.sum(probs * moved, axis=0, keepdims=True)
                grad = (probs * (moved - inner)).astype(BF16)
                total = total + jnp.dot(
                    turned_ref[half, :, :keys], grad, preferred_element_type=F32
                )
                key_total[:keys, :] += jnp.dot(
                    grad, jnp.where(mine, query, BF16(0)), preferred_element_type=F32
                )
                value_total[:keys, :] += jnp.dot(
                    probs.astype(BF16), jnp.where(mine, back, BF16(0)), preferred_element_type=F32
                )
            query_total[here, columns] = total.T * HD**-0.5
    for j in range(devices):
        place = pl.multiple_of(block_place(meta_ref, j, devices) * block, block)
        here = slice(j * block, (j + 1) * block)
        cosine, sine = cos_ref[here, :], sin_ref[here, :]
        lane = lax.broadcasted_iota(jnp.int32, cosine.shape, 1)
        for t in range(2):
            columns = slice(t * LANES, (t + 1) * LANES)
            tile = query_total[here, columns]
            grad_ref[pl.ds(place, block), columns] = (
                tile * cosine - exchange_halves(tile) * sine
            ).astype(BF16)
        tile = key_total[here, :]
        tile = tile + pltpu.roll(tile, HD, 1)
        other = value_total[here, :]
        other = other + pltpu.roll(other, HD, 1)
        tile = jnp.where(lane < HD, tile * cosine - exchange_halves(tile) * sine, other)
        grad_ref[pl.ds(place, block), 2 * LANES : 3 * LANES] = tile.astype(BF16)


def attend_forward(meta, joined, cosine, sine, docs, devices):
    rows, width = joined.shape
    wide = (GROUP + 2) * HD
    groups = width // wide
    whole = pl.BlockSpec((rows, LANES), lambda g: (0, 0))
    return pl.pallas_call(
        functools.partial(forward_kernel, docs, devices),
        grid=(groups,),
        in_specs=[
            pl.BlockSpec(memory_space=pltpu.SMEM),
            pl.BlockSpec((rows, wide), lambda g: (0, g)),
            whole,
            whole,
        ],
        out_specs=[
            pl.BlockSpec((rows, GROUP * HD), lambda g: (0, g)),
            pl.BlockSpec((rows, wide), lambda g: (0, g)),
            pl.BlockSpec((1, 8, rows), lambda g: (g, 0, 0)),
        ],
        out_shape=[
            jax.ShapeDtypeStruct((rows, groups * GROUP * HD), BF16),
            jax.ShapeDtypeStruct((rows, width), BF16),
            jax.ShapeDtypeStruct((groups, 8, rows), F32),
        ],
        scratch_shapes=[
            pltpu.VMEM((2, rows, LANES), BF16),
            pltpu.VMEM((2, LANES, rows), BF16),
        ],
        compiler_params=pltpu.CompilerParams(vmem_limit_bytes=32 * 2**20),
        cost_estimate=pl.CostEstimate(
            flops=groups * GROUP * rows * rows * LANES * 4,
            bytes_accessed=rows * width * 8,
            transcendentals=groups * GROUP * rows * rows // 2,
        ),
        name="attend_forward",
    )(meta, joined, cosine, sine)


def attend_backward(meta, qkv, logs, back, cosine, sine, docs, devices, group):
    rows = qkv.shape[0]
    wide = (GROUP + 2) * HD
    whole = pl.BlockSpec((rows, LANES), lambda g: (0, 0))
    return pl.pallas_call(
        functools.partial(backward_kernel, docs, devices),
        grid=(1,),
        in_specs=[
            pl.BlockSpec(memory_space=pltpu.SMEM),
            pl.BlockSpec((rows, wide), lambda g: (0, group)),
            pl.BlockSpec((1, 8, rows), lambda g: (group, 0, 0)),
            pl.BlockSpec((rows, GROUP * HD), lambda g: (0, group)),
            whole,
            whole,
        ],
        out_specs=pl.BlockSpec((rows, wide), lambda g: (0, 0)),
        out_shape=jax.ShapeDtypeStruct((rows, wide), BF16),
        scratch_shapes=[
            pltpu.VMEM((2, rows, LANES), BF16),
            pltpu.VMEM((2, rows, LANES), BF16),
            pltpu.VMEM((2, LANES, rows), BF16),
            pltpu.VMEM((rows, LANES), F32),
            pltpu.VMEM((rows, LANES), F32),
            pltpu.VMEM((rows, GROUP * HD), F32),
            pltpu.VMEM((rows, GROUP * HD), BF16),
        ],
        compiler_params=pltpu.CompilerParams(vmem_limit_bytes=32 * 2**20),
        cost_estimate=pl.CostEstimate(
            flops=GROUP * rows * rows * LANES * 10,
            bytes_accessed=rows * wide * 8,
            transcendentals=GROUP * rows * rows // 2,
        ),
        name="attend_backward",
    )(meta, qkv, logs, back, cosine, sine)


def product(left, right, left_dim, right_dim):
    return lax.dot_general(
        left, right, (((left_dim,), (right_dim,)), ((), ())), preferred_element_type=F32
    )


def norm_rate(vector):
    return lax.rsqrt(jnp.mean(vector * vector, axis=-1, keepdims=True) + EPSILON)


def norm_back(vector, rate, gain, grad):
    scaled = gain * grad
    inner = jnp.mean(vector * scaled, axis=-1, keepdims=True)
    return (
        rate * scaled - vector * (rate * rate * rate * inner),
        jnp.sum(grad * vector * rate, axis=0),
    )


def adam(weight, grad, moment, square, clip, rate, decay):
    clipped = clip * grad
    moment_new = BETA_ONE * moment + (1.0 - BETA_ONE) * clipped
    square_new = BETA_TWO * square + (1.0 - BETA_TWO) * clipped * clipped
    direction = (
        moment_new
        / (1.0 - BETA_ONE**STEP)
        / (jnp.sqrt(square_new / (1.0 - BETA_TWO**STEP)) + ADAM_EPSILON)
    )
    return (weight - rate * (direction + decay * weight), moment_new, square_new)


def adam_kernel(rate, decay, clip_ref, weight_ref, grad_ref, moment_ref, square_ref, *out_refs):
    done = adam(
        weight_ref[...],
        grad_ref[...].astype(F32),
        moment_ref[...],
        square_ref[...],
        clip_ref[0],
        rate,
        decay,
    )
    for ref, value in zip(out_refs, done):
        ref[...] = value


def update(weight, grad, moment, square, clip, rate, decay):
    shape = weight.shape
    rows, columns = math.prod(shape[:-1]), shape[-1]
    tall = rows // 2
    spec = pl.BlockSpec((tall, columns), lambda i: (i, 0))
    flat = [a.reshape(rows, columns) for a in (weight, grad, moment, square)]
    done = pl.pallas_call(
        functools.partial(adam_kernel, rate, decay),
        grid=(rows // tall,),
        in_specs=[pl.BlockSpec(memory_space=pltpu.SMEM)] + [spec] * 4,
        out_specs=[spec] * 3,
        out_shape=[jax.ShapeDtypeStruct((rows, columns), F32)] * 3,
        compiler_params=pltpu.CompilerParams(vmem_limit_bytes=60 * 2**20),
        cost_estimate=pl.CostEstimate(
            flops=rows * columns * 16, bytes_accessed=rows * columns * 26, transcendentals=rows * columns
        ),
        name="update",
    )(clip.reshape(1), *flat)
    return [a.reshape(shape) for a in done]


def adam_rows_kernel(rate, decay, side_ref, clip_ref, weight_ref, grad_ref, moment_ref, square_ref, *out_refs):
    heads, _, columns = weight_ref.shape
    halves = grad_ref.shape[1]
    unit = columns // (2 * UNITS)
    per_half = UNITS // halves
    for n in range(2 * UNITS):
        which, half, place = n // UNITS, n % UNITS // per_half, n % per_half
        cut = slice(n * unit, (n + 1) * unit)
        for j in range(heads):
            first = (heads * place + j) * unit
            done = adam(
                weight_ref[j, :, cut],
                grad_ref[which ^ side_ref[0], half, :, first : first + unit].astype(F32),
                moment_ref[j, :, cut],
                square_ref[j, :, cut],
                clip_ref[0],
                rate,
                decay,
            )
            for ref, value in zip(out_refs, done):
                ref[j, :, cut] = value


def adam_columns_kernel(rate, decay, side_ref, clip_ref, weight_ref, grad_ref, moment_ref, square_ref, *out_refs):
    done = adam(
        weight_ref[...],
        grad_ref[0, 0].astype(F32).T,
        moment_ref[...],
        square_ref[...],
        clip_ref[0],
        rate,
        decay,
    )
    for ref, value in zip(out_refs, done):
        ref[...] = value


def update_pieces(kernel, weight, pieces, moment, square, clip, side, block, at, piece_block, piece_at, rate, decay):
    spec = pl.BlockSpec(block, lambda i, s: at(i))
    grid_spec = pltpu.PrefetchScalarGridSpec(
        num_scalar_prefetch=1,
        grid=(weight.size // math.prod(block),),
        in_specs=[
            pl.BlockSpec(memory_space=pltpu.SMEM),
            spec,
            pl.BlockSpec(piece_block, lambda i, s: piece_at(i, s[0])),
            spec,
            spec,
        ],
        out_specs=[spec] * 3,
    )
    return pl.pallas_call(
        functools.partial(kernel, rate, decay),
        grid_spec=grid_spec,
        out_shape=[jax.ShapeDtypeStruct(weight.shape, F32)] * 3,
        compiler_params=pltpu.CompilerParams(vmem_limit_bytes=60 * 2**20),
        cost_estimate=pl.CostEstimate(
            flops=weight.size * 16, bytes_accessed=weight.size * 26, transcendentals=weight.size
        ),
        name="update_pieces",
    )(side.reshape(1).astype(jnp.int32), clip.reshape(1), weight, pieces, moment, square)


def split_kernel(side_ref, in_ref, out_ref, *unit_refs):
    unit = unit_refs[0].shape[1] // 3
    for n, ref in enumerate(unit_refs):
        cut = slice(n * unit, (n + 1) * unit)
        ref[:, :unit] = in_ref[0, :, cut].astype(BF16)
        ref[:, unit : 2 * unit] = in_ref[1, :, cut].astype(BF16)
        ref[:, 2 * unit :] = out_ref[cut, :].T.astype(BF16)


def split_feed(feed_in, feed_out, side, unit):
    depth, hidden = feed_in.shape[1], feed_in.shape[2] // 2
    part = jax.ShapeDtypeStruct((depth, 3 * unit), BF16)
    grid_spec = pltpu.PrefetchScalarGridSpec(
        num_scalar_prefetch=1,
        grid=(1,),
        in_specs=[
            pl.BlockSpec((2, depth, hidden), lambda i, s: (0, 0, s[0])),
            pl.BlockSpec((hidden, depth), lambda i, s: (s[0], 0)),
        ],
        out_specs=[pl.BlockSpec(part.shape, lambda i, s: (0, 0))] * (hidden // unit),
    )
    return pl.pallas_call(
        split_kernel,
        grid_spec=grid_spec,
        out_shape=[part] * (hidden // unit),
        compiler_params=pltpu.CompilerParams(vmem_limit_bytes=60 * 2**20),
        cost_estimate=pl.CostEstimate(
            flops=depth * hidden * 3, bytes_accessed=depth * hidden * 18, transcendentals=0
        ),
        name="split_feed",
    )(side.reshape(1).astype(jnp.int32), feed_in, feed_out)


def feed_kernel(rows_ref, back_ref, *refs):
    *weight_refs, activated_ref, grad_ref = refs
    for n, weight_ref in enumerate(weight_refs):
        unit = weight_ref.shape[1] // 3
        both = jnp.dot(rows_ref[...], weight_ref[:, : 2 * unit], preferred_element_type=F32)
        back = jnp.dot(back_ref[...], weight_ref[:, 2 * unit :], preferred_element_type=F32)
        gate, upward = both[:, :unit], both[:, unit:]
        chance = jax.nn.sigmoid(gate)
        silu = gate * chance
        activated_ref[:, n * unit : (n + 1) * unit] = (silu * upward).astype(BF16)
        grad_ref[:, 2 * n * unit : (2 * n + 1) * unit] = (
            back * upward * (chance + silu * (1.0 - chance))
        ).astype(BF16)
        grad_ref[:, (2 * n + 1) * unit : 2 * (n + 1) * unit] = (back * silu).astype(BF16)


def feed_both_ways(rows, back, weights):
    count, width = rows.shape
    slim = sum(w.shape[1] // 3 for w in weights)
    tall = min(count, 512)
    return pl.pallas_call(
        feed_kernel,
        grid=(count // tall,),
        in_specs=[
            pl.BlockSpec((tall, width), lambda i: (i, 0)),
            pl.BlockSpec((tall, width), lambda i: (i, 0)),
        ]
        + [pl.BlockSpec(w.shape, lambda i: (0, 0)) for w in weights],
        out_specs=[
            pl.BlockSpec((tall, slim), lambda i: (i, 0)),
            pl.BlockSpec((tall, 2 * slim), lambda i: (i, 0)),
        ],
        out_shape=[
            jax.ShapeDtypeStruct((count, slim), BF16),
            jax.ShapeDtypeStruct((count, 2 * slim), BF16),
        ],
        compiler_params=pltpu.CompilerParams(vmem_limit_bytes=48 * 2**20),
        cost_estimate=pl.CostEstimate(
            flops=6 * count * width * slim,
            bytes_accessed=4 * count * width + 6 * width * slim + 6 * count * slim,
            transcendentals=count * slim,
        ),
        name="feed_both_ways",
    )(rows, back, *weights)


def weights_kernel(scale, rows_ref, grad_ref, back_ref, activated_ref, out_ref):
    wide = grad_ref.shape[1]
    out_ref[0, :, :wide] = (product(rows_ref[...], grad_ref[...], 0, 0) * scale).astype(BF16)
    out_ref[0, :, wide:] = (product(back_ref[...], activated_ref[...], 0, 0) * scale).astype(BF16)


def weight_gradients(rows, grad, back, activated, parts, scale):
    count, width = rows.shape
    cut, slim = width // parts, activated.shape[1]
    return pl.pallas_call(
        functools.partial(weights_kernel, scale),
        grid=(parts,),
        in_specs=[
            pl.BlockSpec((count, cut), lambda i: (0, i)),
            pl.BlockSpec(grad.shape, lambda i: (0, 0)),
            pl.BlockSpec((count, cut), lambda i: (0, i)),
            pl.BlockSpec(activated.shape, lambda i: (0, 0)),
        ],
        out_specs=pl.BlockSpec((1, cut, 3 * slim), lambda i: (i, 0, 0)),
        out_shape=jax.ShapeDtypeStruct((parts, cut, 3 * slim), BF16),
        compiler_params=pltpu.CompilerParams(vmem_limit_bytes=48 * 2**20),
        cost_estimate=pl.CostEstimate(
            flops=6 * count * width * slim,
            bytes_accessed=4 * count * width + 6 * count * slim + 6 * width * slim,
            transcendentals=0,
        ),
        name="weight_gradients",
    )(rows, grad, back, activated)


def back_kernel(first, last, counts, *refs):
    total, refs = 0.0, list(refs)
    for count in counts:
        left = refs.pop(0)
        for n in range(count):
            right = refs.pop(0)
            unit = right.shape[1] // 3
            wide = (last - first) * unit
            total = total + product(
                left[:, n * wide : (n + 1) * wide],
                right[:, first * unit : last * unit],
                1,
                1,
            )
    refs[0][...] = total.astype(BF16)


def back_products(pairs, first, last, half):
    count, width = pairs[0][0].shape[0] // 2, pairs[0][1][0].shape[0]
    tall = min(count, 512)
    skip = half * (count // tall)
    specs, operands = [], []
    for left, right in pairs:
        specs.append(pl.BlockSpec((tall, left.shape[1]), lambda i: (i + skip, 0)))
        specs += [pl.BlockSpec(w.shape, lambda i: (0, 0)) for w in right]
        operands += [left, *right]
    depth = sum(left.shape[1] for left, _ in pairs)
    return pl.pallas_call(
        functools.partial(back_kernel, first, last, [len(right) for _, right in pairs]),
        grid=(count // tall,),
        in_specs=specs,
        out_specs=pl.BlockSpec((tall, width), lambda i: (i, 0)),
        out_shape=jax.ShapeDtypeStruct((count, width), BF16),
        compiler_params=pltpu.CompilerParams(vmem_limit_bytes=56 * 2**20),
        cost_estimate=pl.CostEstimate(
            flops=2 * count * width * depth,
            bytes_accessed=2 * count * (width + depth) + 2 * width * depth,
            transcendentals=0,
        ),
        name="back_products",
    )(*operands)


def in_order(mine, other, first, axis):
    return jnp.where(
        first,
        jnp.concatenate([mine, other], axis=axis),
        jnp.concatenate([other, mine], axis=axis),
    )


def shards(
    sizes,
    tensor,
    tokens,
    cotangent,
    doc_lengths,
    attend_in,
    attend_out,
    feed_in,
    feed_out,
    norm_gains,
    moment_attend_in,
    square_attend_in,
    moment_attend_out,
    square_attend_out,
    moment_feed_in,
    square_feed_in,
    moment_feed_out,
    square_feed_out,
    moment_gains,
    square_gains,
):
    pack_links, core = tensor[:-1], tensor[-1]
    feed_links = ("x",) + tuple(pack_links)
    devices = math.prod(sizes[a] for a in tensor)
    side = lax.axis_index("x")
    is_first = side == 0
    local_rows, width = tokens.shape
    rows = local_rows * devices
    token_total = rows * 2 * sizes["z"]
    inverse_total = 1.0 / token_total
    docs = doc_lengths.shape[1]
    meta = jnp.concatenate(
        [lax.axis_index(tuple(tensor))[None].astype(jnp.int32), jnp.cumsum(doc_lengths[0])]
    )
    cosine, sine = rotation_tables(doc_lengths[0], rows)

    hidden = feed_in.shape[2] // 2
    slim = hidden // 2
    unit = hidden // UNITS
    depth = attend_in.shape[0]
    half = rows // 2

    def halves(array, axis):
        size = array.shape[axis] // 2
        mine = lax.dynamic_slice_in_dim(array, side * size, size, axis)
        other = lax.dynamic_slice_in_dim(array, (1 - side) * size, size, axis)
        return mine, other

    def sends(block, links):
        return [flip(block, c, sizes) for c in combos(links)[1:]]

    def over_core(blocks):
        mine = jnp.concatenate(blocks, axis=0)
        return jnp.concatenate([mine, flip(mine, (core,), sizes)], axis=0)

    def both_sides(mine, other):
        pair = jnp.where(
            is_first, jnp.stack([mine, other], axis=1), jnp.stack([other, mine], axis=1)
        )
        return pair

    gain_rows = jnp.pad(
        norm_gains.astype(BF16), ((0, 14), (0, attend_in.shape[1] - norm_gains.shape[1]))
    )
    in_z = lax.all_gather(
        jnp.concatenate([attend_in.astype(BF16), gain_rows], axis=0), "z", axis=0, tiled=False
    )
    out_z = lax.all_gather(attend_out.T.astype(BF16), "z", axis=0, tiled=False)
    tokens_moved = sends(tokens, pack_links)
    away = split_feed(feed_in, feed_out, 1 - side, unit)
    moved = [flip(part, ("x",), sizes) for part in away]
    kept = split_feed(feed_in, feed_out, side, unit)
    (in_z, cotangent_then), tokens_moved, moved = lax.optimization_barrier(
        ((in_z, cotangent), tokens_moved, moved)
    )

    locals_ = [in_order(part, other, is_first, 0) for part, other in zip(kept, moved)]
    weights = [lax.all_gather(part, "z", axis=0, tiled=True) for part in locals_[:3]]
    weights.append(gather_depth(locals_[3], sizes).reshape(width, -1))
    in_x = flip(in_z, ("x",), sizes)
    back_moved = sends(cotangent_then, pack_links)
    tokens_all = over_core([tokens] + tokens_moved)
    in_x, out_z, back_moved, tokens_all = lax.optimization_barrier(
        (in_x, out_z, back_moved, tokens_all)
    )

    out_x = flip(out_z, ("x",), sizes)
    in_both = both_sides(in_z, in_x)
    full_in = in_both[:, :, :depth].reshape(width, attend_in.shape[1])
    gains = (
        in_both[:, :, depth : depth + 2, : norm_gains.shape[1]]
        .astype(F32)
        .transpose(2, 0, 1, 3)
        .reshape(2, width)
    )
    inputs_all = tokens_all.astype(F32)
    normed_one = (inputs_all * norm_rate(inputs_all) * gains[0]).astype(BF16)
    joined = product(normed_one, full_in, 1, 0)
    attended, qkv, logs = attend_forward(meta, joined, cosine, sine, docs, devices)
    back_near = jnp.concatenate([cotangent] + back_moved, axis=0)
    attended, out_x, left, right = lax.optimization_barrier(
        (attended, out_x, back_near[:, : width // 2], back_near[:, width // 2 :])
    )

    full_out = both_sides(out_z, out_x).reshape(width, attend_out.shape[0])
    near = product(attended[half:], full_out, 1, 1).astype(BF16)
    mine = product(attended[:half], full_out, 1, 1).astype(BF16)
    own, moved = collect(mine, near, pack_links, core, sizes)
    left = flip(left, ("x",), sizes)
    own, moved, left, right = lax.optimization_barrier((own, moved, left, right))

    inputs = tokens.astype(F32)
    hidden_state = inputs + added(own, moved)
    rate_two = norm_rate(hidden_state)
    normed_two = (hidden_state * rate_two * gains[1]).astype(BF16)
    normed_moved = sends(normed_two, feed_links)
    right = flip(right, ("x",), sizes)
    normed_moved, left, right = lax.optimization_barrier((normed_moved, left, right))
    gathered_two = over_core([normed_two] + normed_moved)
    gathered_back = over_core([back_near, jnp.concatenate([left, right], axis=1)])

    def gradients(grad, activated):
        return weight_gradients(
            gathered_two, grad, gathered_back, activated, sizes["z"], inverse_total
        )

    def summed(parts):
        return lax.psum_scatter(parts, "z", scatter_dimension=0, tiled=False)

    activated_a, grad_a = feed_both_ways(gathered_two, gathered_back, weights[:2])
    activated_a, grad_a, weights[2] = lax.optimization_barrier((activated_a, grad_a, weights[2]))
    parts_a = gradients(grad_a, activated_a)
    parts_a, weights[3] = lax.optimization_barrier((parts_a, weights[3]))
    sums_a = summed(parts_a)
    activated_b, grad_b = feed_both_ways(gathered_two, gathered_back, weights[2:])
    pairs = [(grad_a, weights[:2]), (grad_b, weights[2:])]
    near = flip(back_products(pairs, 0, 2, 1), (core,), sizes)
    mine = back_products(pairs, 0, 2, 0)
    blocks = add_blocks(mine, near, 2 ** len(feed_links))
    blocks, grad_b, activated_a, activated_b = lax.optimization_barrier(
        (blocks, grad_b, activated_a, activated_b)
    )
    moved = [flip(block, c, sizes) for block, c in zip(blocks[1:], combos(feed_links)[1:])]
    parts_b = gradients(grad_b, activated_b)
    sums_b = summed(parts_b)
    pairs = [(activated_a, weights[:2]), (activated_b, weights[2:])]
    forward_near = back_products(pairs, 2, 3, 1)
    forward_mine = back_products(pairs, 2, 3, 0)
    moved, forward_near, forward_mine, parts_b = lax.optimization_barrier(
        (moved, forward_near, forward_mine, parts_b)
    )

    grad_from_two, gain_two_grad = norm_back(
        hidden_state, rate_two, gains[1], added(blocks[0], moved)
    )
    grad_hidden = cotangent.astype(F32) + grad_from_two
    grad_branch = grad_hidden.astype(BF16)
    grad_moved = sends(grad_branch, pack_links)
    forward_blocks = add_blocks(
        forward_mine, flip(forward_near, (core,), sizes), 2 ** len(feed_links)
    )
    grad_moved, forward_blocks = lax.optimization_barrier((grad_moved, forward_blocks))
    gathered_grad = over_core([grad_branch] + grad_moved)
    grad_attended = product(gathered_grad, full_out, 1, 0).astype(BF16)
    forward_moved = [
        flip(block, c, sizes) for block, c in zip(forward_blocks[1:], combos(feed_links)[1:])
    ]
    groups = attend_in.shape[1] // ((GROUP + 2) * HD)
    grad_joined = [
        attend_backward(meta, qkv, logs, grad_attended, cosine, sine, docs, devices, group)
        for group in range(groups)
    ]

    def split_sides(grad):
        split = (grad * inverse_total).astype(BF16).reshape(sizes["z"], 2, -1, grad.shape[1])
        mine = lax.dynamic_index_in_dim(split, side, 1, keepdims=False)
        other = lax.dynamic_index_in_dim(split, 1 - side, 1, keepdims=False)
        return mine, flip(other, ("x",), sizes)

    out_mine, out_other = split_sides(product(gathered_grad, attended, 0, 0))
    grad_joined[-1], forward_moved, out_other = lax.optimization_barrier(
        (grad_joined[-1], forward_moved, out_other)
    )
    block_out = (hidden_state + added(forward_blocks[0], forward_moved)).astype(BF16)
    attend_out_shard = sum_depth(added(out_mine, [out_other]).astype(BF16)).T
    in_parts = [
        added(mine, [other]).astype(BF16)
        for mine, other in (split_sides(product(normed_one, grad, 0, 0)) for grad in grad_joined)
    ]
    attend_in_shard = sum_depth(jnp.concatenate(in_parts, axis=2))
    joined_back = jnp.concatenate(grad_joined, axis=1)
    own, moved = collect(
        product(joined_back[:half], full_in, 1, 1).astype(BF16),
        product(joined_back[half:], full_in, 1, 1).astype(BF16),
        pack_links,
        core,
        sizes,
    )
    grad_normed_one = added(own, moved)
    grad_from_one, gain_one_grad = norm_back(inputs, norm_rate(inputs), gains[0], grad_normed_one)
    tokens_grad = (grad_hidden + grad_from_one).astype(BF16)

    def regroup(sums):
        mine, other = halves(sums, 0)
        return jnp.stack([mine, flip(other, ("x",), sizes)])

    pieces = jnp.stack([regroup(sums_a), regroup(sums_b)], axis=1)

    def squares(shard):
        shard = shard.astype(F32)
        return jnp.sum(shard * shard)

    matrix_squares = (
        squares(attend_in_shard)
        + squares(attend_out_shard)
        + squares(pieces)
    )
    total = sum_everywhere(
        jnp.concatenate(
            [
                gain_one_grad * inverse_total,
                gain_two_grad * inverse_total,
                jnp.full((LANES,), matrix_squares),
            ]
        ),
        tensor,
        sizes,
    )
    gain_grads = total[: 2 * width].reshape(2, width)
    grad_norm = jnp.sqrt(total[2 * width] + jnp.sum(gain_grads * gain_grads))
    clip = jnp.minimum(1.0, CLIP_LIMIT / (grad_norm + 1e-06))
    gain_width = norm_gains.shape[1]
    gain_shard = lax.dynamic_slice_in_dim(
        gain_grads, lax.axis_index(("z", "x")) * gain_width, gain_width, 1
    )
    first = update(attend_in, attend_in_shard, moment_attend_in, square_attend_in, clip, MATRIX_RATE, MATRIX_DECAY)
    second = update(attend_out, attend_out_shard, moment_attend_out, square_attend_out, clip, OUTPUT_RATE, MATRIX_DECAY)
    tall = depth // 2
    third = update_pieces(
        adam_rows_kernel, feed_in, pieces, moment_feed_in, square_feed_in, clip, side,
        (2, tall, feed_in.shape[2]), lambda i: (0, i, 0),
        (2, 2, tall, 2 * slim), lambda i, s: (0, 0, i, 0),
        MATRIX_RATE, MATRIX_DECAY,
    )
    fourth = update_pieces(
        adam_columns_kernel, feed_out, pieces, moment_feed_out, square_feed_out, clip, side,
        (slim, depth), lambda i: (i, 0),
        (1, 1, depth, slim), lambda i, s: ((i // 2) ^ s, i % 2, 0, 2),
        MATRIX_RATE, MATRIX_DECAY,
    )
    fifth = adam(norm_gains, gain_shard, moment_gains, square_gains, clip, GAIN_RATE, 0.0)
    return (block_out, tokens_grad, grad_norm, *first, *second, *third, *fourth, *fifth)


def solution(mesh):
    depth, across = mesh.shape["dp"], mesh.shape["tensor"]
    tensor = tuple("t" + str(i) for i in range(across.bit_length() - 1))
    sizes = {"z": depth // 2, "x": 2, **{a: 2 for a in tensor}}
    assert depth % 2 == 0 and 2 ** len(tensor) == across
    fine = Mesh(mesh.devices.reshape(tuple(sizes.values())), tuple(sizes))
    dp = ("z", "x")
    both = P(dp + tensor, None)
    rows_cut, columns_cut = P(dp, tensor), P(tensor, dp)
    feed_cut, gain_cut = P(None, dp, tensor), P(None, dp)
    state = (rows_cut,) * 3 + (columns_cut,) * 3 + (feed_cut,) * 3 + (columns_cut,) * 3 + (gain_cut,) * 3
    return jax.shard_map(
        functools.partial(shards, sizes, tensor),
        mesh=fine,
        in_specs=(both, both, P(dp, None), rows_cut, columns_cut, feed_cut, columns_cut, gain_cut)
        + (rows_cut,) * 2
        + (columns_cut,) * 2
        + (feed_cut,) * 2
        + (columns_cut,) * 2
        + (gain_cut,) * 2,
        out_specs=(both, both, P()) + state,
        check_vma=False,
    )
```

```python
import functools
import math

import jax
import jax.numpy as jnp
from jax import lax
from jax.experimental import pallas as pl
from jax.experimental.pallas import tpu as pltpu
from jax.sharding import Mesh
from jax.sharding import PartitionSpec as P

H = 32
KV = 8
HD = 64
GROUP = H // KV
STEP = 10
LANES = 128
QUERY_ROWS = 256
UNITS = 4

EPSILON = 1e-05
NEGATIVE = -1e30
CLIP_LIMIT = 0.25
BETA_ONE = 0.9
BETA_TWO = 0.95
ADAM_EPSILON = 1e-08
MATRIX_RATE = 0.04
OUTPUT_RATE = 0.3
MATRIX_DECAY = 0.1
GAIN_RATE = 0.6

BF16 = jnp.bfloat16
F32 = jnp.float32


def flip(value, axes, sizes):
    count = math.prod(sizes[a] for a in axes)
    pairs = [(i, i ^ (count - 1)) for i in range(count)]
    return lax.ppermute(value, tuple(axes), pairs)


def combos(axes):
    return [
        tuple(a for i, a in enumerate(axes) if place >> (len(axes) - 1 - i) & 1)
        for place in range(2 ** len(axes))
    ]


def add_kernel(mine_ref, near_ref, *out_refs):
    for k, ref in enumerate(out_refs):

        @pl.when(pl.program_id(0) == k)
        def _():
            ref[...] = (mine_ref[...].astype(F32) + near_ref[...].astype(F32)).astype(BF16)


def add_blocks(mine, near, count):
    rows, width = mine.shape[0] // count, mine.shape[1]
    cut = pl.BlockSpec((rows, width), lambda i: (i, 0))
    return pl.pallas_call(
        add_kernel,
        grid=(count,),
        in_specs=[cut, cut],
        out_specs=[pl.BlockSpec((rows, width), lambda i: (0, 0))] * count,
        out_shape=[jax.ShapeDtypeStruct((rows, width), BF16)] * count,
        compiler_params=pltpu.CompilerParams(vmem_limit_bytes=32 * 2**20),
        cost_estimate=pl.CostEstimate(
            flops=mine.size, bytes_accessed=6 * mine.size, transcendentals=0
        ),
        name="add_blocks",
    )(mine, near)


def collect(mine, near, links, core, sizes):
    places = combos(links)
    blocks = add_blocks(mine, flip(near, (core,), sizes), len(places))
    return blocks[0], [flip(block, c, sizes) for block, c in zip(blocks[1:], places[1:])]


def added(own, moved):
    return sum((block.astype(F32) for block in moved), own.astype(F32))


def gather_depth(block, sizes):
    copies = jnp.broadcast_to(block, (sizes["z"],) + block.shape)
    return lax.all_to_all(copies, "z", 0, 0, tiled=True)


def sum_depth(blocks):
    arrived = lax.all_to_all(blocks, "z", 0, 0, tiled=True)
    return jnp.sum(arrived.astype(F32), axis=0).astype(BF16)


def sum_everywhere(value, tensor, sizes):
    for a in tuple(reversed(tensor)) + ("x",):
        value = value + flip(value, (a,), sizes)
    step, count = 1, sizes["z"]
    while step < count:
        value = value + lax.ppermute(value, "z", [(i, i ^ step) for i in range(count)])
        step *= 2
    return value


def frequencies(head_size):
    half_index = jnp.arange(head_size // 2, dtype=F32)
    inverse = jnp.power(500000.0, -2.0 * half_index / head_size)
    wavelength = 2.0 * math.pi / inverse
    smooth = (8192.0 / wavelength - 1.0) / 3.0
    blended = (1.0 - smooth) * inverse / 32.0 + smooth * inverse
    return jnp.where(
        wavelength < 2048.0, inverse, jnp.where(wavelength > 8192.0, inverse / 32.0, blended)
    )


def rotation_tables(lengths_row, rows):
    token_ids = jnp.arange(rows, dtype=jnp.int32)
    ends = jnp.cumsum(lengths_row)
    past = (token_ids[:, None] >= ends[None, :]).astype(jnp.int32)
    positions = token_ids - jnp.sum(past * lengths_row[None, :], axis=1)
    angles = positions.astype(F32)[:, None] * frequencies(HD)[None, :]
    cosine, sine = jnp.cos(angles), jnp.sin(angles)
    return (
        jnp.concatenate([cosine] * 4, axis=1),
        jnp.concatenate([-sine, sine, -sine, sine], axis=1),
    )


def exchange_halves(tile):
    lane = lax.broadcasted_iota(jnp.int32, tile.shape, 1)
    return jnp.where(
        lane % HD < HD // 2,
        pltpu.roll(tile, LANES - HD // 2, 1),
        pltpu.roll(tile, HD // 2, 1),
    )


def block_place(meta_ref, j, devices):
    relative = meta_ref[0] ^ j
    return (relative & 1) * (devices // 2) + (relative >> 1)


def allowed_bias(meta_ref, docs, first, keys, queries):
    token = lax.broadcasted_iota(jnp.int32, (1, queries), 1) + first
    start = jnp.zeros((1, queries), jnp.int32)
    for j in range(docs - 1):
        start = jnp.where(token >= meta_ref[1 + j], meta_ref[1 + j], start)
    other = lax.broadcasted_iota(jnp.int32, (keys, queries), 0)
    return jnp.where((other <= token) & (other >= start), 0.0, NEGATIVE)


def last_dims(left, right):
    return lax.dot_general(left, right, (((1,), (1,)), ((), ())), preferred_element_type=F32)


def key_halves(qkv_ref, keep_keys, keep_values, keep_turned):
    tile = qkv_ref[:, 2 * LANES : 3 * LANES].astype(F32)
    lane = lax.broadcasted_iota(jnp.int32, tile.shape, 1)
    low = jnp.where(lane < HD, tile, 0.0)
    high = jnp.where(lane < HD, 0.0, tile)
    pairs = ((low, pltpu.roll(low, HD, 1)), (pltpu.roll(high, HD, 1), high))
    for half in range(2):
        if keep_keys is not None:
            keep_keys[half] = pairs[0][half].astype(BF16)
        if keep_values is not None:
            keep_values[half] = pairs[1][half].astype(BF16)
        if keep_turned is not None:
            source, ref = keep_turned
            ref[half] = pairs[source][half].T.astype(BF16)


def forward_kernel(docs, devices, meta_ref, joined_ref, cos_ref, sin_ref, attended_ref, qkv_ref, log_ref, keys_ref, turned_ref):
    rows = joined_ref.shape[0]
    block = rows // devices
    for j in range(devices):
        source = pl.multiple_of(block_place(meta_ref, j, devices) * block, block)
        here = slice(j * block, (j + 1) * block)
        cosine, sine = cos_ref[here, :], sin_ref[here, :]
        lane = lax.broadcasted_iota(jnp.int32, cosine.shape, 1)
        for t in range(3):
            tile = joined_ref[pl.ds(source, block), t * LANES : (t + 1) * LANES]
            turned = tile * cosine + exchange_halves(tile) * sine
            if t == 2:
                turned = jnp.where(lane < HD, turned, tile)
            qkv_ref[here, t * LANES : (t + 1) * LANES] = turned.astype(BF16)
    key_halves(qkv_ref, keys_ref, None, (1, turned_ref))
    for i in range(rows // QUERY_ROWS):
        keys = (i + 1) * QUERY_ROWS
        here = slice(i * QUERY_ROWS, keys)
        bias = allowed_bias(meta_ref, docs, i * QUERY_ROWS, keys, QUERY_ROWS)
        for t in range(2):
            query = qkv_ref[here, t * LANES : (t + 1) * LANES] * BF16(HD**-0.5)
            total = jnp.zeros((LANES, QUERY_ROWS), F32)
            for half in range(2):
                scores = last_dims(keys_ref[half, :keys, :], query) + bias
                peak = jnp.max(scores, axis=0, keepdims=True)
                raised = jnp.exp(scores - peak)
                mass = jnp.sum(raised, axis=0, keepdims=True)
                probs = (raised * (1.0 / mass)).astype(BF16)
                total = total + jnp.dot(
                    turned_ref[half, :, :keys], probs, preferred_element_type=F32
                )
                head = 2 * t + half
                log_ref[0, head : head + 1, here] = peak + jnp.log(mass)
            done = total.T.astype(BF16)
            step = min(block, QUERY_ROWS)
            for part in range(QUERY_ROWS // step):
                first = i * QUERY_ROWS + part * step
                place = block_place(meta_ref, first // block, devices) * block + first % block
                attended_ref[
                    pl.ds(pl.multiple_of(place, step), step), t * LANES : (t + 1) * LANES
                ] = done[part * step : (part + 1) * step, :]


def backward_kernel(docs, devices, meta_ref, qkv_ref, log_ref, back_ref, cos_ref, sin_ref, grad_ref, keys_ref, values_ref, turned_ref, key_total, value_total, query_total, back_here):
    rows = qkv_ref.shape[0]
    block = rows // devices
    key_halves(qkv_ref, keys_ref, values_ref, (0, turned_ref))
    for j in range(devices):
        source = pl.multiple_of(block_place(meta_ref, j, devices) * block, block)
        back_here[j * block : (j + 1) * block, :] = back_ref[pl.ds(source, block), :]
    key_total[...] = jnp.zeros_like(key_total)
    value_total[...] = jnp.zeros_like(value_total)
    for i in range(rows // QUERY_ROWS):
        keys = (i + 1) * QUERY_ROWS
        here = slice(i * QUERY_ROWS, keys)
        bias = allowed_bias(meta_ref, docs, i * QUERY_ROWS, keys, QUERY_ROWS)
        lane = lax.broadcasted_iota(jnp.int32, (QUERY_ROWS, LANES), 1)
        for t in range(2):
            columns = slice(t * LANES, (t + 1) * LANES)
            query = qkv_ref[here, columns] * BF16(HD**-0.5)
            back = back_here[here, columns]
            total = jnp.zeros((LANES, QUERY_ROWS), F32)
            for half in range(2):
                head = 2 * t + half
                mine = (lane < HD) if half == 0 else (lane >= HD)
                scores = last_dims(keys_ref[half, :keys, :], query) + bias
                probs = jnp.exp(scores - log_ref[0, head : head + 1, here])
                moved = last_dims(values_ref[half, :keys, :], back)
                inner = jnp.sum(probs * moved, axis=0, keepdims=True)
                grad = (probs * (moved - inner)).astype(BF16)
                total = total + jnp.dot(
                    turned_ref[half, :, :keys], grad, preferred_element_type=F32
                )
                key_total[:keys, :] += jnp.dot(
                    grad, jnp.where(mine, query, BF16(0)), preferred_element_type=F32
                )
                value_total[:keys, :] += jnp.dot(
                    probs.astype(BF16), jnp.where(mine, back, BF16(0)), preferred_element_type=F32
                )
            query_total[here, columns] = total.T * HD**-0.5
    for j in range(devices):
        place = pl.multiple_of(block_place(meta_ref, j, devices) * block, block)
        here = slice(j * block, (j + 1) * block)
        cosine, sine = cos_ref[here, :], sin_ref[here, :]
        lane = lax.broadcasted_iota(jnp.int32, cosine.shape, 1)
        for t in range(2):
            columns = slice(t * LANES, (t + 1) * LANES)
            tile = query_total[here, columns]
            grad_ref[pl.ds(place, block), columns] = (
                tile * cosine - exchange_halves(tile) * sine
            ).astype(BF16)
        tile = key_total[here, :]
        tile = tile + pltpu.roll(tile, HD, 1)
        other = value_total[here, :]
        other = other + pltpu.roll(other, HD, 1)
        tile = jnp.where(lane < HD, tile * cosine - exchange_halves(tile) * sine, other)
        grad_ref[pl.ds(place, block), 2 * LANES : 3 * LANES] = tile.astype(BF16)


def attend_forward(meta, joined, cosine, sine, docs, devices):
    rows, width = joined.shape
    wide = (GROUP + 2) * HD
    groups = width // wide
    whole = pl.BlockSpec((rows, LANES), lambda g: (0, 0))
    return pl.pallas_call(
        functools.partial(forward_kernel, docs, devices),
        grid=(groups,),
        in_specs=[
            pl.BlockSpec(memory_space=pltpu.SMEM),
            pl.BlockSpec((rows, wide), lambda g: (0, g)),
            whole,
            whole,
        ],
        out_specs=[
            pl.BlockSpec((rows, GROUP * HD), lambda g: (0, g)),
            pl.BlockSpec((rows, wide), lambda g: (0, g)),
            pl.BlockSpec((1, 8, rows), lambda g: (g, 0, 0)),
        ],
        out_shape=[
            jax.ShapeDtypeStruct((rows, groups * GROUP * HD), BF16),
            jax.ShapeDtypeStruct((rows, width), BF16),
            jax.ShapeDtypeStruct((groups, 8, rows), F32),
        ],
        scratch_shapes=[
            pltpu.VMEM((2, rows, LANES), BF16),
            pltpu.VMEM((2, LANES, rows), BF16),
        ],
        compiler_params=pltpu.CompilerParams(vmem_limit_bytes=32 * 2**20),
        cost_estimate=pl.CostEstimate(
            flops=groups * GROUP * rows * rows * LANES * 4,
            bytes_accessed=rows * width * 8,
            transcendentals=groups * GROUP * rows * rows // 2,
        ),
        name="attend_forward",
    )(meta, joined, cosine, sine)


def attend_backward(meta, qkv, logs, back, cosine, sine, docs, devices, group):
    rows = qkv.shape[0]
    wide = (GROUP + 2) * HD
    whole = pl.BlockSpec((rows, LANES), lambda g: (0, 0))
    return pl.pallas_call(
        functools.partial(backward_kernel, docs, devices),
        grid=(1,),
        in_specs=[
            pl.BlockSpec(memory_space=pltpu.SMEM),
            pl.BlockSpec((rows, wide), lambda g: (0, group)),
            pl.BlockSpec((1, 8, rows), lambda g: (group, 0, 0)),
            pl.BlockSpec((rows, GROUP * HD), lambda g: (0, group)),
            whole,
            whole,
        ],
        out_specs=pl.BlockSpec((rows, wide), lambda g: (0, 0)),
        out_shape=jax.ShapeDtypeStruct((rows, wide), BF16),
        scratch_shapes=[
            pltpu.VMEM((2, rows, LANES), BF16),
            pltpu.VMEM((2, rows, LANES), BF16),
            pltpu.VMEM((2, LANES, rows), BF16),
            pltpu.VMEM((rows, LANES), F32),
            pltpu.VMEM((rows, LANES), F32),
            pltpu.VMEM((rows, GROUP * HD), F32),
            pltpu.VMEM((rows, GROUP * HD), BF16),
        ],
        compiler_params=pltpu.CompilerParams(vmem_limit_bytes=32 * 2**20),
        cost_estimate=pl.CostEstimate(
            flops=GROUP * rows * rows * LANES * 10,
            bytes_accessed=rows * wide * 8,
            transcendentals=GROUP * rows * rows // 2,
        ),
        name="attend_backward",
    )(meta, qkv, logs, back, cosine, sine)


def product(left, right, left_dim, right_dim):
    return lax.dot_general(
        left, right, (((left_dim,), (right_dim,)), ((), ())), preferred_element_type=F32
    )


def norm_rate(vector):
    return lax.rsqrt(jnp.mean(vector * vector, axis=-1, keepdims=True) + EPSILON)


def norm_back(vector, rate, gain, grad):
    scaled = gain * grad
    inner = jnp.mean(vector * scaled, axis=-1, keepdims=True)
    return (
        rate * scaled - vector * (rate * rate * rate * inner),
        jnp.sum(grad * vector * rate, axis=0),
    )


def adam(weight, grad, moment, square, clip, rate, decay):
    clipped = clip * grad
    moment_new = BETA_ONE * moment + (1.0 - BETA_ONE) * clipped
    square_new = BETA_TWO * square + (1.0 - BETA_TWO) * clipped * clipped
    direction = (
        moment_new
        / (1.0 - BETA_ONE**STEP)
        / (jnp.sqrt(square_new / (1.0 - BETA_TWO**STEP)) + ADAM_EPSILON)
    )
    return (weight - rate * (direction + decay * weight), moment_new, square_new)


def adam_kernel(rate, decay, clip_ref, weight_ref, grad_ref, moment_ref, square_ref, *out_refs):
    done = adam(
        weight_ref[...],
        grad_ref[...].astype(F32),
        moment_ref[...],
        square_ref[...],
        clip_ref[0],
        rate,
        decay,
    )
    for ref, value in zip(out_refs, done):
        ref[...] = value


def update(weight, grad, moment, square, clip, rate, decay):
    shape = weight.shape
    rows, columns = math.prod(shape[:-1]), shape[-1]
    tall = rows // 2
    spec = pl.BlockSpec((tall, columns), lambda i: (i, 0))
    flat = [a.reshape(rows, columns) for a in (weight, grad, moment, square)]
    done = pl.pallas_call(
        functools.partial(adam_kernel, rate, decay),
        grid=(rows // tall,),
        in_specs=[pl.BlockSpec(memory_space=pltpu.SMEM)] + [spec] * 4,
        out_specs=[spec] * 3,
        out_shape=[jax.ShapeDtypeStruct((rows, columns), F32)] * 3,
        compiler_params=pltpu.CompilerParams(vmem_limit_bytes=60 * 2**20),
        cost_estimate=pl.CostEstimate(
            flops=rows * columns * 16, bytes_accessed=rows * columns * 26, transcendentals=rows * columns
        ),
        name="update",
    )(clip.reshape(1), *flat)
    return [a.reshape(shape) for a in done]


def adam_rows_kernel(rate, decay, side_ref, clip_ref, weight_ref, grad_ref, moment_ref, square_ref, *out_refs):
    heads, _, columns = weight_ref.shape
    halves = grad_ref.shape[1]
    unit = columns // (2 * UNITS)
    per_half = UNITS // halves
    for n in range(2 * UNITS):
        which, half, place = n // UNITS, n % UNITS // per_half, n % per_half
        cut = slice(n * unit, (n + 1) * unit)
        for j in range(heads):
            first = (heads * place + j) * unit
            done = adam(
                weight_ref[j, :, cut],
                grad_ref[which ^ side_ref[0], half, :, first : first + unit].astype(F32),
                moment_ref[j, :, cut],
                square_ref[j, :, cut],
                clip_ref[0],
                rate,
                decay,
            )
            for ref, value in zip(out_refs, done):
                ref[j, :, cut] = value


def adam_columns_kernel(rate, decay, side_ref, clip_ref, weight_ref, grad_ref, moment_ref, square_ref, *out_refs):
    done = adam(
        weight_ref[...],
        grad_ref[0, 0].astype(F32).T,
        moment_ref[...],
        square_ref[...],
        clip_ref[0],
        rate,
        decay,
    )
    for ref, value in zip(out_refs, done):
        ref[...] = value


def update_pieces(kernel, weight, pieces, moment, square, clip, side, block, at, piece_block, piece_at, rate, decay):
    spec = pl.BlockSpec(block, lambda i, s: at(i))
    grid_spec = pltpu.PrefetchScalarGridSpec(
        num_scalar_prefetch=1,
        grid=(weight.size // math.prod(block),),
        in_specs=[
            pl.BlockSpec(memory_space=pltpu.SMEM),
            spec,
            pl.BlockSpec(piece_block, lambda i, s: piece_at(i, s[0])),
            spec,
            spec,
        ],
        out_specs=[spec] * 3,
    )
    return pl.pallas_call(
        functools.partial(kernel, rate, decay),
        grid_spec=grid_spec,
        out_shape=[jax.ShapeDtypeStruct(weight.shape, F32)] * 3,
        compiler_params=pltpu.CompilerParams(vmem_limit_bytes=60 * 2**20),
        cost_estimate=pl.CostEstimate(
            flops=weight.size * 16, bytes_accessed=weight.size * 26, transcendentals=weight.size
        ),
        name="update_pieces",
    )(side.reshape(1).astype(jnp.int32), clip.reshape(1), weight, pieces, moment, square)


def split_kernel(unit, side_ref, in_ref, out_ref, *part_refs):
    slim = part_refs[0].shape[1] // 3
    for part, ref in enumerate(part_refs):
        for n in range(slim // unit):
            cut = slice(part * slim + n * unit, part * slim + (n + 1) * unit)
            for j in range(2):
                first = (2 * n + j) * unit
                ref[:, first : first + unit] = in_ref[j, :, cut].astype(BF16)
        ref[:, 2 * slim :] = out_ref[part * slim : (part + 1) * slim, :].T.astype(BF16)


def split_feed(feed_in, feed_out, side, unit):
    depth, hidden = feed_in.shape[1], feed_in.shape[2] // 2
    part = jax.ShapeDtypeStruct((depth, 3 * hidden // 2), BF16)
    grid_spec = pltpu.PrefetchScalarGridSpec(
        num_scalar_prefetch=1,
        grid=(1,),
        in_specs=[
            pl.BlockSpec((2, depth, hidden), lambda i, s: (0, 0, s[0])),
            pl.BlockSpec((hidden, depth), lambda i, s: (s[0], 0)),
        ],
        out_specs=[pl.BlockSpec(part.shape, lambda i, s: (0, 0))] * 2,
    )
    return pl.pallas_call(
        functools.partial(split_kernel, unit),
        grid_spec=grid_spec,
        out_shape=[part] * 2,
        compiler_params=pltpu.CompilerParams(vmem_limit_bytes=60 * 2**20),
        cost_estimate=pl.CostEstimate(
            flops=depth * hidden * 3, bytes_accessed=depth * hidden * 18, transcendentals=0
        ),
        name="split_feed",
    )(side.reshape(1).astype(jnp.int32), feed_in, feed_out)


def feed_kernel(unit, rows_ref, back_ref, weight_ref, activated_ref, grad_ref):
    units = activated_ref.shape[1] // unit
    for n in range(units):
        first = 2 * n * unit
        both = jnp.dot(
            rows_ref[...], weight_ref[:, first : first + 2 * unit], preferred_element_type=F32
        )
        first = (2 * units + n) * unit
        back = jnp.dot(
            back_ref[...], weight_ref[:, first : first + unit], preferred_element_type=F32
        )
        gate, upward = both[:, :unit], both[:, unit:]
        chance = jax.nn.sigmoid(gate)
        silu = gate * chance
        activated_ref[:, n * unit : (n + 1) * unit] = (silu * upward).astype(BF16)
        grad_ref[:, 2 * n * unit : (2 * n + 1) * unit] = (
            back * upward * (chance + silu * (1.0 - chance))
        ).astype(BF16)
        grad_ref[:, (2 * n + 1) * unit : 2 * (n + 1) * unit] = (back * silu).astype(BF16)


def feed_both_ways(rows, back, weight, unit):
    count, width = rows.shape
    slim = weight.shape[1] // 3
    tall = min(count, 512)
    return pl.pallas_call(
        functools.partial(feed_kernel, unit),
        grid=(count // tall,),
        in_specs=[
            pl.BlockSpec((tall, width), lambda i: (i, 0)),
            pl.BlockSpec((tall, width), lambda i: (i, 0)),
            pl.BlockSpec(weight.shape, lambda i: (0, 0)),
        ],
        out_specs=[
            pl.BlockSpec((tall, slim), lambda i: (i, 0)),
            pl.BlockSpec((tall, 2 * slim), lambda i: (i, 0)),
        ],
        out_shape=[
            jax.ShapeDtypeStruct((count, slim), BF16),
            jax.ShapeDtypeStruct((count, 2 * slim), BF16),
        ],
        compiler_params=pltpu.CompilerParams(vmem_limit_bytes=48 * 2**20),
        cost_estimate=pl.CostEstimate(
            flops=6 * count * width * slim,
            bytes_accessed=4 * count * width + 6 * width * slim + 6 * count * slim,
            transcendentals=count * slim,
        ),
        name="feed_both_ways",
    )(rows, back, weight)


def weights_kernel(scale, rows_ref, grad_ref, back_ref, activated_ref, out_ref):
    wide = grad_ref.shape[1]
    out_ref[0, :, :wide] = (product(rows_ref[...], grad_ref[...], 0, 0) * scale).astype(BF16)
    out_ref[0, :, wide:] = (product(back_ref[...], activated_ref[...], 0, 0) * scale).astype(BF16)


def weight_gradients(rows, grad, back, activated, parts, scale):
    count, width = rows.shape
    cut, slim = width // parts, activated.shape[1]
    return pl.pallas_call(
        functools.partial(weights_kernel, scale),
        grid=(parts,),
        in_specs=[
            pl.BlockSpec((count, cut), lambda i: (0, i)),
            pl.BlockSpec(grad.shape, lambda i: (0, 0)),
            pl.BlockSpec((count, cut), lambda i: (0, i)),
            pl.BlockSpec(activated.shape, lambda i: (0, 0)),
        ],
        out_specs=pl.BlockSpec((1, cut, 3 * slim), lambda i: (i, 0, 0)),
        out_shape=jax.ShapeDtypeStruct((parts, cut, 3 * slim), BF16),
        compiler_params=pltpu.CompilerParams(vmem_limit_bytes=48 * 2**20),
        cost_estimate=pl.CostEstimate(
            flops=6 * count * width * slim,
            bytes_accessed=4 * count * width + 6 * count * slim + 6 * width * slim,
            transcendentals=0,
        ),
        name="weight_gradients",
    )(rows, grad, back, activated)


def back_kernel(*refs):
    total = 0.0
    for left, right in zip(refs[:-1:2], refs[1:-1:2]):
        total = total + product(left[...], right[...], 1, 1)
    refs[-1][...] = total.astype(BF16)


def back_products(pairs, first, last, half):
    count, width = pairs[0][0].shape[0] // 2, pairs[0][1].shape[0]
    tall = min(count, 512)
    skip, place = half * (count // tall), first // (last - first)
    specs, operands = [], []
    for left, right in pairs:
        depth = left.shape[1]
        specs.append(pl.BlockSpec((tall, depth), lambda i: (i + skip, 0)))
        specs.append(pl.BlockSpec((width, depth), lambda i: (0, place)))
        operands += [left, right]
    depth = sum(left.shape[1] for left, _ in pairs)
    return pl.pallas_call(
        back_kernel,
        grid=(count // tall,),
        in_specs=specs,
        out_specs=pl.BlockSpec((tall, width), lambda i: (i, 0)),
        out_shape=jax.ShapeDtypeStruct((count, width), BF16),
        compiler_params=pltpu.CompilerParams(vmem_limit_bytes=56 * 2**20),
        cost_estimate=pl.CostEstimate(
            flops=2 * count * width * depth,
            bytes_accessed=2 * count * (width + depth) + 2 * width * depth,
            transcendentals=0,
        ),
        name="back_products",
    )(*operands)


def in_order(mine, other, first, axis):
    return jnp.where(
        first,
        jnp.concatenate([mine, other], axis=axis),
        jnp.concatenate([other, mine], axis=axis),
    )


def shards(
    sizes,
    tensor,
    tokens,
    cotangent,
    doc_lengths,
    attend_in,
    attend_out,
    feed_in,
    feed_out,
    norm_gains,
    moment_attend_in,
    square_attend_in,
    moment_attend_out,
    square_attend_out,
    moment_feed_in,
    square_feed_in,
    moment_feed_out,
    square_feed_out,
    moment_gains,
    square_gains,
):
    pack_links, core = tensor[:-1], tensor[-1]
    feed_links = ("x",) + tuple(pack_links)
    devices = math.prod(sizes[a] for a in tensor)
    side = lax.axis_index("x")
    is_first = side == 0
    local_rows, width = tokens.shape
    rows = local_rows * devices
    token_total = rows * 2 * sizes["z"]
    inverse_total = 1.0 / token_total
    docs = doc_lengths.shape[1]
    meta = jnp.concatenate(
        [lax.axis_index(tuple(tensor))[None].astype(jnp.int32), jnp.cumsum(doc_lengths[0])]
    )
    cosine, sine = rotation_tables(doc_lengths[0], rows)

    hidden = feed_in.shape[2] // 2
    slim = hidden // 2
    unit = hidden // UNITS
    depth = attend_in.shape[0]
    half = rows // 2

    def halves(array, axis):
        size = array.shape[axis] // 2
        mine = lax.dynamic_slice_in_dim(array, side * size, size, axis)
        other = lax.dynamic_slice_in_dim(array, (1 - side) * size, size, axis)
        return mine, other

    def sends(block, links):
        return [flip(block, c, sizes) for c in combos(links)[1:]]

    def over_core(blocks):
        mine = jnp.concatenate(blocks, axis=0)
        return jnp.concatenate([mine, flip(mine, (core,), sizes)], axis=0)

    def both_sides(mine, other):
        pair = jnp.where(
            is_first, jnp.stack([mine, other], axis=1), jnp.stack([other, mine], axis=1)
        )
        return pair

    gain_rows = jnp.pad(
        norm_gains.astype(BF16), ((0, 14), (0, attend_in.shape[1] - norm_gains.shape[1]))
    )
    in_z = lax.all_gather(
        jnp.concatenate([attend_in.astype(BF16), gain_rows], axis=0), "z", axis=0, tiled=False
    )
    out_z = gather_depth(attend_out.T.astype(BF16), sizes)
    tokens_moved = sends(tokens, pack_links)
    away = split_feed(feed_in, feed_out, 1 - side, unit)
    moved = [flip(part, ("x",), sizes) for part in away]
    kept = split_feed(feed_in, feed_out, side, unit)
    locals_ = [in_order(part, other, is_first, 0) for part, other in zip(kept, moved)]
    in_z, out_z, cotangent_then, tokens_moved, locals_ = lax.optimization_barrier(
        (in_z, out_z, cotangent, tokens_moved, locals_)
    )

    weight_a, weight_b = [lax.all_gather(part, "z", axis=0, tiled=True) for part in locals_]
    in_x = flip(in_z, ("x",), sizes)
    back_moved = sends(cotangent_then, pack_links)
    tokens_all = over_core([tokens] + tokens_moved)
    in_x, back_moved, tokens_all = lax.optimization_barrier((in_x, back_moved, tokens_all))

    out_x = flip(out_z, ("x",), sizes)
    in_both = both_sides(in_z, in_x)
    full_in = in_both[:, :, :depth].reshape(width, attend_in.shape[1])
    gains = (
        in_both[:, :, depth : depth + 2, : norm_gains.shape[1]]
        .astype(F32)
        .transpose(2, 0, 1, 3)
        .reshape(2, width)
    )
    inputs_all = tokens_all.astype(F32)
    normed_one = (inputs_all * norm_rate(inputs_all) * gains[0]).astype(BF16)
    joined = product(normed_one, full_in, 1, 0)
    attended, qkv, logs = attend_forward(meta, joined, cosine, sine, docs, devices)
    back_near = jnp.concatenate([cotangent] + back_moved, axis=0)
    attended, out_x, left, right = lax.optimization_barrier(
        (attended, out_x, back_near[:, : width // 2], back_near[:, width // 2 :])
    )

    full_out = both_sides(out_z, out_x).reshape(width, attend_out.shape[0])
    near = product(attended[half:], full_out, 1, 1).astype(BF16)
    mine = product(attended[:half], full_out, 1, 1).astype(BF16)
    own, moved = collect(mine, near, pack_links, core, sizes)
    left = flip(left, ("x",), sizes)
    right = flip(right, ("x",), sizes)
    own, moved, left, right = lax.optimization_barrier((own, moved, left, right))

    inputs = tokens.astype(F32)
    hidden_state = inputs + added(own, moved)
    rate_two = norm_rate(hidden_state)
    normed_two = (hidden_state * rate_two * gains[1]).astype(BF16)
    normed_moved = sends(normed_two, feed_links)
    gathered_back = over_core([back_near, jnp.concatenate([left, right], axis=1)])
    normed_moved, gathered_back = lax.optimization_barrier((normed_moved, gathered_back))
    gathered_two = over_core([normed_two] + normed_moved)

    def gradients(grad, activated):
        return weight_gradients(
            gathered_two, grad, gathered_back, activated, sizes["z"], inverse_total
        )

    def summed(parts):
        return lax.psum_scatter(parts, "z", scatter_dimension=0, tiled=False)

    activated_a, grad_a = feed_both_ways(gathered_two, gathered_back, weight_a, unit)
    parts_a = gradients(grad_a, activated_a)
    parts_a, weight_b = lax.optimization_barrier((parts_a, weight_b))
    sums_a = summed(parts_a)
    activated_b, grad_b = feed_both_ways(gathered_two, gathered_back, weight_b, unit)
    pairs = [(grad_a, weight_a), (grad_b, weight_b)]
    near = flip(back_products(pairs, 0, 2, 1), (core,), sizes)
    mine = back_products(pairs, 0, 2, 0)
    blocks = add_blocks(mine, near, 2 ** len(feed_links))
    blocks, grad_b, activated_a, activated_b = lax.optimization_barrier(
        (blocks, grad_b, activated_a, activated_b)
    )
    moved = [flip(block, c, sizes) for block, c in zip(blocks[1:], combos(feed_links)[1:])]
    pairs = [(activated_a, weight_a), (activated_b, weight_b)]
    forward_near = flip(back_products(pairs, 2, 3, 1), (core,), sizes)
    forward_mine = back_products(pairs, 2, 3, 0)
    forward_blocks = add_blocks(forward_mine, forward_near, 2 ** len(feed_links))
    parts_b = gradients(grad_b, activated_b)
    sums_b = summed(parts_b)
    moved, forward_blocks, parts_b = lax.optimization_barrier((moved, forward_blocks, parts_b))

    grad_from_two, gain_two_grad = norm_back(
        hidden_state, rate_two, gains[1], added(blocks[0], moved)
    )
    grad_hidden = cotangent.astype(F32) + grad_from_two
    grad_branch = grad_hidden.astype(BF16)
    forward_links = combos(feed_links)[1:]
    forward_moved = {("x",): flip(forward_blocks[forward_links.index(("x",)) + 1], ("x",), sizes)}

    def regroup(sums):
        mine, other = halves(sums, 0)
        return jnp.stack([mine, flip(other, ("x",), sizes)])

    sums_a, grad_branch = lax.optimization_barrier((sums_a, grad_branch))
    grad_moved = sends(grad_branch, pack_links)
    pieces_a = regroup(sums_a)
    grad_moved, forward_moved, pieces_a = lax.optimization_barrier(
        (grad_moved, forward_moved, pieces_a)
    )
    gathered_grad = over_core([grad_branch] + grad_moved)
    grad_attended = product(gathered_grad, full_out, 1, 0).astype(BF16)
    groups = attend_in.shape[1] // ((GROUP + 2) * HD)
    grad_joined = [
        attend_backward(meta, qkv, logs, grad_attended, cosine, sine, docs, devices, group)
        for group in range(groups)
    ]

    def split_sides(grad):
        split = (grad * inverse_total).astype(BF16).reshape(sizes["z"], 2, -1, grad.shape[1])
        mine = lax.dynamic_index_in_dim(split, side, 1, keepdims=False)
        other = lax.dynamic_index_in_dim(split, 1 - side, 1, keepdims=False)
        return mine, flip(other, ("x",), sizes)

    out_mine, out_other = split_sides(product(gathered_grad, attended, 0, 0))
    grad_joined[-1], out_other = lax.optimization_barrier((grad_joined[-1], out_other))
    attend_out_shard = sum_depth(added(out_mine, [out_other]).astype(BF16)).T
    in_pairs = [split_sides(product(normed_one, grad, 0, 0)) for grad in grad_joined]
    forward_moved |= {
        c: flip(block, c, sizes)
        for block, c in zip(forward_blocks[1:], forward_links)
        if c != ("x",)
    }
    in_pairs, forward_moved = lax.optimization_barrier((in_pairs, forward_moved))
    block_out = added(forward_blocks[0], list(forward_moved.values()))
    block_out = (hidden_state + block_out).astype(BF16)
    in_parts = [added(mine, [other]).astype(BF16) for mine, other in in_pairs]
    attend_in_shard = sum_depth(jnp.concatenate(in_parts, axis=2))
    joined_back = jnp.concatenate(grad_joined, axis=1)
    own, moved = collect(
        product(joined_back[:half], full_in, 1, 1).astype(BF16),
        product(joined_back[half:], full_in, 1, 1).astype(BF16),
        pack_links,
        core,
        sizes,
    )
    grad_normed_one = added(own, moved)
    grad_from_one, gain_one_grad = norm_back(inputs, norm_rate(inputs), gains[0], grad_normed_one)
    tokens_grad = (grad_hidden + grad_from_one).astype(BF16)

    pieces = jnp.stack([pieces_a, regroup(sums_b)], axis=1)

    def squares(shard):
        shard = shard.astype(F32)
        return jnp.sum(shard * shard)

    matrix_squares = (
        squares(attend_in_shard)
        + squares(attend_out_shard)
        + squares(pieces)
    )
    total = sum_everywhere(
        jnp.concatenate(
            [
                gain_one_grad * inverse_total,
                gain_two_grad * inverse_total,
                jnp.full((LANES,), matrix_squares),
            ]
        ),
        tensor,
        sizes,
    )
    gain_grads = total[: 2 * width].reshape(2, width)
    grad_norm = jnp.sqrt(total[2 * width] + jnp.sum(gain_grads * gain_grads))
    clip = jnp.minimum(1.0, CLIP_LIMIT / (grad_norm + 1e-06))
    gain_width = norm_gains.shape[1]
    gain_shard = lax.dynamic_slice_in_dim(
        gain_grads, lax.axis_index(("z", "x")) * gain_width, gain_width, 1
    )
    first = update(attend_in, attend_in_shard, moment_attend_in, square_attend_in, clip, MATRIX_RATE, MATRIX_DECAY)
    second = update(attend_out, attend_out_shard, moment_attend_out, square_attend_out, clip, OUTPUT_RATE, MATRIX_DECAY)
    tall = depth // 2
    third = update_pieces(
        adam_rows_kernel, feed_in, pieces, moment_feed_in, square_feed_in, clip, side,
        (2, tall, feed_in.shape[2]), lambda i: (0, i, 0),
        (2, 2, tall, 2 * slim), lambda i, s: (0, 0, i, 0),
        MATRIX_RATE, MATRIX_DECAY,
    )
    fourth = update_pieces(
        adam_columns_kernel, feed_out, pieces, moment_feed_out, square_feed_out, clip, side,
        (slim, depth), lambda i: (i, 0),
        (1, 1, depth, slim), lambda i, s: ((i // 2) ^ s, i % 2, 0, 2),
        MATRIX_RATE, MATRIX_DECAY,
    )
    fifth = adam(norm_gains, gain_shard, moment_gains, square_gains, clip, GAIN_RATE, 0.0)
    return (block_out, tokens_grad, grad_norm, *first, *second, *third, *fourth, *fifth)


def solution(mesh):
    depth, across = mesh.shape["dp"], mesh.shape["tensor"]
    tensor = tuple("t" + str(i) for i in range(across.bit_length() - 1))
    sizes = {"z": depth // 2, "x": 2, **{a: 2 for a in tensor}}
    assert depth % 2 == 0 and 2 ** len(tensor) == across
    fine = Mesh(mesh.devices.reshape(tuple(sizes.values())), tuple(sizes))
    dp = ("z", "x")
    both = P(dp + tensor, None)
    rows_cut, columns_cut = P(dp, tensor), P(tensor, dp)
    feed_cut, gain_cut = P(None, dp, tensor), P(None, dp)
    state = (rows_cut,) * 3 + (columns_cut,) * 3 + (feed_cut,) * 3 + (columns_cut,) * 3 + (gain_cut,) * 3
    return jax.shard_map(
        functools.partial(shards, sizes, tensor),
        mesh=fine,
        in_specs=(both, both, P(dp, None), rows_cut, columns_cut, feed_cut, columns_cut, gain_cut)
        + (rows_cut,) * 2
        + (columns_cut,) * 2
        + (feed_cut,) * 2
        + (columns_cut,) * 2
        + (gain_cut,) * 2,
        out_specs=(both, both, P()) + state,
        check_vma=False,
    )
```

```python
import functools
import math

import jax
import jax.numpy as jnp
from jax import lax
from jax.experimental import pallas as pl
from jax.experimental.pallas import tpu as pltpu
from jax.sharding import Mesh
from jax.sharding import PartitionSpec as P

H = 32
KV = 8
HD = 64
GROUP = H // KV
STEP = 10
LANES = 128
QUERY_ROWS = 256
UNITS = 4

EPSILON = 1e-05
NEGATIVE = -1e30
CLIP_LIMIT = 0.25
BETA_ONE = 0.9
BETA_TWO = 0.95
ADAM_EPSILON = 1e-08
MATRIX_RATE = 0.04
OUTPUT_RATE = 0.3
MATRIX_DECAY = 0.1
GAIN_RATE = 0.6

BF16 = jnp.bfloat16
F32 = jnp.float32


def flip(value, axes, sizes):
    count = math.prod(sizes[a] for a in axes)
    pairs = [(i, i ^ (count - 1)) for i in range(count)]
    return lax.ppermute(value, tuple(axes), pairs)


def combos(axes):
    return [
        tuple(a for i, a in enumerate(axes) if place >> (len(axes) - 1 - i) & 1)
        for place in range(2 ** len(axes))
    ]


def add_kernel(mine_ref, near_ref, *out_refs):
    for k, ref in enumerate(out_refs):

        @pl.when(pl.program_id(0) == k)
        def _():
            ref[...] = (mine_ref[...].astype(F32) + near_ref[...].astype(F32)).astype(BF16)


def add_blocks(mine, near, count):
    rows, width = mine.shape[0] // count, mine.shape[1]
    cut = pl.BlockSpec((rows, width), lambda i: (i, 0))
    return pl.pallas_call(
        add_kernel,
        grid=(count,),
        in_specs=[cut, cut],
        out_specs=[pl.BlockSpec((rows, width), lambda i: (0, 0))] * count,
        out_shape=[jax.ShapeDtypeStruct((rows, width), BF16)] * count,
        compiler_params=pltpu.CompilerParams(vmem_limit_bytes=32 * 2**20),
        cost_estimate=pl.CostEstimate(flops=1, bytes_accessed=1, transcendentals=0),
        name="add_blocks",
    )(mine, near)


def collect(mine, near, links, core, sizes):
    places = combos(links)
    blocks = add_blocks(mine, flip(near, (core,), sizes), len(places))
    return blocks[0], [flip(block, c, sizes) for block, c in zip(blocks[1:], places[1:])]


def added(own, moved):
    return sum((block.astype(F32) for block in moved), own.astype(F32))


def gather_depth(block, sizes):
    copies = jnp.broadcast_to(block, (sizes["z"],) + block.shape)
    return lax.all_to_all(copies, "z", 0, 0, tiled=True)


def to_owners(blocks):
    return lax.all_to_all(blocks, "z", 0, 0, tiled=True)


def sum_terms(terms):
    return jnp.sum(terms.astype(F32), axis=0).astype(BF16)


def sum_near(value, tensor, sizes):
    for a in tuple(reversed(tensor)) + ("x",):
        value = value + flip(value, (a,), sizes)
    return value


def sum_far(value, sizes):
    step, count = 1, sizes["z"]
    while step < count:
        value = value + lax.ppermute(value, "z", [(i, i ^ step) for i in range(count)])
        step *= 2
    return value


def sum_scalar(value, axes, sizes):
    count = math.prod(sizes[a] for a in axes)
    terms = lax.all_to_all(jnp.full((count, LANES), value), axes, 0, 0, tiled=True)
    return jnp.sum(terms[:, 0])


def frequencies(head_size):
    half_index = jnp.arange(head_size // 2, dtype=F32)
    inverse = jnp.power(500000.0, -2.0 * half_index / head_size)
    wavelength = 2.0 * math.pi / inverse
    smooth = (8192.0 / wavelength - 1.0) / 3.0
    blended = (1.0 - smooth) * inverse / 32.0 + smooth * inverse
    return jnp.where(
        wavelength < 2048.0, inverse, jnp.where(wavelength > 8192.0, inverse / 32.0, blended)
    )


def rotation_tables(lengths_row, rows):
    token_ids = jnp.arange(rows, dtype=jnp.int32)
    ends = jnp.cumsum(lengths_row)
    past = (token_ids[:, None] >= ends[None, :]).astype(jnp.int32)
    positions = token_ids - jnp.sum(past * lengths_row[None, :], axis=1)
    angles = positions.astype(F32)[:, None] * frequencies(HD)[None, :]
    cosine, sine = jnp.cos(angles), jnp.sin(angles)
    return (
        jnp.concatenate([cosine] * 4, axis=1),
        jnp.concatenate([-sine, sine, -sine, sine], axis=1),
    )


def exchange_halves(tile):
    lane = lax.broadcasted_iota(jnp.int32, tile.shape, 1)
    return jnp.where(
        lane % HD < HD // 2,
        pltpu.roll(tile, LANES - HD // 2, 1),
        pltpu.roll(tile, HD // 2, 1),
    )


def block_place(meta_ref, j, devices):
    relative = meta_ref[0] ^ j
    return (relative & 1) * (devices // 2) + (relative >> 1)


def allowed_bias(meta_ref, docs, first, keys, queries):
    token = lax.broadcasted_iota(jnp.int32, (1, queries), 1) + first
    start = jnp.zeros((1, queries), jnp.int32)
    for j in range(docs - 1):
        start = jnp.where(token >= meta_ref[1 + j], meta_ref[1 + j], start)
    other = lax.broadcasted_iota(jnp.int32, (keys, queries), 0)
    return jnp.where((other <= token) & (other >= start), 0.0, NEGATIVE)


def last_dims(left, right):
    return lax.dot_general(left, right, (((1,), (1,)), ((), ())), preferred_element_type=F32)


def key_halves(qkv_ref, keep_keys, keep_values, keep_turned):
    tile = qkv_ref[:, 2 * LANES : 3 * LANES].astype(F32)
    lane = lax.broadcasted_iota(jnp.int32, tile.shape, 1)
    low = jnp.where(lane < HD, tile, 0.0)
    high = jnp.where(lane < HD, 0.0, tile)
    pairs = ((low, pltpu.roll(low, HD, 1)), (pltpu.roll(high, HD, 1), high))
    for half in range(2):
        if keep_keys is not None:
            keep_keys[half] = pairs[0][half].astype(BF16)
        if keep_values is not None:
            keep_values[half] = pairs[1][half].astype(BF16)
        if keep_turned is not None:
            source, ref = keep_turned
            ref[half] = pairs[source][half].T.astype(BF16)


def forward_kernel(docs, devices, meta_ref, joined_ref, cos_ref, sin_ref, attended_ref, qkv_ref, log_ref, keys_ref, turned_ref):
    rows = joined_ref.shape[0]
    block = rows // devices
    for j in range(devices):
        source = pl.multiple_of(block_place(meta_ref, j, devices) * block, block)
        here = slice(j * block, (j + 1) * block)
        cosine, sine = cos_ref[here, :], sin_ref[here, :]
        lane = lax.broadcasted_iota(jnp.int32, cosine.shape, 1)
        for t in range(3):
            tile = joined_ref[pl.ds(source, block), t * LANES : (t + 1) * LANES]
            turned = tile * cosine + exchange_halves(tile) * sine
            if t == 2:
                turned = jnp.where(lane < HD, turned, tile)
            qkv_ref[here, t * LANES : (t + 1) * LANES] = turned.astype(BF16)
    key_halves(qkv_ref, keys_ref, None, (1, turned_ref))
    for i in range(rows // QUERY_ROWS):
        keys = (i + 1) * QUERY_ROWS
        here = slice(i * QUERY_ROWS, keys)
        bias = allowed_bias(meta_ref, docs, i * QUERY_ROWS, keys, QUERY_ROWS)
        for t in range(2):
            query = qkv_ref[here, t * LANES : (t + 1) * LANES] * BF16(HD**-0.5)
            total = jnp.zeros((LANES, QUERY_ROWS), F32)
            for half in range(2):
                scores = last_dims(keys_ref[half, :keys, :], query) + bias
                peak = jnp.max(scores, axis=0, keepdims=True)
                raised = jnp.exp(scores - peak)
                mass = jnp.sum(raised, axis=0, keepdims=True)
                probs = (raised * (1.0 / mass)).astype(BF16)
                total = total + jnp.dot(
                    turned_ref[half, :, :keys], probs, preferred_element_type=F32
                )
                head = 2 * t + half
                log_ref[0, head : head + 1, here] = peak + jnp.log(mass)
            done = total.T.astype(BF16)
            step = min(block, QUERY_ROWS)
            for part in range(QUERY_ROWS // step):
                first = i * QUERY_ROWS + part * step
                place = block_place(meta_ref, first // block, devices) * block + first % block
                attended_ref[
                    pl.ds(pl.multiple_of(place, step), step), t * LANES : (t + 1) * LANES
                ] = done[part * step : (part + 1) * step, :]


def backward_kernel(docs, devices, meta_ref, qkv_ref, log_ref, back_ref, cos_ref, sin_ref, grad_ref, keys_ref, values_ref, turned_ref, key_total, value_total, query_total, back_here):
    rows = qkv_ref.shape[0]
    block = rows // devices
    key_halves(qkv_ref, keys_ref, values_ref, (0, turned_ref))
    for j in range(devices):
        source = pl.multiple_of(block_place(meta_ref, j, devices) * block, block)
        back_here[j * block : (j + 1) * block, :] = back_ref[pl.ds(source, block), :]
    key_total[...] = jnp.zeros_like(key_total)
    value_total[...] = jnp.zeros_like(value_total)
    for i in range(rows // QUERY_ROWS):
        keys = (i + 1) * QUERY_ROWS
        here = slice(i * QUERY_ROWS, keys)
        bias = allowed_bias(meta_ref, docs, i * QUERY_ROWS, keys, QUERY_ROWS)
        lane = lax.broadcasted_iota(jnp.int32, (QUERY_ROWS, LANES), 1)
        for t in range(2):
            columns = slice(t * LANES, (t + 1) * LANES)
            query = qkv_ref[here, columns] * BF16(HD**-0.5)
            back = back_here[here, columns]
            total = jnp.zeros((LANES, QUERY_ROWS), F32)
            for half in range(2):
                head = 2 * t + half
                mine = (lane < HD) if half == 0 else (lane >= HD)
                scores = last_dims(keys_ref[half, :keys, :], query) + bias
                probs = jnp.exp(scores - log_ref[0, head : head + 1, here])
                moved = last_dims(values_ref[half, :keys, :], back)
                inner = jnp.sum(probs * moved, axis=0, keepdims=True)
                grad = (probs * (moved - inner)).astype(BF16)
                total = total + jnp.dot(
                    turned_ref[half, :, :keys], grad, preferred_element_type=F32
                )
                key_total[:keys, :] += jnp.dot(
                    grad, jnp.where(mine, query, BF16(0)), preferred_element_type=F32
                )
                value_total[:keys, :] += jnp.dot(
                    probs.astype(BF16), jnp.where(mine, back, BF16(0)), preferred_element_type=F32
                )
            query_total[here, columns] = total.T * HD**-0.5
    for j in range(devices):
        place = pl.multiple_of(block_place(meta_ref, j, devices) * block, block)
        here = slice(j * block, (j + 1) * block)
        cosine, sine = cos_ref[here, :], sin_ref[here, :]
        lane = lax.broadcasted_iota(jnp.int32, cosine.shape, 1)
        for t in range(2):
            columns = slice(t * LANES, (t + 1) * LANES)
            tile = query_total[here, columns]
            grad_ref[pl.ds(place, block), columns] = (
                tile * cosine - exchange_halves(tile) * sine
            ).astype(BF16)
        tile = key_total[here, :]
        tile = tile + pltpu.roll(tile, HD, 1)
        other = value_total[here, :]
        other = other + pltpu.roll(other, HD, 1)
        tile = jnp.where(lane < HD, tile * cosine - exchange_halves(tile) * sine, other)
        grad_ref[pl.ds(place, block), 2 * LANES : 3 * LANES] = tile.astype(BF16)


def attend_forward(meta, joined, cosine, sine, docs, devices):
    rows, width = joined.shape
    wide = (GROUP + 2) * HD
    groups = width // wide
    whole = pl.BlockSpec((rows, LANES), lambda g: (0, 0))
    return pl.pallas_call(
        functools.partial(forward_kernel, docs, devices),
        grid=(groups,),
        in_specs=[
            pl.BlockSpec(memory_space=pltpu.SMEM),
            pl.BlockSpec((rows, wide), lambda g: (0, g)),
            whole,
            whole,
        ],
        out_specs=[
            pl.BlockSpec((rows, GROUP * HD), lambda g: (0, g)),
            pl.BlockSpec((rows, wide), lambda g: (0, g)),
            pl.BlockSpec((1, 8, rows), lambda g: (g, 0, 0)),
        ],
        out_shape=[
            jax.ShapeDtypeStruct((rows, groups * GROUP * HD), BF16),
            jax.ShapeDtypeStruct((rows, width), BF16),
            jax.ShapeDtypeStruct((groups, 8, rows), F32),
        ],
        scratch_shapes=[
            pltpu.VMEM((2, rows, LANES), BF16),
            pltpu.VMEM((2, LANES, rows), BF16),
        ],
        compiler_params=pltpu.CompilerParams(vmem_limit_bytes=32 * 2**20),
        cost_estimate=pl.CostEstimate(flops=1, bytes_accessed=1, transcendentals=0),
        name="attend_forward",
    )(meta, joined, cosine, sine)


def attend_backward(meta, qkv, logs, back, cosine, sine, docs, devices, group):
    rows = qkv.shape[0]
    wide = (GROUP + 2) * HD
    whole = pl.BlockSpec((rows, LANES), lambda g: (0, 0))
    return pl.pallas_call(
        functools.partial(backward_kernel, docs, devices),
        grid=(1,),
        in_specs=[
            pl.BlockSpec(memory_space=pltpu.SMEM),
            pl.BlockSpec((rows, wide), lambda g: (0, group)),
            pl.BlockSpec((1, 8, rows), lambda g: (group, 0, 0)),
            pl.BlockSpec((rows, GROUP * HD), lambda g: (0, group)),
            whole,
            whole,
        ],
        out_specs=pl.BlockSpec((rows, wide), lambda g: (0, 0)),
        out_shape=jax.ShapeDtypeStruct((rows, wide), BF16),
        scratch_shapes=[
            pltpu.VMEM((2, rows, LANES), BF16),
            pltpu.VMEM((2, rows, LANES), BF16),
            pltpu.VMEM((2, LANES, rows), BF16),
            pltpu.VMEM((rows, LANES), F32),
            pltpu.VMEM((rows, LANES), F32),
            pltpu.VMEM((rows, GROUP * HD), F32),
            pltpu.VMEM((rows, GROUP * HD), BF16),
        ],
        compiler_params=pltpu.CompilerParams(vmem_limit_bytes=32 * 2**20),
        cost_estimate=pl.CostEstimate(flops=1, bytes_accessed=1, transcendentals=0),
        name="attend_backward",
    )(meta, qkv, logs, back, cosine, sine)


def product(left, right, left_dim, right_dim):
    return lax.dot_general(
        left, right, (((left_dim,), (right_dim,)), ((), ())), preferred_element_type=F32
    )


def norm_rate(vector):
    return lax.rsqrt(jnp.mean(vector * vector, axis=-1, keepdims=True) + EPSILON)


def norm_back(vector, rate, gain, grad):
    scaled = gain * grad
    inner = jnp.mean(vector * scaled, axis=-1, keepdims=True)
    return (
        rate * scaled - vector * (rate * rate * rate * inner),
        jnp.sum(grad * vector * rate, axis=0),
    )


def adam(weight, grad, moment, square, clip, rate, decay):
    clipped = clip * grad
    moment_new = BETA_ONE * moment + (1.0 - BETA_ONE) * clipped
    square_new = BETA_TWO * square + (1.0 - BETA_TWO) * clipped * clipped
    direction = (
        moment_new
        / (1.0 - BETA_ONE**STEP)
        / (jnp.sqrt(square_new / (1.0 - BETA_TWO**STEP)) + ADAM_EPSILON)
    )
    return (weight - rate * (direction + decay * weight), moment_new, square_new)


def adam_all_kernel(rates, side_ref, clip_ref, *refs):
    side, clip = side_ref[0], clip_ref[0]
    pieces_ref, turned_ref, in_grad_ref, out_grad_ref = refs[:4]
    states, outs = refs[4:16], refs[16:]

    def apply(k, grad, at):
        weight, moment, square = [ref[at] for ref in states[3 * k : 3 * k + 3]]
        done = adam(weight, grad.astype(F32), moment, square, clip, *rates[k])
        for ref, value in zip(outs[3 * k : 3 * k + 3], done):
            ref[at] = value

    columns = states[0].shape[-1]
    unit = columns // (2 * UNITS)
    per_half = UNITS // 2
    for n in range(2 * UNITS):
        which, half, place = n // UNITS, n % UNITS // per_half, n % per_half
        for j in range(2):
            first = (2 * place + j) * unit
            grad = pieces_ref[which ^ side, half, :, first : first + unit]
            apply(0, grad, (j, slice(None), slice(n * unit, (n + 1) * unit)))
    apply(1, turned_ref[0, 0].astype(F32).T, (slice(None), slice(None)))
    apply(2, in_grad_ref[...], (slice(None), slice(None)))
    apply(3, out_grad_ref[...], (slice(None), slice(None)))


def update_all(states, pieces, in_grad, out_grad, clip, side, rates):
    steps = 2 * UNITS
    depth, slim = pieces.shape[2], pieces.shape[3] // 3
    unit = 2 * slim // UNITS

    def rows(array):
        lead = array.shape[:-2]
        block = lead + (array.shape[-2] // steps, array.shape[-1])
        return pl.BlockSpec(block, lambda i, s: (0,) * len(lead) + (i, 0))

    specs = [rows(a) for a in states]
    grid_spec = pltpu.PrefetchScalarGridSpec(
        num_scalar_prefetch=1,
        grid=(steps,),
        in_specs=[
            pl.BlockSpec(memory_space=pltpu.SMEM),
            pl.BlockSpec((2, 2, depth // steps, 2 * slim), lambda i, s: (0, 0, i, 0)),
            pl.BlockSpec(
                (1, 1, depth, unit),
                lambda i, s: ((i // UNITS) ^ s[0], i % UNITS // 2, 0, UNITS + i % 2),
            ),
            rows(in_grad),
            rows(out_grad),
        ]
        + specs,
        out_specs=specs,
    )
    return pl.pallas_call(
        functools.partial(adam_all_kernel, rates),
        grid_spec=grid_spec,
        out_shape=[jax.ShapeDtypeStruct(a.shape, F32) for a in states],
        compiler_params=pltpu.CompilerParams(vmem_limit_bytes=60 * 2**20),
        cost_estimate=pl.CostEstimate(flops=1, bytes_accessed=1, transcendentals=0),
        name="update_all",
    )(
        side.reshape(1).astype(jnp.int32),
        clip.reshape(1),
        pieces,
        pieces,
        in_grad,
        out_grad,
        *states,
    )


def split_kernel(unit, side_ref, in_ref, out_ref, *part_refs):
    slim = part_refs[0].shape[1] // 3
    for part, ref in enumerate(part_refs):
        for n in range(slim // unit):
            cut = slice(part * slim + n * unit, part * slim + (n + 1) * unit)
            for j in range(2):
                first = (2 * n + j) * unit
                ref[:, first : first + unit] = in_ref[j, :, cut].astype(BF16)
        ref[:, 2 * slim :] = out_ref[part * slim : (part + 1) * slim, :].T.astype(BF16)


def split_feed(feed_in, feed_out, side, unit):
    depth, hidden = feed_in.shape[1], feed_in.shape[2] // 2
    part = jax.ShapeDtypeStruct((depth, 3 * hidden // 2), BF16)
    grid_spec = pltpu.PrefetchScalarGridSpec(
        num_scalar_prefetch=1,
        grid=(1,),
        in_specs=[
            pl.BlockSpec((2, depth, hidden), lambda i, s: (0, 0, s[0])),
            pl.BlockSpec((hidden, depth), lambda i, s: (s[0], 0)),
        ],
        out_specs=[pl.BlockSpec(part.shape, lambda i, s: (0, 0))] * 2,
    )
    return pl.pallas_call(
        functools.partial(split_kernel, unit),
        grid_spec=grid_spec,
        out_shape=[part] * 2,
        compiler_params=pltpu.CompilerParams(vmem_limit_bytes=60 * 2**20),
        cost_estimate=pl.CostEstimate(flops=1, bytes_accessed=1, transcendentals=0),
        name="split_feed",
    )(side.reshape(1).astype(jnp.int32), feed_in, feed_out)


def feed_kernel(unit, rows_ref, back_ref, weight_ref, activated_ref, grad_ref):
    units = activated_ref.shape[1] // unit
    for n in range(units):
        first = 2 * n * unit
        both = jnp.dot(
            rows_ref[...], weight_ref[:, first : first + 2 * unit], preferred_element_type=F32
        )
        first = (2 * units + n) * unit
        back = jnp.dot(
            back_ref[...], weight_ref[:, first : first + unit], preferred_element_type=F32
        )
        gate, upward = both[:, :unit], both[:, unit:]
        chance = jax.nn.sigmoid(gate)
        silu = gate * chance
        activated_ref[:, n * unit : (n + 1) * unit] = (silu * upward).astype(BF16)
        grad_ref[:, 2 * n * unit : (2 * n + 1) * unit] = (
            back * upward * (chance + silu * (1.0 - chance))
        ).astype(BF16)
        grad_ref[:, (2 * n + 1) * unit : 2 * (n + 1) * unit] = (back * silu).astype(BF16)


def feed_both_ways(rows, back, weight, unit):
    count, width = rows.shape
    slim = weight.shape[1] // 3
    tall = min(count, 512)
    return pl.pallas_call(
        functools.partial(feed_kernel, unit),
        grid=(count // tall,),
        in_specs=[
            pl.BlockSpec((tall, width), lambda i: (i, 0)),
            pl.BlockSpec((tall, width), lambda i: (i, 0)),
            pl.BlockSpec(weight.shape, lambda i: (0, 0)),
        ],
        out_specs=[
            pl.BlockSpec((tall, slim), lambda i: (i, 0)),
            pl.BlockSpec((tall, 2 * slim), lambda i: (i, 0)),
        ],
        out_shape=[
            jax.ShapeDtypeStruct((count, slim), BF16),
            jax.ShapeDtypeStruct((count, 2 * slim), BF16),
        ],
        compiler_params=pltpu.CompilerParams(vmem_limit_bytes=48 * 2**20),
        cost_estimate=pl.CostEstimate(flops=1, bytes_accessed=1, transcendentals=0),
        name="feed_both_ways",
    )(rows, back, weight)


def weights_kernel(scale, rows_ref, grad_ref, back_ref, activated_ref, out_ref):
    wide = grad_ref.shape[1]
    out_ref[0, :, :wide] = (product(rows_ref[...], grad_ref[...], 0, 0) * scale).astype(BF16)
    out_ref[0, :, wide:] = (product(back_ref[...], activated_ref[...], 0, 0) * scale).astype(BF16)


def weight_gradients(rows, grad, back, activated, parts, scale):
    count, width = rows.shape
    cut, slim = width // parts, activated.shape[1]
    return pl.pallas_call(
        functools.partial(weights_kernel, scale),
        grid=(parts,),
        in_specs=[
            pl.BlockSpec((count, cut), lambda i: (0, i)),
            pl.BlockSpec(grad.shape, lambda i: (0, 0)),
            pl.BlockSpec((count, cut), lambda i: (0, i)),
            pl.BlockSpec(activated.shape, lambda i: (0, 0)),
        ],
        out_specs=pl.BlockSpec((1, cut, 3 * slim), lambda i: (i, 0, 0)),
        out_shape=jax.ShapeDtypeStruct((parts, cut, 3 * slim), BF16),
        compiler_params=pltpu.CompilerParams(vmem_limit_bytes=48 * 2**20),
        cost_estimate=pl.CostEstimate(flops=1, bytes_accessed=1, transcendentals=0),
        name="weight_gradients",
    )(rows, grad, back, activated)


def back_kernel(*refs):
    total = 0.0
    for left, right in zip(refs[:-1:2], refs[1:-1:2]):
        total = total + product(left[...], right[...], 1, 1)
    refs[-1][...] = total.astype(BF16)


def back_products(pairs, first, last, half):
    count, width = pairs[0][0].shape[0] // 2, pairs[0][1].shape[0]
    tall = min(count, 512)
    skip, place = half * (count // tall), first // (last - first)
    specs, operands = [], []
    for left, right in pairs:
        depth = left.shape[1]
        specs.append(pl.BlockSpec((tall, depth), lambda i: (i + skip, 0)))
        specs.append(pl.BlockSpec((width, depth), lambda i: (0, place)))
        operands += [left, right]
    depth = sum(left.shape[1] for left, _ in pairs)
    return pl.pallas_call(
        back_kernel,
        grid=(count // tall,),
        in_specs=specs,
        out_specs=pl.BlockSpec((tall, width), lambda i: (i, 0)),
        out_shape=jax.ShapeDtypeStruct((count, width), BF16),
        compiler_params=pltpu.CompilerParams(vmem_limit_bytes=56 * 2**20),
        cost_estimate=pl.CostEstimate(flops=1, bytes_accessed=1, transcendentals=0),
        name="back_products",
    )(*operands)


def in_order(mine, other, first, axis):
    return jnp.where(
        first,
        jnp.concatenate([mine, other], axis=axis),
        jnp.concatenate([other, mine], axis=axis),
    )


def shards(
    sizes,
    tensor,
    tokens,
    cotangent,
    doc_lengths,
    attend_in,
    attend_out,
    feed_in,
    feed_out,
    norm_gains,
    moment_attend_in,
    square_attend_in,
    moment_attend_out,
    square_attend_out,
    moment_feed_in,
    square_feed_in,
    moment_feed_out,
    square_feed_out,
    moment_gains,
    square_gains,
):
    pack_links, core = tensor[:-1], tensor[-1]
    feed_links = ("x",) + tuple(pack_links)
    devices = math.prod(sizes[a] for a in tensor)
    side = lax.axis_index("x")
    is_first = side == 0
    local_rows, width = tokens.shape
    rows = local_rows * devices
    token_total = rows * 2 * sizes["z"]
    inverse_total = 1.0 / token_total
    docs = doc_lengths.shape[1]
    meta = jnp.concatenate(
        [lax.axis_index(tuple(tensor))[None].astype(jnp.int32), jnp.cumsum(doc_lengths[0])]
    )
    cosine, sine = rotation_tables(doc_lengths[0], rows)

    hidden = feed_in.shape[2] // 2
    slim = hidden // 2
    unit = hidden // UNITS
    depth = attend_in.shape[0]
    half = rows // 2

    def halves(array, axis):
        size = array.shape[axis] // 2
        mine = lax.dynamic_slice_in_dim(array, side * size, size, axis)
        other = lax.dynamic_slice_in_dim(array, (1 - side) * size, size, axis)
        return mine, other

    def sends(block, links):
        return [flip(block, c, sizes) for c in combos(links)[1:]]

    def over_core(blocks):
        mine = jnp.concatenate(blocks, axis=0)
        return jnp.concatenate([mine, flip(mine, (core,), sizes)], axis=0)

    def both_sides(mine, other):
        pair = jnp.where(
            is_first, jnp.stack([mine, other], axis=1), jnp.stack([other, mine], axis=1)
        )
        return pair

    gain_rows = jnp.pad(
        norm_gains.astype(BF16), ((0, 14), (0, attend_in.shape[1] - norm_gains.shape[1]))
    )
    in_z = lax.all_gather(
        jnp.concatenate([attend_in.astype(BF16), gain_rows], axis=0), "z", axis=0, tiled=False
    )
    out_z = gather_depth(attend_out.T.astype(BF16), sizes)
    tokens_moved = sends(tokens, pack_links)
    away = split_feed(feed_in, feed_out, 1 - side, unit)
    moved = [flip(part, ("x",), sizes) for part in away]
    kept = split_feed(feed_in, feed_out, side, unit)
    locals_ = [in_order(part, other, is_first, 0) for part, other in zip(kept, moved)]
    in_z, out_z, cotangent_then, tokens_moved, locals_ = lax.optimization_barrier(
        (in_z, out_z, cotangent, tokens_moved, locals_)
    )

    weight_a, weight_b = [lax.all_gather(part, "z", axis=0, tiled=True) for part in locals_]
    in_x = flip(in_z, ("x",), sizes)
    back_moved = sends(cotangent_then, pack_links)
    tokens_all = over_core([tokens] + tokens_moved)
    in_x, back_moved, tokens_all = lax.optimization_barrier((in_x, back_moved, tokens_all))

    out_x = flip(out_z, ("x",), sizes)
    in_both = both_sides(in_z, in_x)
    full_in = in_both[:, :, :depth].reshape(width, attend_in.shape[1])
    gains = (
        in_both[:, :, depth : depth + 2, : norm_gains.shape[1]]
        .astype(F32)
        .transpose(2, 0, 1, 3)
        .reshape(2, width)
    )
    inputs_all = tokens_all.astype(F32)
    normed_one = (inputs_all * norm_rate(inputs_all) * gains[0]).astype(BF16)
    joined = product(normed_one, full_in, 1, 0)
    attended, qkv, logs = attend_forward(meta, joined, cosine, sine, docs, devices)
    back_near = jnp.concatenate([cotangent] + back_moved, axis=0)
    attended, out_x, left, right = lax.optimization_barrier(
        (attended, out_x, back_near[:, : width // 2], back_near[:, width // 2 :])
    )

    full_out = both_sides(out_z, out_x).reshape(width, attend_out.shape[0])
    near = product(attended[half:], full_out, 1, 1).astype(BF16)
    mine = product(attended[:half], full_out, 1, 1).astype(BF16)
    own, moved = collect(mine, near, pack_links, core, sizes)
    left = flip(left, ("x",), sizes)
    right = flip(right, ("x",), sizes)
    own, moved, left, right = lax.optimization_barrier((own, moved, left, right))

    inputs = tokens.astype(F32)
    hidden_state = inputs + added(own, moved)
    rate_two = norm_rate(hidden_state)
    normed_two = (hidden_state * rate_two * gains[1]).astype(BF16)
    normed_moved = sends(normed_two, feed_links)
    gathered_back = over_core([back_near, jnp.concatenate([left, right], axis=1)])
    normed_moved, gathered_back = lax.optimization_barrier((normed_moved, gathered_back))
    gathered_two = over_core([normed_two] + normed_moved)

    def gradients(grad, activated):
        return weight_gradients(
            gathered_two, grad, gathered_back, activated, sizes["z"], inverse_total
        )

    def summed(parts):
        return lax.psum_scatter(parts, "z", scatter_dimension=0, tiled=False)

    activated_a, grad_a = feed_both_ways(gathered_two, gathered_back, weight_a, unit)
    parts_a = gradients(grad_a, activated_a)
    parts_a, weight_b = lax.optimization_barrier((parts_a, weight_b))
    sums_a = summed(parts_a)
    activated_b, grad_b = feed_both_ways(gathered_two, gathered_back, weight_b, unit)
    pairs = [(grad_a, weight_a), (grad_b, weight_b)]
    near = flip(back_products(pairs, 0, 2, 1), (core,), sizes)
    mine = back_products(pairs, 0, 2, 0)
    blocks = add_blocks(mine, near, 2 ** len(feed_links))
    blocks, grad_b, activated_a, activated_b = lax.optimization_barrier(
        (blocks, grad_b, activated_a, activated_b)
    )
    moved = [flip(block, c, sizes) for block, c in zip(blocks[1:], combos(feed_links)[1:])]
    parts_b = gradients(grad_b, activated_b)
    sums_b = summed(parts_b)
    pairs = [(activated_a, weight_a), (activated_b, weight_b)]
    forward_near = back_products(pairs, 2, 3, 1)
    moved, parts_b, forward_near, activated_a, activated_b = lax.optimization_barrier(
        (moved, parts_b, forward_near, activated_a, activated_b)
    )

    grad_from_two, gain_two_grad = norm_back(
        hidden_state, rate_two, gains[1], added(blocks[0], moved)
    )
    grad_hidden = cotangent.astype(F32) + grad_from_two
    grad_branch = grad_hidden.astype(BF16)

    def regroup(sums):
        mine, other = halves(sums, 0)
        return jnp.stack([mine, flip(other, ("x",), sizes)])

    pairs = [(activated_a, weight_a), (activated_b, weight_b)]
    forward_mine = back_products(pairs, 2, 3, 0)
    forward_blocks = add_blocks(
        forward_mine, flip(forward_near, (core,), sizes), 2 ** len(feed_links)
    )
    sums_a, grad_branch = lax.optimization_barrier((sums_a, grad_branch))
    grad_moved = sends(grad_branch, pack_links)
    pieces_a = regroup(sums_a)
    grad_moved, forward_blocks, pieces_a = lax.optimization_barrier(
        (grad_moved, forward_blocks, pieces_a)
    )
    forward_links = combos(feed_links)[1:]
    forward_first = [
        flip(block, c, sizes)
        for block, c in zip(forward_blocks[1:], forward_links)
        if "x" not in c
    ]
    gathered_grad = over_core([grad_branch] + grad_moved)
    grad_attended = product(gathered_grad, full_out, 1, 0).astype(BF16)
    groups = attend_in.shape[1] // ((GROUP + 2) * HD)
    grad_joined = [
        attend_backward(meta, qkv, logs, grad_attended, cosine, sine, docs, devices, group)
        for group in range(groups)
    ]

    def split_sides(grad):
        split = (grad * inverse_total).astype(BF16).reshape(sizes["z"], 2, -1, grad.shape[1])
        mine = lax.dynamic_index_in_dim(split, side, 1, keepdims=False)
        other = lax.dynamic_index_in_dim(split, 1 - side, 1, keepdims=False)
        return mine, flip(other, ("x",), sizes)

    out_mine, out_other = split_sides(product(gathered_grad, attended, 0, 0))
    in_pairs = [split_sides(product(normed_one, grad, 0, 0)) for grad in grad_joined[:-1]]
    grad_joined[-1], out_other, forward_first, in_pairs = lax.optimization_barrier(
        (grad_joined[-1], out_other, forward_first, in_pairs)
    )
    out_sums = added(out_mine, [out_other]).astype(BF16)
    in_pairs.append(split_sides(product(normed_one, grad_joined[-1], 0, 0)))
    in_pairs, forward_blocks = lax.optimization_barrier((in_pairs, forward_blocks))
    in_parts = [added(mine, [other]).astype(BF16) for mine, other in in_pairs]
    forward_last = [
        flip(block, c, sizes) for block, c in zip(forward_blocks[1:], forward_links) if "x" in c
    ]
    attend_terms = to_owners(jnp.concatenate(in_parts + [out_sums], axis=2))
    joined_back = jnp.concatenate(grad_joined, axis=1)
    own, moved = collect(
        product(joined_back[:half], full_in, 1, 1).astype(BF16),
        product(joined_back[half:], full_in, 1, 1).astype(BF16),
        pack_links,
        core,
        sizes,
    )
    sums_b, forward_last, moved = lax.optimization_barrier((sums_b, forward_last, moved))
    grad_normed_one = added(own, moved)
    grad_from_one, gain_one_grad = norm_back(inputs, norm_rate(inputs), gains[0], grad_normed_one)
    tokens_grad = (grad_hidden + grad_from_one).astype(BF16)

    gain_grads = sum_near(
        jnp.stack([gain_one_grad, gain_two_grad]) * inverse_total, tensor, sizes
    )
    pieces_b = regroup(sums_b)
    def squares(shard):
        shard = shard.astype(F32)
        return jnp.sum(shard * shard)

    feed_squares = squares(sums_a) + squares(sums_b)
    attend_terms, gain_grads, tokens_grad, pieces_b, feed_squares = lax.optimization_barrier(
        (attend_terms, gain_grads, tokens_grad, pieces_b, feed_squares)
    )
    gain_grads = sum_far(gain_grads, sizes)
    attend_sums = sum_terms(attend_terms)
    attend_in_shard = attend_sums[:, : attend_in.shape[1]]
    attend_out_shard = attend_sums[:, attend_in.shape[1] :].T
    block_out = added(forward_blocks[0], forward_first + forward_last)
    block_out = (hidden_state + block_out).astype(BF16)
    pieces = jnp.stack([pieces_a, pieces_b], axis=1)

    matrix_squares = feed_squares + squares(attend_sums)
    total_squares = sum_scalar(matrix_squares, ("z", "x") + tuple(tensor), sizes)
    grad_norm = jnp.sqrt(total_squares + jnp.sum(gain_grads * gain_grads))
    clip = jnp.minimum(1.0, CLIP_LIMIT / (grad_norm + 1e-06))
    clip, block_out = lax.optimization_barrier((clip, block_out))
    gain_width = norm_gains.shape[1]
    gain_shard = lax.dynamic_slice_in_dim(
        gain_grads, lax.axis_index(("z", "x")) * gain_width, gain_width, 1
    )
    states = (
        (feed_in, moment_feed_in, square_feed_in)
        + (feed_out, moment_feed_out, square_feed_out)
        + (attend_in, moment_attend_in, square_attend_in)
        + (attend_out, moment_attend_out, square_attend_out)
    )
    matrix, output = (MATRIX_RATE, MATRIX_DECAY), (OUTPUT_RATE, MATRIX_DECAY)
    done = update_all(
        states, pieces, attend_in_shard, attend_out_shard, clip, side, (matrix, matrix, matrix, output)
    )
    third, fourth, first, second = done[:3], done[3:6], done[6:9], done[9:]
    fifth = adam(norm_gains, gain_shard, moment_gains, square_gains, clip, GAIN_RATE, 0.0)
    return (block_out, tokens_grad, grad_norm, *first, *second, *third, *fourth, *fifth)


def solution(mesh):
    depth, across = mesh.shape["dp"], mesh.shape["tensor"]
    tensor = tuple("t" + str(i) for i in range(across.bit_length() - 1))
    sizes = {"z": depth // 2, "x": 2, **{a: 2 for a in tensor}}
    assert depth % 2 == 0 and 2 ** len(tensor) == across
    fine = Mesh(mesh.devices.reshape(tuple(sizes.values())), tuple(sizes))
    dp = ("z", "x")
    both = P(dp + tensor, None)
    rows_cut, columns_cut = P(dp, tensor), P(tensor, dp)
    feed_cut, gain_cut = P(None, dp, tensor), P(None, dp)
    state = (rows_cut,) * 3 + (columns_cut,) * 3 + (feed_cut,) * 3 + (columns_cut,) * 3 + (gain_cut,) * 3
    return jax.shard_map(
        functools.partial(shards, sizes, tensor),
        mesh=fine,
        in_specs=(both, both, P(dp, None), rows_cut, columns_cut, feed_cut, columns_cut, gain_cut)
        + (rows_cut,) * 2
        + (columns_cut,) * 2
        + (feed_cut,) * 2
        + (columns_cut,) * 2
        + (gain_cut,) * 2,
        out_specs=(both, both, P()) + state,
        check_vma=False,
    )
```

```python
import functools
import math

import jax
import jax.numpy as jnp
from jax import lax
from jax.experimental import pallas as pl
from jax.experimental.pallas import tpu as pltpu
from jax.sharding import Mesh
from jax.sharding import PartitionSpec as P

H = 32
KV = 8
HD = 64
GROUP = H // KV
STEP = 10
LANES = 128
QUERY_ROWS = 256
UNITS = 4

EPSILON = 1e-05
NEGATIVE = -1e30
CLIP_LIMIT = 0.25
BETA_ONE = 0.9
BETA_TWO = 0.95
ADAM_EPSILON = 1e-08
MATRIX_RATE = 0.04
OUTPUT_RATE = 0.3
MATRIX_DECAY = 0.1
GAIN_RATE = 0.6

BF16 = jnp.bfloat16
F32 = jnp.float32


def flip(value, axes, sizes):
    count = math.prod(sizes[a] for a in axes)
    pairs = [(i, i ^ (count - 1)) for i in range(count)]
    return lax.ppermute(value, tuple(axes), pairs)


def combos(axes):
    return [
        tuple(a for i, a in enumerate(axes) if place >> (len(axes) - 1 - i) & 1)
        for place in range(2 ** len(axes))
    ]


def add_kernel(mine_ref, near_ref, *out_refs):
    for k, ref in enumerate(out_refs):

        @pl.when(pl.program_id(0) == k)
        def _():
            ref[...] = (mine_ref[...].astype(F32) + near_ref[...].astype(F32)).astype(BF16)


def add_blocks(mine, near, count):
    rows, width = mine.shape[0] // count, mine.shape[1]
    cut = pl.BlockSpec((rows, width), lambda i: (i, 0))
    return pl.pallas_call(
        add_kernel,
        grid=(count,),
        in_specs=[cut, cut],
        out_specs=[pl.BlockSpec((rows, width), lambda i: (0, 0))] * count,
        out_shape=[jax.ShapeDtypeStruct((rows, width), BF16)] * count,
        compiler_params=pltpu.CompilerParams(vmem_limit_bytes=32 * 2**20),
        cost_estimate=pl.CostEstimate(flops=1, bytes_accessed=1, transcendentals=0),
        name="add_blocks",
    )(mine, near)


def collect(mine, near, links, core, sizes):
    places = combos(links)
    blocks = add_blocks(mine, flip(near, (core,), sizes), len(places))
    return blocks[0], [flip(block, c, sizes) for block, c in zip(blocks[1:], places[1:])]


def added(own, moved):
    return sum((block.astype(F32) for block in moved), own.astype(F32))


def gather_depth(block, sizes):
    copies = jnp.broadcast_to(block, (sizes["z"],) + block.shape)
    return lax.all_to_all(copies, "z", 0, 0, tiled=True)


def sum_near(value, tensor, sizes):
    for a in ("x",) + tuple(reversed(tensor)):
        value = value + flip(value, (a,), sizes)
    return value


def sum_far(value, sizes):
    step, count = 1, sizes["z"]
    while step < count:
        value = value + lax.ppermute(value, "z", [(i, i ^ step) for i in range(count)])
        step *= 2
    return value


def sum_scalar(value, axes, sizes):
    count = math.prod(sizes[a] for a in axes)
    terms = lax.all_to_all(jnp.full((count, LANES), value), axes, 0, 0, tiled=True)
    return jnp.sum(terms[:, 0])


def frequencies(head_size):
    half_index = jnp.arange(head_size // 2, dtype=F32)
    inverse = jnp.power(500000.0, -2.0 * half_index / head_size)
    wavelength = 2.0 * math.pi / inverse
    smooth = (8192.0 / wavelength - 1.0) / 3.0
    blended = (1.0 - smooth) * inverse / 32.0 + smooth * inverse
    return jnp.where(
        wavelength < 2048.0, inverse, jnp.where(wavelength > 8192.0, inverse / 32.0, blended)
    )


def rotation_tables(lengths_row, rows):
    token_ids = jnp.arange(rows, dtype=jnp.int32)
    ends = jnp.cumsum(lengths_row)
    past = (token_ids[:, None] >= ends[None, :]).astype(jnp.int32)
    positions = token_ids - jnp.sum(past * lengths_row[None, :], axis=1)
    angles = positions.astype(F32)[:, None] * frequencies(HD)[None, :]
    cosine, sine = jnp.cos(angles), jnp.sin(angles)
    return (
        jnp.concatenate([cosine] * 4, axis=1),
        jnp.concatenate([-sine, sine, -sine, sine], axis=1),
    )


def exchange_halves(tile):
    lane = lax.broadcasted_iota(jnp.int32, tile.shape, 1)
    return jnp.where(
        lane % HD < HD // 2,
        pltpu.roll(tile, LANES - HD // 2, 1),
        pltpu.roll(tile, HD // 2, 1),
    )


def block_place(meta_ref, j, devices):
    relative = meta_ref[0] ^ j
    return (relative & 1) * (devices // 2) + (relative >> 1)


def allowed_bias(meta_ref, docs, first, keys, queries):
    token = lax.broadcasted_iota(jnp.int32, (1, queries), 1) + first
    start = jnp.zeros((1, queries), jnp.int32)
    for j in range(docs - 1):
        start = jnp.where(token >= meta_ref[1 + j], meta_ref[1 + j], start)
    other = lax.broadcasted_iota(jnp.int32, (keys, queries), 0)
    return jnp.where((other <= token) & (other >= start), 0.0, NEGATIVE)


def last_dims(left, right):
    return lax.dot_general(left, right, (((1,), (1,)), ((), ())), preferred_element_type=F32)


def key_halves(qkv_ref, keep_keys, keep_values, keep_turned):
    tile = qkv_ref[:, 2 * LANES : 3 * LANES].astype(F32)
    lane = lax.broadcasted_iota(jnp.int32, tile.shape, 1)
    low = jnp.where(lane < HD, tile, 0.0)
    high = jnp.where(lane < HD, 0.0, tile)
    pairs = ((low, pltpu.roll(low, HD, 1)), (pltpu.roll(high, HD, 1), high))
    for half in range(2):
        if keep_keys is not None:
            keep_keys[half] = pairs[0][half].astype(BF16)
        if keep_values is not None:
            keep_values[half] = pairs[1][half].astype(BF16)
        if keep_turned is not None:
            source, ref = keep_turned
            ref[half] = pairs[source][half].T.astype(BF16)


def forward_kernel(docs, devices, meta_ref, joined_ref, cos_ref, sin_ref, attended_ref, qkv_ref, log_ref, keys_ref, turned_ref):
    rows = joined_ref.shape[0]
    block = rows // devices
    for j in range(devices):
        source = pl.multiple_of(block_place(meta_ref, j, devices) * block, block)
        here = slice(j * block, (j + 1) * block)
        cosine, sine = cos_ref[here, :], sin_ref[here, :]
        lane = lax.broadcasted_iota(jnp.int32, cosine.shape, 1)
        for t in range(3):
            tile = joined_ref[pl.ds(source, block), t * LANES : (t + 1) * LANES]
            turned = tile * cosine + exchange_halves(tile) * sine
            if t == 2:
                turned = jnp.where(lane < HD, turned, tile)
            qkv_ref[here, t * LANES : (t + 1) * LANES] = turned.astype(BF16)
    key_halves(qkv_ref, keys_ref, None, (1, turned_ref))
    for i in range(rows // QUERY_ROWS):
        keys = (i + 1) * QUERY_ROWS
        here = slice(i * QUERY_ROWS, keys)
        bias = allowed_bias(meta_ref, docs, i * QUERY_ROWS, keys, QUERY_ROWS)
        for t in range(2):
            query = qkv_ref[here, t * LANES : (t + 1) * LANES] * BF16(HD**-0.5)
            total = jnp.zeros((LANES, QUERY_ROWS), F32)
            for half in range(2):
                scores = last_dims(keys_ref[half, :keys, :], query) + bias
                peak = jnp.max(scores, axis=0, keepdims=True)
                raised = jnp.exp(scores - peak)
                mass = jnp.sum(raised, axis=0, keepdims=True)
                probs = (raised * (1.0 / mass)).astype(BF16)
                total = total + jnp.dot(
                    turned_ref[half, :, :keys], probs, preferred_element_type=F32
                )
                head = 2 * t + half
                log_ref[0, head : head + 1, here] = peak + jnp.log(mass)
            done = total.T.astype(BF16)
            step = min(block, QUERY_ROWS)
            for part in range(QUERY_ROWS // step):
                first = i * QUERY_ROWS + part * step
                place = block_place(meta_ref, first // block, devices) * block + first % block
                attended_ref[
                    pl.ds(pl.multiple_of(place, step), step), t * LANES : (t + 1) * LANES
                ] = done[part * step : (part + 1) * step, :]


def backward_kernel(docs, devices, meta_ref, qkv_ref, log_ref, back_ref, cos_ref, sin_ref, grad_ref, keys_ref, values_ref, turned_ref, key_total, value_total, query_total, back_here):
    rows = qkv_ref.shape[0]
    block = rows // devices
    key_halves(qkv_ref, keys_ref, values_ref, (0, turned_ref))
    for j in range(devices):
        source = pl.multiple_of(block_place(meta_ref, j, devices) * block, block)
        back_here[j * block : (j + 1) * block, :] = back_ref[pl.ds(source, block), :]
    key_total[...] = jnp.zeros_like(key_total)
    value_total[...] = jnp.zeros_like(value_total)
    for i in range(rows // QUERY_ROWS):
        keys = (i + 1) * QUERY_ROWS
        here = slice(i * QUERY_ROWS, keys)
        bias = allowed_bias(meta_ref, docs, i * QUERY_ROWS, keys, QUERY_ROWS)
        lane = lax.broadcasted_iota(jnp.int32, (QUERY_ROWS, LANES), 1)
        for t in range(2):
            columns = slice(t * LANES, (t + 1) * LANES)
            query = qkv_ref[here, columns] * BF16(HD**-0.5)
            back = back_here[here, columns]
            total = jnp.zeros((LANES, QUERY_ROWS), F32)
            for half in range(2):
                head = 2 * t + half
                mine = (lane < HD) if half == 0 else (lane >= HD)
                scores = last_dims(keys_ref[half, :keys, :], query) + bias
                probs = jnp.exp(scores - log_ref[0, head : head + 1, here])
                moved = last_dims(values_ref[half, :keys, :], back)
                inner = jnp.sum(probs * moved, axis=0, keepdims=True)
                grad = (probs * (moved - inner)).astype(BF16)
                total = total + jnp.dot(
                    turned_ref[half, :, :keys], grad, preferred_element_type=F32
                )
                key_total[:keys, :] += jnp.dot(
                    grad, jnp.where(mine, query, BF16(0)), preferred_element_type=F32
                )
                value_total[:keys, :] += jnp.dot(
                    probs.astype(BF16), jnp.where(mine, back, BF16(0)), preferred_element_type=F32
                )
            query_total[here, columns] = total.T * HD**-0.5
    for j in range(devices):
        place = pl.multiple_of(block_place(meta_ref, j, devices) * block, block)
        here = slice(j * block, (j + 1) * block)
        cosine, sine = cos_ref[here, :], sin_ref[here, :]
        lane = lax.broadcasted_iota(jnp.int32, cosine.shape, 1)
        for t in range(2):
            columns = slice(t * LANES, (t + 1) * LANES)
            tile = query_total[here, columns]
            grad_ref[pl.ds(place, block), columns] = (
                tile * cosine - exchange_halves(tile) * sine
            ).astype(BF16)
        tile = key_total[here, :]
        tile = tile + pltpu.roll(tile, HD, 1)
        other = value_total[here, :]
        other = other + pltpu.roll(other, HD, 1)
        tile = jnp.where(lane < HD, tile * cosine - exchange_halves(tile) * sine, other)
        grad_ref[pl.ds(place, block), 2 * LANES : 3 * LANES] = tile.astype(BF16)


def attend_forward(meta, joined, cosine, sine, docs, devices):
    rows, width = joined.shape
    wide = (GROUP + 2) * HD
    groups = width // wide
    whole = pl.BlockSpec((rows, LANES), lambda g: (0, 0))
    return pl.pallas_call(
        functools.partial(forward_kernel, docs, devices),
        grid=(groups,),
        in_specs=[
            pl.BlockSpec(memory_space=pltpu.SMEM),
            pl.BlockSpec((rows, wide), lambda g: (0, g)),
            whole,
            whole,
        ],
        out_specs=[
            pl.BlockSpec((rows, GROUP * HD), lambda g: (0, g)),
            pl.BlockSpec((rows, wide), lambda g: (0, g)),
            pl.BlockSpec((1, 8, rows), lambda g: (g, 0, 0)),
        ],
        out_shape=[
            jax.ShapeDtypeStruct((rows, groups * GROUP * HD), BF16),
            jax.ShapeDtypeStruct((rows, width), BF16),
            jax.ShapeDtypeStruct((groups, 8, rows), F32),
        ],
        scratch_shapes=[
            pltpu.VMEM((2, rows, LANES), BF16),
            pltpu.VMEM((2, LANES, rows), BF16),
        ],
        compiler_params=pltpu.CompilerParams(vmem_limit_bytes=32 * 2**20),
        cost_estimate=pl.CostEstimate(flops=1, bytes_accessed=1, transcendentals=0),
        name="attend_forward",
    )(meta, joined, cosine, sine)


def attend_backward(meta, qkv, logs, back, cosine, sine, docs, devices, group):
    rows = qkv.shape[0]
    wide = (GROUP + 2) * HD
    whole = pl.BlockSpec((rows, LANES), lambda g: (0, 0))
    return pl.pallas_call(
        functools.partial(backward_kernel, docs, devices),
        grid=(1,),
        in_specs=[
            pl.BlockSpec(memory_space=pltpu.SMEM),
            pl.BlockSpec((rows, wide), lambda g: (0, group)),
            pl.BlockSpec((1, 8, rows), lambda g: (group, 0, 0)),
            pl.BlockSpec((rows, GROUP * HD), lambda g: (0, group)),
            whole,
            whole,
        ],
        out_specs=pl.BlockSpec((rows, wide), lambda g: (0, 0)),
        out_shape=jax.ShapeDtypeStruct((rows, wide), BF16),
        scratch_shapes=[
            pltpu.VMEM((2, rows, LANES), BF16),
            pltpu.VMEM((2, rows, LANES), BF16),
            pltpu.VMEM((2, LANES, rows), BF16),
            pltpu.VMEM((rows, LANES), F32),
            pltpu.VMEM((rows, LANES), F32),
            pltpu.VMEM((rows, GROUP * HD), F32),
            pltpu.VMEM((rows, GROUP * HD), BF16),
        ],
        compiler_params=pltpu.CompilerParams(vmem_limit_bytes=32 * 2**20),
        cost_estimate=pl.CostEstimate(flops=1, bytes_accessed=1, transcendentals=0),
        name="attend_backward",
    )(meta, qkv, logs, back, cosine, sine)


def product(left, right, left_dim, right_dim):
    return lax.dot_general(
        left, right, (((left_dim,), (right_dim,)), ((), ())), preferred_element_type=F32
    )


def norm_rate(vector):
    return lax.rsqrt(jnp.mean(vector * vector, axis=-1, keepdims=True) + EPSILON)


def norm_back(vector, rate, gain, grad):
    scaled = gain * grad
    inner = jnp.mean(vector * scaled, axis=-1, keepdims=True)
    return (
        rate * scaled - vector * (rate * rate * rate * inner),
        jnp.sum(grad * vector * rate, axis=0),
    )


def adam(weight, grad, moment, square, clip, rate, decay):
    clipped = clip * grad
    moment_new = BETA_ONE * moment + (1.0 - BETA_ONE) * clipped
    square_new = BETA_TWO * square + (1.0 - BETA_TWO) * clipped * clipped
    direction = (
        moment_new
        / (1.0 - BETA_ONE**STEP)
        / (jnp.sqrt(square_new / (1.0 - BETA_TWO**STEP)) + ADAM_EPSILON)
    )
    return (weight - rate * (direction + decay * weight), moment_new, square_new)


def adam_all_kernel(rates, side_ref, clip_ref, *refs):
    side, clip = side_ref[0], clip_ref[0]
    pieces_ref, turned_ref, in_grad_ref, out_grad_ref = refs[:4]
    states, outs = refs[4:16], refs[16:]

    def apply(k, grad, at):
        weight, moment, square = [ref[at] for ref in states[3 * k : 3 * k + 3]]
        done = adam(weight, grad.astype(F32), moment, square, clip, *rates[k])
        for ref, value in zip(outs[3 * k : 3 * k + 3], done):
            ref[at] = value

    columns = states[0].shape[-1]
    unit = columns // (2 * UNITS)
    per_half = UNITS // 2
    for n in range(2 * UNITS):
        which, half, place = n // UNITS, n % UNITS // per_half, n % per_half
        for j in range(2):
            first = (2 * place + j) * unit
            grad = pieces_ref[which ^ side, half, :, first : first + unit]
            apply(0, grad, (j, slice(None), slice(n * unit, (n + 1) * unit)))
    apply(1, turned_ref[0, 0].astype(F32).T, (slice(None), slice(None)))
    apply(2, in_grad_ref[...], (slice(None), slice(None)))
    apply(3, out_grad_ref[...], (slice(None), slice(None)))


def update_all(states, pieces, in_grad, out_grad, clip, side, rates):
    steps = 2 * UNITS
    depth, slim = pieces.shape[2], pieces.shape[3] // 3
    unit = 2 * slim // UNITS

    def rows(array):
        lead = array.shape[:-2]
        block = lead + (array.shape[-2] // steps, array.shape[-1])
        return pl.BlockSpec(block, lambda i, s: (0,) * len(lead) + (i, 0))

    specs = [rows(a) for a in states]
    grid_spec = pltpu.PrefetchScalarGridSpec(
        num_scalar_prefetch=1,
        grid=(steps,),
        in_specs=[
            pl.BlockSpec(memory_space=pltpu.SMEM),
            pl.BlockSpec((2, 2, depth // steps, 2 * slim), lambda i, s: (0, 0, i, 0)),
            pl.BlockSpec(
                (1, 1, depth, unit),
                lambda i, s: ((i // UNITS) ^ s[0], i % UNITS // 2, 0, UNITS + i % 2),
            ),
            rows(in_grad),
            rows(out_grad),
        ]
        + specs,
        out_specs=specs,
    )
    return pl.pallas_call(
        functools.partial(adam_all_kernel, rates),
        grid_spec=grid_spec,
        out_shape=[jax.ShapeDtypeStruct(a.shape, F32) for a in states],
        compiler_params=pltpu.CompilerParams(vmem_limit_bytes=60 * 2**20),
        cost_estimate=pl.CostEstimate(flops=1, bytes_accessed=1, transcendentals=0),
        name="update_all",
    )(
        side.reshape(1).astype(jnp.int32),
        clip.reshape(1),
        pieces,
        pieces,
        in_grad,
        out_grad,
        *states,
    )


def split_kernel(unit, side_ref, in_ref, out_ref, *part_refs):
    slim = part_refs[0].shape[1] // 3
    for part, ref in enumerate(part_refs):
        for n in range(slim // unit):
            cut = slice(part * slim + n * unit, part * slim + (n + 1) * unit)
            for j in range(2):
                first = (2 * n + j) * unit
                ref[:, first : first + unit] = in_ref[j, :, cut].astype(BF16)
        ref[:, 2 * slim :] = out_ref[part * slim : (part + 1) * slim, :].T.astype(BF16)


def split_feed(feed_in, feed_out, side, unit):
    depth, hidden = feed_in.shape[1], feed_in.shape[2] // 2
    part = jax.ShapeDtypeStruct((depth, 3 * hidden // 2), BF16)
    grid_spec = pltpu.PrefetchScalarGridSpec(
        num_scalar_prefetch=1,
        grid=(1,),
        in_specs=[
            pl.BlockSpec((2, depth, hidden), lambda i, s: (0, 0, s[0])),
            pl.BlockSpec((hidden, depth), lambda i, s: (s[0], 0)),
        ],
        out_specs=[pl.BlockSpec(part.shape, lambda i, s: (0, 0))] * 2,
    )
    return pl.pallas_call(
        functools.partial(split_kernel, unit),
        grid_spec=grid_spec,
        out_shape=[part] * 2,
        compiler_params=pltpu.CompilerParams(vmem_limit_bytes=60 * 2**20),
        cost_estimate=pl.CostEstimate(flops=1, bytes_accessed=1, transcendentals=0),
        name="split_feed",
    )(side.reshape(1).astype(jnp.int32), feed_in, feed_out)


def feed_kernel(unit, rows_ref, back_ref, weight_ref, activated_ref, grad_ref):
    units = activated_ref.shape[1] // unit
    for n in range(units):
        first = 2 * n * unit
        both = jnp.dot(
            rows_ref[...], weight_ref[:, first : first + 2 * unit], preferred_element_type=F32
        )
        first = (2 * units + n) * unit
        back = jnp.dot(
            back_ref[...], weight_ref[:, first : first + unit], preferred_element_type=F32
        )
        gate, upward = both[:, :unit], both[:, unit:]
        chance = jax.nn.sigmoid(gate)
        silu = gate * chance
        activated_ref[:, n * unit : (n + 1) * unit] = (silu * upward).astype(BF16)
        grad_ref[:, 2 * n * unit : (2 * n + 1) * unit] = (
            back * upward * (chance + silu * (1.0 - chance))
        ).astype(BF16)
        grad_ref[:, (2 * n + 1) * unit : 2 * (n + 1) * unit] = (back * silu).astype(BF16)


def feed_both_ways(rows, back, weight, unit):
    count, width = rows.shape
    slim = weight.shape[1] // 3
    tall = min(count, 512)
    return pl.pallas_call(
        functools.partial(feed_kernel, unit),
        grid=(count // tall,),
        in_specs=[
            pl.BlockSpec((tall, width), lambda i: (i, 0)),
            pl.BlockSpec((tall, width), lambda i: (i, 0)),
            pl.BlockSpec(weight.shape, lambda i: (0, 0)),
        ],
        out_specs=[
            pl.BlockSpec((tall, slim), lambda i: (i, 0)),
            pl.BlockSpec((tall, 2 * slim), lambda i: (i, 0)),
        ],
        out_shape=[
            jax.ShapeDtypeStruct((count, slim), BF16),
            jax.ShapeDtypeStruct((count, 2 * slim), BF16),
        ],
        compiler_params=pltpu.CompilerParams(vmem_limit_bytes=48 * 2**20),
        cost_estimate=pl.CostEstimate(flops=1, bytes_accessed=1, transcendentals=0),
        name="feed_both_ways",
    )(rows, back, weight)


def weights_kernel(scale, rows_ref, grad_ref, back_ref, activated_ref, out_ref):
    wide = grad_ref.shape[1]
    out_ref[0, :, :wide] = (product(rows_ref[...], grad_ref[...], 0, 0) * scale).astype(BF16)
    out_ref[0, :, wide:] = (product(back_ref[...], activated_ref[...], 0, 0) * scale).astype(BF16)


def weight_gradients(rows, grad, back, activated, parts, scale):
    count, width = rows.shape
    cut, slim = width // parts, activated.shape[1]
    return pl.pallas_call(
        functools.partial(weights_kernel, scale),
        grid=(parts,),
        in_specs=[
            pl.BlockSpec((count, cut), lambda i: (0, i)),
            pl.BlockSpec(grad.shape, lambda i: (0, 0)),
            pl.BlockSpec((count, cut), lambda i: (0, i)),
            pl.BlockSpec(activated.shape, lambda i: (0, 0)),
        ],
        out_specs=pl.BlockSpec((1, cut, 3 * slim), lambda i: (i, 0, 0)),
        out_shape=jax.ShapeDtypeStruct((parts, cut, 3 * slim), BF16),
        compiler_params=pltpu.CompilerParams(vmem_limit_bytes=48 * 2**20),
        cost_estimate=pl.CostEstimate(flops=1, bytes_accessed=1, transcendentals=0),
        name="weight_gradients",
    )(rows, grad, back, activated)


def back_kernel(*refs):
    total = 0.0
    for left, right in zip(refs[:-1:2], refs[1:-1:2]):
        total = total + product(left[...], right[...], 1, 1)
    refs[-1][...] = total.astype(BF16)


def back_products(pairs, first, last, half):
    count, width = pairs[0][0].shape[0] // 2, pairs[0][1].shape[0]
    tall = min(count, 512)
    skip, place = half * (count // tall), first // (last - first)
    specs, operands = [], []
    for left, right in pairs:
        depth = left.shape[1]
        specs.append(pl.BlockSpec((tall, depth), lambda i: (i + skip, 0)))
        specs.append(pl.BlockSpec((width, depth), lambda i: (0, place)))
        operands += [left, right]
    depth = sum(left.shape[1] for left, _ in pairs)
    return pl.pallas_call(
        back_kernel,
        grid=(count // tall,),
        in_specs=specs,
        out_specs=pl.BlockSpec((tall, width), lambda i: (i, 0)),
        out_shape=jax.ShapeDtypeStruct((count, width), BF16),
        compiler_params=pltpu.CompilerParams(vmem_limit_bytes=56 * 2**20),
        cost_estimate=pl.CostEstimate(flops=1, bytes_accessed=1, transcendentals=0),
        name="back_products",
    )(*operands)


def in_order(mine, other, first, axis):
    return jnp.where(
        first,
        jnp.concatenate([mine, other], axis=axis),
        jnp.concatenate([other, mine], axis=axis),
    )


def shards(
    sizes,
    tensor,
    tokens,
    cotangent,
    doc_lengths,
    attend_in,
    attend_out,
    feed_in,
    feed_out,
    norm_gains,
    moment_attend_in,
    square_attend_in,
    moment_attend_out,
    square_attend_out,
    moment_feed_in,
    square_feed_in,
    moment_feed_out,
    square_feed_out,
    moment_gains,
    square_gains,
):
    pack_links, core = tensor[:-1], tensor[-1]
    feed_links = ("x",) + tuple(pack_links)
    devices = math.prod(sizes[a] for a in tensor)
    side = lax.axis_index("x")
    is_first = side == 0
    local_rows, width = tokens.shape
    rows = local_rows * devices
    token_total = rows * 2 * sizes["z"]
    inverse_total = 1.0 / token_total
    docs = doc_lengths.shape[1]
    meta = jnp.concatenate(
        [lax.axis_index(tuple(tensor))[None].astype(jnp.int32), jnp.cumsum(doc_lengths[0])]
    )
    cosine, sine = rotation_tables(doc_lengths[0], rows)

    hidden = feed_in.shape[2] // 2
    slim = hidden // 2
    unit = hidden // UNITS
    depth = attend_in.shape[0]
    half = rows // 2

    def halves(array, axis):
        size = array.shape[axis] // 2
        mine = lax.dynamic_slice_in_dim(array, side * size, size, axis)
        other = lax.dynamic_slice_in_dim(array, (1 - side) * size, size, axis)
        return mine, other

    def sends(block, links):
        return [flip(block, c, sizes) for c in combos(links)[1:]]

    def over_core(blocks):
        mine = jnp.concatenate(blocks, axis=0)
        return jnp.concatenate([mine, flip(mine, (core,), sizes)], axis=0)

    def both_sides(mine, other):
        pair = jnp.where(
            is_first, jnp.stack([mine, other], axis=1), jnp.stack([other, mine], axis=1)
        )
        return pair

    gain_rows = jnp.pad(
        norm_gains.astype(BF16), ((0, 14), (0, attend_in.shape[1] - norm_gains.shape[1]))
    )
    in_z = lax.all_gather(
        jnp.concatenate([attend_in.astype(BF16), gain_rows], axis=0), "z", axis=0, tiled=False
    )
    out_z = gather_depth(attend_out.T.astype(BF16), sizes)
    tokens_moved = sends(tokens, pack_links)
    away = split_feed(feed_in, feed_out, 1 - side, unit)
    moved = [flip(part, ("x",), sizes) for part in away]
    kept = split_feed(feed_in, feed_out, side, unit)
    locals_ = [in_order(part, other, is_first, 0) for part, other in zip(kept, moved)]
    in_z, out_z, cotangent_then, tokens_moved, locals_ = lax.optimization_barrier(
        (in_z, out_z, cotangent, tokens_moved, locals_)
    )

    weight_a, weight_b = [lax.all_gather(part, "z", axis=0, tiled=True) for part in locals_]
    in_x = flip(in_z, ("x",), sizes)
    back_moved = sends(cotangent_then, pack_links)
    tokens_all = over_core([tokens] + tokens_moved)
    in_x, back_moved, tokens_all = lax.optimization_barrier((in_x, back_moved, tokens_all))

    out_x = flip(out_z, ("x",), sizes)
    in_both = both_sides(in_z, in_x)
    full_in = in_both[:, :, :depth].reshape(width, attend_in.shape[1])
    gains = (
        in_both[:, :, depth : depth + 2, : norm_gains.shape[1]]
        .astype(F32)
        .transpose(2, 0, 1, 3)
        .reshape(2, width)
    )
    inputs_all = tokens_all.astype(F32)
    normed_one = (inputs_all * norm_rate(inputs_all) * gains[0]).astype(BF16)
    joined = product(normed_one, full_in, 1, 0)
    attended, qkv, logs = attend_forward(meta, joined, cosine, sine, docs, devices)
    back_near = jnp.concatenate([cotangent] + back_moved, axis=0)
    attended, out_x, left, right = lax.optimization_barrier(
        (attended, out_x, back_near[:, : width // 2], back_near[:, width // 2 :])
    )

    full_out = both_sides(out_z, out_x).reshape(width, attend_out.shape[0])
    near = product(attended[half:], full_out, 1, 1).astype(BF16)
    mine = product(attended[:half], full_out, 1, 1).astype(BF16)
    own, moved = collect(mine, near, pack_links, core, sizes)
    left = flip(left, ("x",), sizes)
    right = flip(right, ("x",), sizes)
    own, moved, left, right = lax.optimization_barrier((own, moved, left, right))

    inputs = tokens.astype(F32)
    hidden_state = inputs + added(own, moved)
    rate_two = norm_rate(hidden_state)
    normed_two = (hidden_state * rate_two * gains[1]).astype(BF16)
    normed_moved = sends(normed_two, feed_links)
    gathered_back = over_core([back_near, jnp.concatenate([left, right], axis=1)])
    normed_moved, gathered_back = lax.optimization_barrier((normed_moved, gathered_back))
    gathered_two = over_core([normed_two] + normed_moved)

    def gradients(grad, activated):
        return weight_gradients(
            gathered_two, grad, gathered_back, activated, sizes["z"], inverse_total
        )

    def summed(parts):
        return lax.psum_scatter(parts, "z", scatter_dimension=0, tiled=False)

    activated_a, grad_a = feed_both_ways(gathered_two, gathered_back, weight_a, unit)
    parts_a = gradients(grad_a, activated_a)
    parts_a, weight_b = lax.optimization_barrier((parts_a, weight_b))
    sums_a = summed(parts_a)
    activated_b, grad_b = feed_both_ways(gathered_two, gathered_back, weight_b, unit)
    pairs = [(grad_a, weight_a), (grad_b, weight_b)]
    near = flip(back_products(pairs, 0, 2, 1), (core,), sizes)
    mine = back_products(pairs, 0, 2, 0)
    blocks = add_blocks(mine, near, 2 ** len(feed_links))
    blocks, grad_b, activated_a, activated_b = lax.optimization_barrier(
        (blocks, grad_b, activated_a, activated_b)
    )
    moved = [flip(block, c, sizes) for block, c in zip(blocks[1:], combos(feed_links)[1:])]
    parts_b = gradients(grad_b, activated_b)
    sums_b = summed(parts_b)
    pairs = [(activated_a, weight_a), (activated_b, weight_b)]
    forward_near = back_products(pairs, 2, 3, 1)
    moved, parts_b, forward_near, activated_a, activated_b = lax.optimization_barrier(
        (moved, parts_b, forward_near, activated_a, activated_b)
    )

    grad_from_two, gain_two_grad = norm_back(
        hidden_state, rate_two, gains[1], added(blocks[0], moved)
    )
    grad_hidden = cotangent.astype(F32) + grad_from_two
    grad_branch = grad_hidden.astype(BF16)

    def regroup(sums):
        mine, other = halves(sums, 0)
        return jnp.stack([mine, flip(other, ("x",), sizes)])

    pairs = [(activated_a, weight_a), (activated_b, weight_b)]
    forward_mine = back_products(pairs, 2, 3, 0)
    forward_blocks = add_blocks(
        forward_mine, flip(forward_near, (core,), sizes), 2 ** len(feed_links)
    )
    sums_a, grad_branch = lax.optimization_barrier((sums_a, grad_branch))
    grad_moved = sends(grad_branch, pack_links)
    pieces_a = regroup(sums_a)
    grad_moved, forward_blocks, pieces_a = lax.optimization_barrier(
        (grad_moved, forward_blocks, pieces_a)
    )
    forward_links = combos(feed_links)[1:]
    forward_first = [
        flip(block, c, sizes)
        for block, c in zip(forward_blocks[1:], forward_links)
        if "x" not in c
    ]
    gathered_grad = over_core([grad_branch] + grad_moved)
    grad_attended = product(gathered_grad, full_out, 1, 0).astype(BF16)
    groups = attend_in.shape[1] // ((GROUP + 2) * HD)
    grad_joined = [
        attend_backward(meta, qkv, logs, grad_attended, cosine, sine, docs, devices, group)
        for group in range(groups)
    ]

    def split_sides(grad):
        split = (grad * inverse_total).astype(BF16).reshape(sizes["z"], 2, -1, grad.shape[1])
        mine = lax.dynamic_index_in_dim(split, side, 1, keepdims=False)
        other = lax.dynamic_index_in_dim(split, 1 - side, 1, keepdims=False)
        return mine, flip(other, ("x",), sizes)

    out_mine, out_other = split_sides(product(gathered_grad, attended, 0, 0))
    in_pairs = [split_sides(product(normed_one, grad, 0, 0)) for grad in grad_joined[:-1]]
    grad_joined[-1], out_other, forward_first, in_pairs = lax.optimization_barrier(
        (grad_joined[-1], out_other, forward_first, in_pairs)
    )
    out_sums = added(out_mine, [out_other]).astype(BF16)
    in_pairs.append(split_sides(product(normed_one, grad_joined[-1], 0, 0)))
    in_pairs, forward_blocks = lax.optimization_barrier((in_pairs, forward_blocks))
    in_parts = [added(mine, [other]).astype(BF16) for mine, other in in_pairs]
    attend_sums = summed(jnp.concatenate(in_parts + [out_sums], axis=2))
    joined_back = jnp.concatenate(grad_joined, axis=1)
    own, moved = collect(
        product(joined_back[:half], full_in, 1, 1).astype(BF16),
        product(joined_back[half:], full_in, 1, 1).astype(BF16),
        pack_links,
        core,
        sizes,
    )
    forward_x = flip(forward_blocks[forward_links.index(("x",)) + 1], ("x",), sizes)
    sums_b, forward_x, own, moved = lax.optimization_barrier((sums_b, forward_x, own, moved))
    pieces_b = regroup(sums_b)
    grad_normed_one = added(own, moved)
    grad_from_one, gain_one_grad = norm_back(inputs, norm_rate(inputs), gains[0], grad_normed_one)
    tokens_grad = (grad_hidden + grad_from_one).astype(BF16)

    gain_grads = sum_near(
        jnp.stack([gain_one_grad, gain_two_grad]) * inverse_total, tensor, sizes
    )
    def squares(shard):
        shard = shard.astype(F32)
        return jnp.sum(shard * shard)

    feed_squares = squares(sums_a) + squares(sums_b)
    attend_sums, gain_grads, tokens_grad, feed_squares = lax.optimization_barrier(
        (attend_sums, gain_grads, tokens_grad, feed_squares)
    )
    gain_grads = sum_far(gain_grads, sizes)
    attend_in_shard = attend_sums[:, : attend_in.shape[1]]
    attend_out_shard = attend_sums[:, attend_in.shape[1] :].T
    pieces = jnp.stack([pieces_a, pieces_b], axis=1)

    matrix_squares = feed_squares + squares(attend_sums)
    total_squares = sum_scalar(matrix_squares, ("z", "x") + tuple(tensor), sizes)
    grad_norm = jnp.sqrt(total_squares + jnp.sum(gain_grads * gain_grads))
    clip = jnp.minimum(1.0, CLIP_LIMIT / (grad_norm + 1e-06))
    clip, forward_blocks = lax.optimization_barrier((clip, forward_blocks))
    forward_last = [
        flip(block, c, sizes)
        for block, c in zip(forward_blocks[1:], forward_links)
        if "x" in c and len(c) > 1
    ]
    block_out = added(forward_blocks[0], forward_first + [forward_x] + forward_last)
    block_out = (hidden_state + block_out).astype(BF16)
    gain_width = norm_gains.shape[1]
    gain_shard = lax.dynamic_slice_in_dim(
        gain_grads, lax.axis_index(("z", "x")) * gain_width, gain_width, 1
    )
    states = (
        (feed_in, moment_feed_in, square_feed_in)
        + (feed_out, moment_feed_out, square_feed_out)
        + (attend_in, moment_attend_in, square_attend_in)
        + (attend_out, moment_attend_out, square_attend_out)
    )
    matrix, output = (MATRIX_RATE, MATRIX_DECAY), (OUTPUT_RATE, MATRIX_DECAY)
    done = update_all(
        states, pieces, attend_in_shard, attend_out_shard, clip, side, (matrix, matrix, matrix, output)
    )
    third, fourth, first, second = done[:3], done[3:6], done[6:9], done[9:]
    fifth = adam(norm_gains, gain_shard, moment_gains, square_gains, clip, GAIN_RATE, 0.0)
    return (block_out, tokens_grad, grad_norm, *first, *second, *third, *fourth, *fifth)


def solution(mesh):
    depth, across = mesh.shape["dp"], mesh.shape["tensor"]
    tensor = tuple("t" + str(i) for i in range(across.bit_length() - 1))
    sizes = {"z": depth // 2, "x": 2, **{a: 2 for a in tensor}}
    assert depth % 2 == 0 and 2 ** len(tensor) == across
    fine = Mesh(mesh.devices.reshape(tuple(sizes.values())), tuple(sizes))
    dp = ("z", "x")
    both = P(dp + tensor, None)
    rows_cut, columns_cut = P(dp, tensor), P(tensor, dp)
    feed_cut, gain_cut = P(None, dp, tensor), P(None, dp)
    state = (rows_cut,) * 3 + (columns_cut,) * 3 + (feed_cut,) * 3 + (columns_cut,) * 3 + (gain_cut,) * 3
    return jax.shard_map(
        functools.partial(shards, sizes, tensor),
        mesh=fine,
        in_specs=(both, both, P(dp, None), rows_cut, columns_cut, feed_cut, columns_cut, gain_cut)
        + (rows_cut,) * 2
        + (columns_cut,) * 2
        + (feed_cut,) * 2
        + (columns_cut,) * 2
        + (gain_cut,) * 2,
        out_specs=(both, both, P()) + state,
        check_vma=False,
    )
```

```python
import functools
import math

import jax
import jax.numpy as jnp
from jax import lax
from jax.experimental import pallas as pl
from jax.experimental.pallas import tpu as pltpu
from jax.sharding import Mesh
from jax.sharding import PartitionSpec as P

H = 32
KV = 8
HD = 64
GROUP = H // KV
STEP = 10
LANES = 128
QUERY_ROWS = 256
UNITS = 4

EPSILON = 1e-05
NEGATIVE = -1e30
CLIP_LIMIT = 0.25
BETA_ONE = 0.9
BETA_TWO = 0.95
ADAM_EPSILON = 1e-08
MATRIX_RATE = 0.04
OUTPUT_RATE = 0.3
MATRIX_DECAY = 0.1
GAIN_RATE = 0.6

BF16 = jnp.bfloat16
F32 = jnp.float32


def flip(value, axes, sizes):
    count = math.prod(sizes[a] for a in axes)
    pairs = [(i, i ^ (count - 1)) for i in range(count)]
    return lax.ppermute(value, tuple(axes), pairs)


def combos(axes):
    return [
        tuple(a for i, a in enumerate(axes) if place >> (len(axes) - 1 - i) & 1)
        for place in range(2 ** len(axes))
    ]


def add_kernel(mine_ref, near_ref, *out_refs):
    for k, ref in enumerate(out_refs):

        @pl.when(pl.program_id(0) == k)
        def _():
            ref[...] = (mine_ref[...].astype(F32) + near_ref[...].astype(F32)).astype(BF16)


def add_blocks(mine, near, count):
    rows, width = mine.shape[0] // count, mine.shape[1]
    cut = pl.BlockSpec((rows, width), lambda i: (i, 0))
    return pl.pallas_call(
        add_kernel,
        grid=(count,),
        in_specs=[cut, cut],
        out_specs=[pl.BlockSpec((rows, width), lambda i: (0, 0))] * count,
        out_shape=[jax.ShapeDtypeStruct((rows, width), BF16)] * count,
        compiler_params=pltpu.CompilerParams(vmem_limit_bytes=32 * 2**20),
        cost_estimate=pl.CostEstimate(flops=1, bytes_accessed=1, transcendentals=0),
        name="add_blocks",
    )(mine, near)


def collect(mine, near, links, core, sizes):
    places = combos(links)
    blocks = add_blocks(mine, flip(near, (core,), sizes), len(places))
    return blocks[0], [flip(block, c, sizes) for block, c in zip(blocks[1:], places[1:])]


def added(own, moved):
    return sum((block.astype(F32) for block in moved), own.astype(F32))


def gather_depth(block, sizes):
    copies = jnp.broadcast_to(block, (sizes["z"],) + block.shape)
    return lax.all_to_all(copies, "z", 0, 0, tiled=True)


def sum_near(value, tensor, sizes):
    for a in ("x",) + tuple(reversed(tensor)):
        value = value + flip(value, (a,), sizes)
    return value


def sum_far(value, sizes):
    step, count = 1, sizes["z"]
    while step < count:
        value = value + lax.ppermute(value, "z", [(i, i ^ step) for i in range(count)])
        step *= 2
    return value


def sum_scalar(value, axes, sizes):
    count = math.prod(sizes[a] for a in axes)
    terms = lax.all_to_all(jnp.full((count, LANES), value), axes, 0, 0, tiled=True)
    return jnp.sum(terms[:, 0])


def frequencies(head_size):
    half_index = jnp.arange(head_size // 2, dtype=F32)
    inverse = jnp.power(500000.0, -2.0 * half_index / head_size)
    wavelength = 2.0 * math.pi / inverse
    smooth = (8192.0 / wavelength - 1.0) / 3.0
    blended = (1.0 - smooth) * inverse / 32.0 + smooth * inverse
    return jnp.where(
        wavelength < 2048.0, inverse, jnp.where(wavelength > 8192.0, inverse / 32.0, blended)
    )


def rotation_tables(lengths_row, rows):
    token_ids = jnp.arange(rows, dtype=jnp.int32)
    ends = jnp.cumsum(lengths_row)
    past = (token_ids[:, None] >= ends[None, :]).astype(jnp.int32)
    positions = token_ids - jnp.sum(past * lengths_row[None, :], axis=1)
    angles = positions.astype(F32)[:, None] * frequencies(HD)[None, :]
    cosine, sine = jnp.cos(angles), jnp.sin(angles)
    return (
        jnp.concatenate([cosine] * 4, axis=1),
        jnp.concatenate([-sine, sine, -sine, sine], axis=1),
    )


def exchange_halves(tile):
    lane = lax.broadcasted_iota(jnp.int32, tile.shape, 1)
    return jnp.where(
        lane % HD < HD // 2,
        pltpu.roll(tile, LANES - HD // 2, 1),
        pltpu.roll(tile, HD // 2, 1),
    )


def block_place(meta_ref, j, devices):
    relative = meta_ref[0] ^ j
    return (relative & 1) * (devices // 2) + (relative >> 1)


def allowed_bias(meta_ref, docs, first, keys, queries):
    token = lax.broadcasted_iota(jnp.int32, (1, queries), 1) + first
    start = jnp.zeros((1, queries), jnp.int32)
    for j in range(docs - 1):
        start = jnp.where(token >= meta_ref[1 + j], meta_ref[1 + j], start)
    other = lax.broadcasted_iota(jnp.int32, (keys, queries), 0)
    return jnp.where((other <= token) & (other >= start), 0.0, NEGATIVE)


def last_dims(left, right):
    return lax.dot_general(left, right, (((1,), (1,)), ((), ())), preferred_element_type=F32)


def key_halves(qkv_ref, keep_keys, keep_values, keep_turned):
    tile = qkv_ref[:, 2 * LANES : 3 * LANES].astype(F32)
    lane = lax.broadcasted_iota(jnp.int32, tile.shape, 1)
    low = jnp.where(lane < HD, tile, 0.0)
    high = jnp.where(lane < HD, 0.0, tile)
    pairs = ((low, pltpu.roll(low, HD, 1)), (pltpu.roll(high, HD, 1), high))
    for half in range(2):
        if keep_keys is not None:
            keep_keys[half] = pairs[0][half].astype(BF16)
        if keep_values is not None:
            keep_values[half] = pairs[1][half].astype(BF16)
        if keep_turned is not None:
            source, ref = keep_turned
            ref[half] = pairs[source][half].T.astype(BF16)


def forward_kernel(docs, devices, meta_ref, joined_ref, cos_ref, sin_ref, attended_ref, qkv_ref, log_ref, keys_ref, turned_ref):
    rows = joined_ref.shape[0]
    block = rows // devices
    for j in range(devices):
        source = pl.multiple_of(block_place(meta_ref, j, devices) * block, block)
        here = slice(j * block, (j + 1) * block)
        cosine, sine = cos_ref[here, :], sin_ref[here, :]
        lane = lax.broadcasted_iota(jnp.int32, cosine.shape, 1)
        for t in range(3):
            tile = joined_ref[pl.ds(source, block), t * LANES : (t + 1) * LANES]
            turned = tile * cosine + exchange_halves(tile) * sine
            if t == 2:
                turned = jnp.where(lane < HD, turned, tile)
            qkv_ref[here, t * LANES : (t + 1) * LANES] = turned.astype(BF16)
    key_halves(qkv_ref, keys_ref, None, (1, turned_ref))
    for i in range(rows // QUERY_ROWS):
        keys = (i + 1) * QUERY_ROWS
        here = slice(i * QUERY_ROWS, keys)
        bias = allowed_bias(meta_ref, docs, i * QUERY_ROWS, keys, QUERY_ROWS)
        for t in range(2):
            query = qkv_ref[here, t * LANES : (t + 1) * LANES] * BF16(HD**-0.5)
            total = jnp.zeros((LANES, QUERY_ROWS), F32)
            for half in range(2):
                scores = last_dims(keys_ref[half, :keys, :], query) + bias
                peak = jnp.max(scores, axis=0, keepdims=True)
                raised = jnp.exp(scores - peak)
                mass = jnp.sum(raised, axis=0, keepdims=True)
                probs = (raised * (1.0 / mass)).astype(BF16)
                total = total + jnp.dot(
                    turned_ref[half, :, :keys], probs, preferred_element_type=F32
                )
                head = 2 * t + half
                log_ref[0, head : head + 1, here] = peak + jnp.log(mass)
            done = total.T.astype(BF16)
            step = min(block, QUERY_ROWS)
            for part in range(QUERY_ROWS // step):
                first = i * QUERY_ROWS + part * step
                place = block_place(meta_ref, first // block, devices) * block + first % block
                attended_ref[
                    pl.ds(pl.multiple_of(place, step), step), t * LANES : (t + 1) * LANES
                ] = done[part * step : (part + 1) * step, :]


def backward_kernel(docs, devices, meta_ref, qkv_ref, log_ref, back_ref, cos_ref, sin_ref, grad_ref, keys_ref, values_ref, turned_ref, key_total, value_total, query_total, back_here):
    rows = qkv_ref.shape[0]
    block = rows // devices
    key_halves(qkv_ref, keys_ref, values_ref, (0, turned_ref))
    for j in range(devices):
        source = pl.multiple_of(block_place(meta_ref, j, devices) * block, block)
        back_here[j * block : (j + 1) * block, :] = back_ref[pl.ds(source, block), :]
    key_total[...] = jnp.zeros_like(key_total)
    value_total[...] = jnp.zeros_like(value_total)
    for i in range(rows // QUERY_ROWS):
        keys = (i + 1) * QUERY_ROWS
        here = slice(i * QUERY_ROWS, keys)
        bias = allowed_bias(meta_ref, docs, i * QUERY_ROWS, keys, QUERY_ROWS)
        lane = lax.broadcasted_iota(jnp.int32, (QUERY_ROWS, LANES), 1)
        for t in range(2):
            columns = slice(t * LANES, (t + 1) * LANES)
            query = qkv_ref[here, columns] * BF16(HD**-0.5)
            back = back_here[here, columns]
            total = jnp.zeros((LANES, QUERY_ROWS), F32)
            for half in range(2):
                head = 2 * t + half
                mine = (lane < HD) if half == 0 else (lane >= HD)
                scores = last_dims(keys_ref[half, :keys, :], query) + bias
                probs = jnp.exp(scores - log_ref[0, head : head + 1, here])
                moved = last_dims(values_ref[half, :keys, :], back)
                inner = jnp.sum(probs * moved, axis=0, keepdims=True)
                grad = (probs * (moved - inner)).astype(BF16)
                total = total + jnp.dot(
                    turned_ref[half, :, :keys], grad, preferred_element_type=F32
                )
                key_total[:keys, :] += jnp.dot(
                    grad, jnp.where(mine, query, BF16(0)), preferred_element_type=F32
                )
                value_total[:keys, :] += jnp.dot(
                    probs.astype(BF16), jnp.where(mine, back, BF16(0)), preferred_element_type=F32
                )
            query_total[here, columns] = total.T * HD**-0.5
    for j in range(devices):
        place = pl.multiple_of(block_place(meta_ref, j, devices) * block, block)
        here = slice(j * block, (j + 1) * block)
        cosine, sine = cos_ref[here, :], sin_ref[here, :]
        lane = lax.broadcasted_iota(jnp.int32, cosine.shape, 1)
        for t in range(2):
            columns = slice(t * LANES, (t + 1) * LANES)
            tile = query_total[here, columns]
            grad_ref[pl.ds(place, block), columns] = (
                tile * cosine - exchange_halves(tile) * sine
            ).astype(BF16)
        tile = key_total[here, :]
        tile = tile + pltpu.roll(tile, HD, 1)
        other = value_total[here, :]
        other = other + pltpu.roll(other, HD, 1)
        tile = jnp.where(lane < HD, tile * cosine - exchange_halves(tile) * sine, other)
        grad_ref[pl.ds(place, block), 2 * LANES : 3 * LANES] = tile.astype(BF16)


def attend_forward(meta, joined, cosine, sine, docs, devices):
    rows, width = joined.shape
    wide = (GROUP + 2) * HD
    groups = width // wide
    whole = pl.BlockSpec((rows, LANES), lambda g: (0, 0))
    return pl.pallas_call(
        functools.partial(forward_kernel, docs, devices),
        grid=(groups,),
        in_specs=[
            pl.BlockSpec(memory_space=pltpu.SMEM),
            pl.BlockSpec((rows, wide), lambda g: (0, g)),
            whole,
            whole,
        ],
        out_specs=[
            pl.BlockSpec((rows, GROUP * HD), lambda g: (0, g)),
            pl.BlockSpec((rows, wide), lambda g: (0, g)),
            pl.BlockSpec((1, 8, rows), lambda g: (g, 0, 0)),
        ],
        out_shape=[
            jax.ShapeDtypeStruct((rows, groups * GROUP * HD), BF16),
            jax.ShapeDtypeStruct((rows, width), BF16),
            jax.ShapeDtypeStruct((groups, 8, rows), F32),
        ],
        scratch_shapes=[
            pltpu.VMEM((2, rows, LANES), BF16),
            pltpu.VMEM((2, LANES, rows), BF16),
        ],
        compiler_params=pltpu.CompilerParams(vmem_limit_bytes=32 * 2**20),
        cost_estimate=pl.CostEstimate(flops=1, bytes_accessed=1, transcendentals=0),
        name="attend_forward",
    )(meta, joined, cosine, sine)


def attend_backward(meta, qkv, logs, back, cosine, sine, docs, devices, group):
    rows = qkv.shape[0]
    wide = (GROUP + 2) * HD
    whole = pl.BlockSpec((rows, LANES), lambda g: (0, 0))
    return pl.pallas_call(
        functools.partial(backward_kernel, docs, devices),
        grid=(1,),
        in_specs=[
            pl.BlockSpec(memory_space=pltpu.SMEM),
            pl.BlockSpec((rows, wide), lambda g: (0, group)),
            pl.BlockSpec((1, 8, rows), lambda g: (group, 0, 0)),
            pl.BlockSpec((rows, GROUP * HD), lambda g: (0, group)),
            whole,
            whole,
        ],
        out_specs=pl.BlockSpec((rows, wide), lambda g: (0, 0)),
        out_shape=jax.ShapeDtypeStruct((rows, wide), BF16),
        scratch_shapes=[
            pltpu.VMEM((2, rows, LANES), BF16),
            pltpu.VMEM((2, rows, LANES), BF16),
            pltpu.VMEM((2, LANES, rows), BF16),
            pltpu.VMEM((rows, LANES), F32),
            pltpu.VMEM((rows, LANES), F32),
            pltpu.VMEM((rows, GROUP * HD), F32),
            pltpu.VMEM((rows, GROUP * HD), BF16),
        ],
        compiler_params=pltpu.CompilerParams(vmem_limit_bytes=32 * 2**20),
        cost_estimate=pl.CostEstimate(flops=1, bytes_accessed=1, transcendentals=0),
        name="attend_backward",
    )(meta, qkv, logs, back, cosine, sine)


def product(left, right, left_dim, right_dim):
    return lax.dot_general(
        left, right, (((left_dim,), (right_dim,)), ((), ())), preferred_element_type=F32
    )


def norm_rate(vector):
    return lax.rsqrt(jnp.mean(vector * vector, axis=-1, keepdims=True) + EPSILON)


def norm_back(vector, rate, gain, grad):
    scaled = gain * grad
    inner = jnp.mean(vector * scaled, axis=-1, keepdims=True)
    return (
        rate * scaled - vector * (rate * rate * rate * inner),
        jnp.sum(grad * vector * rate, axis=0),
    )


def adam(weight, grad, moment, square, clip, rate, decay):
    clipped = clip * grad
    moment_new = BETA_ONE * moment + (1.0 - BETA_ONE) * clipped
    square_new = BETA_TWO * square + (1.0 - BETA_TWO) * clipped * clipped
    direction = (
        moment_new
        / (1.0 - BETA_ONE**STEP)
        / (jnp.sqrt(square_new / (1.0 - BETA_TWO**STEP)) + ADAM_EPSILON)
    )
    return (weight - rate * (direction + decay * weight), moment_new, square_new)


def adam_all_kernel(rates, side_ref, clip_ref, *refs):
    side, clip = side_ref[0], clip_ref[0]
    pieces_ref, turned_ref, in_grad_ref, out_grad_ref = refs[:4]
    states, outs = refs[4:16], refs[16:]

    def apply(k, grad, at):
        weight, moment, square = [ref[at] for ref in states[3 * k : 3 * k + 3]]
        done = adam(weight, grad.astype(F32), moment, square, clip, *rates[k])
        for ref, value in zip(outs[3 * k : 3 * k + 3], done):
            ref[at] = value

    columns = states[0].shape[-1]
    unit = columns // (2 * UNITS)
    per_half = UNITS // 2
    for n in range(2 * UNITS):
        which, half, place = n // UNITS, n % UNITS // per_half, n % per_half
        for j in range(2):
            first = (2 * place + j) * unit
            grad = pieces_ref[which ^ side, half, :, first : first + unit]
            apply(0, grad, (j, slice(None), slice(n * unit, (n + 1) * unit)))
    apply(1, turned_ref[0, 0].astype(F32).T, (slice(None), slice(None)))
    apply(2, in_grad_ref[...], (slice(None), slice(None)))
    apply(3, out_grad_ref[...], (slice(None), slice(None)))


def update_all(states, pieces, in_grad, out_grad, clip, side, rates):
    steps = 2 * UNITS
    depth, slim = pieces.shape[2], pieces.shape[3] // 3
    unit = 2 * slim // UNITS

    def rows(array):
        lead = array.shape[:-2]
        block = lead + (array.shape[-2] // steps, array.shape[-1])
        return pl.BlockSpec(block, lambda i, s: (0,) * len(lead) + (i, 0))

    specs = [rows(a) for a in states]
    grid_spec = pltpu.PrefetchScalarGridSpec(
        num_scalar_prefetch=1,
        grid=(steps,),
        in_specs=[
            pl.BlockSpec(memory_space=pltpu.SMEM),
            pl.BlockSpec((2, 2, depth // steps, 2 * slim), lambda i, s: (0, 0, i, 0)),
            pl.BlockSpec(
                (1, 1, depth, unit),
                lambda i, s: ((i // UNITS) ^ s[0], i % UNITS // 2, 0, UNITS + i % 2),
            ),
            rows(in_grad),
            rows(out_grad),
        ]
        + specs,
        out_specs=specs,
    )
    return pl.pallas_call(
        functools.partial(adam_all_kernel, rates),
        grid_spec=grid_spec,
        out_shape=[jax.ShapeDtypeStruct(a.shape, F32) for a in states],
        compiler_params=pltpu.CompilerParams(vmem_limit_bytes=60 * 2**20),
        cost_estimate=pl.CostEstimate(flops=1, bytes_accessed=1, transcendentals=0),
        name="update_all",
    )(
        side.reshape(1).astype(jnp.int32),
        clip.reshape(1),
        pieces,
        pieces,
        in_grad,
        out_grad,
        *states,
    )


def split_kernel(unit, side_ref, in_ref, out_ref, *part_refs):
    slim = part_refs[0].shape[1] // 3
    for part, ref in enumerate(part_refs):
        for n in range(slim // unit):
            cut = slice(part * slim + n * unit, part * slim + (n + 1) * unit)
            for j in range(2):
                first = (2 * n + j) * unit
                ref[:, first : first + unit] = in_ref[j, :, cut].astype(BF16)
        ref[:, 2 * slim :] = out_ref[part * slim : (part + 1) * slim, :].T.astype(BF16)


def split_feed(feed_in, feed_out, side, unit):
    depth, hidden = feed_in.shape[1], feed_in.shape[2] // 2
    part = jax.ShapeDtypeStruct((depth, 3 * hidden // 2), BF16)
    grid_spec = pltpu.PrefetchScalarGridSpec(
        num_scalar_prefetch=1,
        grid=(1,),
        in_specs=[
            pl.BlockSpec((2, depth, hidden), lambda i, s: (0, 0, s[0])),
            pl.BlockSpec((hidden, depth), lambda i, s: (s[0], 0)),
        ],
        out_specs=[pl.BlockSpec(part.shape, lambda i, s: (0, 0))] * 2,
    )
    return pl.pallas_call(
        functools.partial(split_kernel, unit),
        grid_spec=grid_spec,
        out_shape=[part] * 2,
        compiler_params=pltpu.CompilerParams(vmem_limit_bytes=60 * 2**20),
        cost_estimate=pl.CostEstimate(flops=1, bytes_accessed=1, transcendentals=0),
        name="split_feed",
    )(side.reshape(1).astype(jnp.int32), feed_in, feed_out)


def feed_kernel(unit, rows_ref, back_ref, weight_ref, activated_ref, grad_ref):
    units = activated_ref.shape[1] // unit
    for n in range(units):
        first = 2 * n * unit
        both = jnp.dot(
            rows_ref[...], weight_ref[:, first : first + 2 * unit], preferred_element_type=F32
        )
        first = (2 * units + n) * unit
        back = jnp.dot(
            back_ref[...], weight_ref[:, first : first + unit], preferred_element_type=F32
        )
        gate, upward = both[:, :unit], both[:, unit:]
        chance = jax.nn.sigmoid(gate)
        silu = gate * chance
        activated_ref[:, n * unit : (n + 1) * unit] = (silu * upward).astype(BF16)
        grad_ref[:, 2 * n * unit : (2 * n + 1) * unit] = (
            back * upward * (chance + silu * (1.0 - chance))
        ).astype(BF16)
        grad_ref[:, (2 * n + 1) * unit : 2 * (n + 1) * unit] = (back * silu).astype(BF16)


def feed_both_ways(rows, back, weight, unit):
    count, width = rows.shape
    slim = weight.shape[1] // 3
    tall = min(count, 512)
    return pl.pallas_call(
        functools.partial(feed_kernel, unit),
        grid=(count // tall,),
        in_specs=[
            pl.BlockSpec((tall, width), lambda i: (i, 0)),
            pl.BlockSpec((tall, width), lambda i: (i, 0)),
            pl.BlockSpec(weight.shape, lambda i: (0, 0)),
        ],
        out_specs=[
            pl.BlockSpec((tall, slim), lambda i: (i, 0)),
            pl.BlockSpec((tall, 2 * slim), lambda i: (i, 0)),
        ],
        out_shape=[
            jax.ShapeDtypeStruct((count, slim), BF16),
            jax.ShapeDtypeStruct((count, 2 * slim), BF16),
        ],
        compiler_params=pltpu.CompilerParams(vmem_limit_bytes=48 * 2**20),
        cost_estimate=pl.CostEstimate(flops=1, bytes_accessed=1, transcendentals=0),
        name="feed_both_ways",
    )(rows, back, weight)


def weights_kernel(scale, rows_ref, grad_ref, back_ref, activated_ref, out_ref):
    wide = grad_ref.shape[1]
    out_ref[0, :, :wide] = (product(rows_ref[...], grad_ref[...], 0, 0) * scale).astype(BF16)
    out_ref[0, :, wide:] = (product(back_ref[...], activated_ref[...], 0, 0) * scale).astype(BF16)


def weight_gradients(rows, grad, back, activated, parts, scale):
    count, width = rows.shape
    cut, slim = width // parts, activated.shape[1]
    return pl.pallas_call(
        functools.partial(weights_kernel, scale),
        grid=(parts,),
        in_specs=[
            pl.BlockSpec((count, cut), lambda i: (0, i)),
            pl.BlockSpec(grad.shape, lambda i: (0, 0)),
            pl.BlockSpec((count, cut), lambda i: (0, i)),
            pl.BlockSpec(activated.shape, lambda i: (0, 0)),
        ],
        out_specs=pl.BlockSpec((1, cut, 3 * slim), lambda i: (i, 0, 0)),
        out_shape=jax.ShapeDtypeStruct((parts, cut, 3 * slim), BF16),
        compiler_params=pltpu.CompilerParams(vmem_limit_bytes=48 * 2**20),
        cost_estimate=pl.CostEstimate(flops=1, bytes_accessed=1, transcendentals=0),
        name="weight_gradients",
    )(rows, grad, back, activated)


def back_kernel(*refs):
    total = 0.0
    for left, right in zip(refs[:-1:2], refs[1:-1:2]):
        total = total + product(left[...], right[...], 1, 1)
    refs[-1][...] = total.astype(BF16)


def back_products(pairs, first, last, half):
    count, width = pairs[0][0].shape[0] // 2, pairs[0][1].shape[0]
    tall = min(count, 512)
    skip, place = half * (count // tall), first // (last - first)
    specs, operands = [], []
    for left, right in pairs:
        depth = left.shape[1]
        specs.append(pl.BlockSpec((tall, depth), lambda i: (i + skip, 0)))
        specs.append(pl.BlockSpec((width, depth), lambda i: (0, place)))
        operands += [left, right]
    depth = sum(left.shape[1] for left, _ in pairs)
    return pl.pallas_call(
        back_kernel,
        grid=(count // tall,),
        in_specs=specs,
        out_specs=pl.BlockSpec((tall, width), lambda i: (i, 0)),
        out_shape=jax.ShapeDtypeStruct((count, width), BF16),
        compiler_params=pltpu.CompilerParams(vmem_limit_bytes=56 * 2**20),
        cost_estimate=pl.CostEstimate(flops=1, bytes_accessed=1, transcendentals=0),
        name="back_products",
    )(*operands)


def in_order(mine, other, first, axis):
    return jnp.where(
        first,
        jnp.concatenate([mine, other], axis=axis),
        jnp.concatenate([other, mine], axis=axis),
    )


def shards(
    sizes,
    tensor,
    tokens,
    cotangent,
    doc_lengths,
    attend_in,
    attend_out,
    feed_in,
    feed_out,
    norm_gains,
    moment_attend_in,
    square_attend_in,
    moment_attend_out,
    square_attend_out,
    moment_feed_in,
    square_feed_in,
    moment_feed_out,
    square_feed_out,
    moment_gains,
    square_gains,
):
    pack_links, core = tensor[:-1], tensor[-1]
    feed_links = ("x",) + tuple(pack_links)
    devices = math.prod(sizes[a] for a in tensor)
    side = lax.axis_index("x")
    is_first = side == 0
    local_rows, width = tokens.shape
    rows = local_rows * devices
    token_total = rows * 2 * sizes["z"]
    inverse_total = 1.0 / token_total
    docs = doc_lengths.shape[1]
    meta = jnp.concatenate(
        [lax.axis_index(tuple(tensor))[None].astype(jnp.int32), jnp.cumsum(doc_lengths[0])]
    )
    cosine, sine = rotation_tables(doc_lengths[0], rows)

    hidden = feed_in.shape[2] // 2
    slim = hidden // 2
    unit = hidden // UNITS
    depth = attend_in.shape[0]
    half = rows // 2

    def halves(array, axis):
        size = array.shape[axis] // 2
        mine = lax.dynamic_slice_in_dim(array, side * size, size, axis)
        other = lax.dynamic_slice_in_dim(array, (1 - side) * size, size, axis)
        return mine, other

    def sends(block, links):
        return [flip(block, c, sizes) for c in combos(links)[1:]]

    def over_core(blocks):
        mine = jnp.concatenate(blocks, axis=0)
        return jnp.concatenate([mine, flip(mine, (core,), sizes)], axis=0)

    def both_sides(mine, other):
        pair = jnp.where(
            is_first, jnp.stack([mine, other], axis=1), jnp.stack([other, mine], axis=1)
        )
        return pair

    gain_rows = jnp.pad(
        norm_gains.astype(BF16), ((0, 14), (0, attend_in.shape[1] - norm_gains.shape[1]))
    )
    in_z = lax.all_gather(
        jnp.concatenate([attend_in.astype(BF16), gain_rows], axis=0), "z", axis=0, tiled=False
    )
    out_z = gather_depth(attend_out.T.astype(BF16), sizes)
    tokens_moved = sends(tokens, pack_links)
    away = split_feed(feed_in, feed_out, 1 - side, unit)
    moved = [flip(part, ("x",), sizes) for part in away]
    kept = split_feed(feed_in, feed_out, side, unit)
    locals_ = [in_order(part, other, is_first, 0) for part, other in zip(kept, moved)]
    in_z, out_z, cotangent_then, tokens_moved, locals_ = lax.optimization_barrier(
        (in_z, out_z, cotangent, tokens_moved, locals_)
    )

    weight_a, weight_b = [lax.all_gather(part, "z", axis=0, tiled=True) for part in locals_]
    in_x = flip(in_z, ("x",), sizes)
    back_moved = sends(cotangent_then, pack_links)
    tokens_all = over_core([tokens] + tokens_moved)
    in_x, back_moved, tokens_all = lax.optimization_barrier((in_x, back_moved, tokens_all))

    out_x = flip(out_z, ("x",), sizes)
    in_both = both_sides(in_z, in_x)
    full_in = in_both[:, :, :depth].reshape(width, attend_in.shape[1])
    gains = (
        in_both[:, :, depth : depth + 2, : norm_gains.shape[1]]
        .astype(F32)
        .transpose(2, 0, 1, 3)
        .reshape(2, width)
    )
    inputs_all = tokens_all.astype(F32)
    normed_one = (inputs_all * norm_rate(inputs_all) * gains[0]).astype(BF16)
    joined = product(normed_one, full_in, 1, 0)
    attended, qkv, logs = attend_forward(meta, joined, cosine, sine, docs, devices)
    back_near = jnp.concatenate([cotangent] + back_moved, axis=0)
    attended, out_x, left, right = lax.optimization_barrier(
        (attended, out_x, back_near[:, : width // 2], back_near[:, width // 2 :])
    )

    full_out = both_sides(out_z, out_x).reshape(width, attend_out.shape[0])
    near = product(attended[half:], full_out, 1, 1).astype(BF16)
    mine = product(attended[:half], full_out, 1, 1).astype(BF16)
    own, moved = collect(mine, near, pack_links, core, sizes)
    left = flip(left, ("x",), sizes)
    right = flip(right, ("x",), sizes)
    own, moved, left, right = lax.optimization_barrier((own, moved, left, right))

    inputs = tokens.astype(F32)
    hidden_state = inputs + added(own, moved)
    rate_two = norm_rate(hidden_state)
    normed_two = (hidden_state * rate_two * gains[1]).astype(BF16)
    normed_moved = sends(normed_two, feed_links)
    gathered_back = over_core([back_near, jnp.concatenate([left, right], axis=1)])
    normed_moved, gathered_back = lax.optimization_barrier((normed_moved, gathered_back))
    gathered_two = over_core([normed_two] + normed_moved)

    def gradients(grad, activated):
        return weight_gradients(
            gathered_two, grad, gathered_back, activated, sizes["z"], inverse_total
        )

    def summed(parts):
        return lax.psum_scatter(parts, "z", scatter_dimension=0, tiled=False)

    activated_a, grad_a = feed_both_ways(gathered_two, gathered_back, weight_a, unit)
    parts_a = gradients(grad_a, activated_a)
    parts_a, weight_b = lax.optimization_barrier((parts_a, weight_b))
    sums_a = summed(parts_a)
    activated_b, grad_b = feed_both_ways(gathered_two, gathered_back, weight_b, unit)
    pairs = [(grad_a, weight_a), (grad_b, weight_b)]
    near = flip(back_products(pairs, 0, 2, 1), (core,), sizes)
    mine = back_products(pairs, 0, 2, 0)
    blocks = add_blocks(mine, near, 2 ** len(feed_links))
    blocks, grad_b, activated_a, activated_b = lax.optimization_barrier(
        (blocks, grad_b, activated_a, activated_b)
    )
    moved = [flip(block, c, sizes) for block, c in zip(blocks[1:], combos(feed_links)[1:])]
    parts_b = gradients(grad_b, activated_b)
    sums_b = summed(parts_b)
    pairs = [(activated_a, weight_a), (activated_b, weight_b)]
    forward_near = back_products(pairs, 2, 3, 1)
    moved, parts_b, forward_near, activated_a, activated_b = lax.optimization_barrier(
        (moved, parts_b, forward_near, activated_a, activated_b)
    )

    grad_from_two, gain_two_grad = norm_back(
        hidden_state, rate_two, gains[1], added(blocks[0], moved)
    )
    grad_hidden = cotangent.astype(F32) + grad_from_two
    grad_branch = grad_hidden.astype(BF16)

    def regroup(sums):
        mine, other = halves(sums, 0)
        return jnp.stack([mine, flip(other, ("x",), sizes)])

    pairs = [(activated_a, weight_a), (activated_b, weight_b)]
    forward_mine = back_products(pairs, 2, 3, 0)
    forward_blocks = add_blocks(
        forward_mine, flip(forward_near, (core,), sizes), 2 ** len(feed_links)
    )
    sums_a, grad_branch = lax.optimization_barrier((sums_a, grad_branch))
    grad_moved = sends(grad_branch, pack_links)
    pieces_a = regroup(sums_a)
    grad_moved, forward_blocks, pieces_a = lax.optimization_barrier(
        (grad_moved, forward_blocks, pieces_a)
    )
    forward_links = combos(feed_links)[1:]
    forward_first = [
        flip(block, c, sizes)
        for block, c in zip(forward_blocks[1:], forward_links)
        if "x" not in c
    ]
    gathered_grad = over_core([grad_branch] + grad_moved)
    grad_attended = product(gathered_grad, full_out, 1, 0).astype(BF16)
    groups = attend_in.shape[1] // ((GROUP + 2) * HD)
    grad_joined = [
        attend_backward(meta, qkv, logs, grad_attended, cosine, sine, docs, devices, group)
        for group in range(groups)
    ]

    def split_sides(grad):
        split = (grad * inverse_total).astype(BF16).reshape(sizes["z"], 2, -1, grad.shape[1])
        mine = lax.dynamic_index_in_dim(split, side, 1, keepdims=False)
        other = lax.dynamic_index_in_dim(split, 1 - side, 1, keepdims=False)
        return mine, flip(other, ("x",), sizes)

    out_mine, out_other = split_sides(product(gathered_grad, attended, 0, 0))
    in_pairs = [split_sides(product(normed_one, grad, 0, 0)) for grad in grad_joined[:-1]]
    grad_joined[-1], out_other, forward_first, in_pairs = lax.optimization_barrier(
        (grad_joined[-1], out_other, forward_first, in_pairs)
    )
    out_sums = added(out_mine, [out_other]).astype(BF16)
    in_pairs.append(split_sides(product(normed_one, grad_joined[-1], 0, 0)))
    in_pairs, forward_blocks = lax.optimization_barrier((in_pairs, forward_blocks))
    in_parts = [added(mine, [other]).astype(BF16) for mine, other in in_pairs]
    attend_sums = summed(jnp.concatenate(in_parts + [out_sums], axis=2))
    joined_back = jnp.concatenate(grad_joined, axis=1)
    own, moved = collect(
        product(joined_back[:half], full_in, 1, 1).astype(BF16),
        product(joined_back[half:], full_in, 1, 1).astype(BF16),
        pack_links,
        core,
        sizes,
    )
    forward_x = flip(forward_blocks[forward_links.index(("x",)) + 1], ("x",), sizes)
    sums_b, forward_x, own, moved = lax.optimization_barrier((sums_b, forward_x, own, moved))
    pieces_b = regroup(sums_b)
    grad_normed_one = added(own, moved)
    grad_from_one, gain_one_grad = norm_back(inputs, norm_rate(inputs), gains[0], grad_normed_one)
    tokens_grad = (grad_hidden + grad_from_one).astype(BF16)

    gain_grads = sum_near(
        jnp.stack([gain_one_grad, gain_two_grad]) * inverse_total, tensor, sizes
    )
    def squares(shard):
        shard = shard.astype(F32)
        return jnp.sum(shard * shard)

    feed_squares = squares(sums_a) + squares(sums_b)
    attend_sums, gain_grads, tokens_grad, feed_squares = lax.optimization_barrier(
        (attend_sums, gain_grads, tokens_grad, feed_squares)
    )
    gain_grads = sum_far(gain_grads, sizes)
    attend_in_shard = attend_sums[:, : attend_in.shape[1]]
    attend_out_shard = attend_sums[:, attend_in.shape[1] :].T
    pieces = jnp.stack([pieces_a, pieces_b], axis=1)

    matrix_squares = feed_squares + squares(attend_sums)
    total_squares = sum_scalar(matrix_squares, ("z", "x") + tuple(tensor), sizes)
    total_squares, pieces, attend_in_shard, attend_out_shard = lax.optimization_barrier(
        (total_squares, pieces, attend_in_shard, attend_out_shard)
    )
    grad_norm = jnp.sqrt(total_squares + jnp.sum(gain_grads * gain_grads))
    clip = jnp.minimum(1.0, CLIP_LIMIT / (grad_norm + 1e-06))
    clip, forward_blocks = lax.optimization_barrier((clip, forward_blocks))
    forward_last = [
        flip(block, c, sizes)
        for block, c in zip(forward_blocks[1:], forward_links)
        if "x" in c and len(c) > 1
    ]
    block_out = added(forward_blocks[0], forward_first + [forward_x] + forward_last)
    block_out = (hidden_state + block_out).astype(BF16)
    gain_width = norm_gains.shape[1]
    gain_shard = lax.dynamic_slice_in_dim(
        gain_grads, lax.axis_index(("z", "x")) * gain_width, gain_width, 1
    )
    states = (
        (feed_in, moment_feed_in, square_feed_in)
        + (feed_out, moment_feed_out, square_feed_out)
        + (attend_in, moment_attend_in, square_attend_in)
        + (attend_out, moment_attend_out, square_attend_out)
    )
    matrix, output = (MATRIX_RATE, MATRIX_DECAY), (OUTPUT_RATE, MATRIX_DECAY)
    done = update_all(
        states, pieces, attend_in_shard, attend_out_shard, clip, side, (matrix, matrix, matrix, output)
    )
    third, fourth, first, second = done[:3], done[3:6], done[6:9], done[9:]
    fifth = adam(norm_gains, gain_shard, moment_gains, square_gains, clip, GAIN_RATE, 0.0)
    return (block_out, tokens_grad, grad_norm, *first, *second, *third, *fourth, *fifth)


def solution(mesh):
    depth, across = mesh.shape["dp"], mesh.shape["tensor"]
    tensor = tuple("t" + str(i) for i in range(across.bit_length() - 1))
    sizes = {"z": depth // 2, "x": 2, **{a: 2 for a in tensor}}
    assert depth % 2 == 0 and 2 ** len(tensor) == across
    fine = Mesh(mesh.devices.reshape(tuple(sizes.values())), tuple(sizes))
    dp = ("z", "x")
    both = P(dp + tensor, None)
    rows_cut, columns_cut = P(dp, tensor), P(tensor, dp)
    feed_cut, gain_cut = P(None, dp, tensor), P(None, dp)
    state = (rows_cut,) * 3 + (columns_cut,) * 3 + (feed_cut,) * 3 + (columns_cut,) * 3 + (gain_cut,) * 3
    return jax.shard_map(
        functools.partial(shards, sizes, tensor),
        mesh=fine,
        in_specs=(both, both, P(dp, None), rows_cut, columns_cut, feed_cut, columns_cut, gain_cut)
        + (rows_cut,) * 2
        + (columns_cut,) * 2
        + (feed_cut,) * 2
        + (columns_cut,) * 2
        + (gain_cut,) * 2,
        out_specs=(both, both, P()) + state,
        check_vma=False,
    )
```
